512 devices in a mesh: dp: 8 (over y), seq: 16 (over z, core), head: 4 (over x).
Axes of the slice: x: 4, y: 8, z: 8, core: 2. Of those that a mesh axis runs over, the one named last changes fastest.
Arguments:
- enc_query: bfloat16 [8, 2048, 1536], P('dp', 'seq', 'head'), may hold values from -240 to 240
- enc_key: bfloat16 [8, 2048, 1536], P('dp', 'seq', 'head'), may hold values from -6 to 6
- enc_value: bfloat16 [8, 2048, 1536], P('dp', 'seq', 'head'), may hold values from -6 to 6
- keep_index: int32 [8, 1536], P('dp', 'seq'), may hold values from 0 to 127, as said below
- keep_count: int32 [8, 16], P('dp', 'seq'), may hold values from 32 to 96, as said below
- text_key: bfloat16 [8, 128, 1536], P('dp', None, 'head'), may hold values from -6 to 6
- text_value: bfloat16 [8, 128, 1536], P('dp', None, 'head'), may hold values from -6 to 6
- dec_query: bfloat16 [8, 2048, 1536], P('dp', 'seq', 'head'), may hold values from -240 to 240
- dec_key: bfloat16 [8, 2048, 1536], P('dp', 'seq', 'head'), may hold values from -6 to 6
- mask_value: bfloat16 [1536], P('head'), may hold values from -5 to 5
- norm_gain: bfloat16 [1536], P('head'), may hold values from 0.25 to 1.75
- target: bfloat16 [8, 2048, 1536], P('dp', 'seq', 'head'), may hold values from -6 to 6
- timesteps: int32 [8], P('dp'), may hold values from 0 to 999
Outputs:
- decoded: bfloat16 [8, 2048, 1536], P('dp', 'seq', 'head')
- total_loss: float32 [], replicated
The draws below stay inside these ranges and needn't reach their ends.
Inputs may be any that keep to these rules, and one draw needn't show every extreme that they name: `keep_count`: each image has one block whose count is exactly 96. `keep_index`: in each block's 96 slots the first keep_count entries are strictly increasing, the rest are 0.
All inputs are finite; a program needn't handle non-finite values.
Results may differ from the reference program's by a relative error of at most 0.004.
Values may be sent and summed in bfloat16 or wider, within the bound.
No kernel may reach another device: no remote copies, remote signals or barrier semaphores. Data moves between devices by JAX's collectives and lax.ppermute only.
A program may use at most 64 MiB of HBM per device.

```python
import jax
import jax.numpy as jnp
from jax import lax

HEAD_DIM = 64
HEADS = 24
TXT = 128
TOK_DEV = 128
IMAGES = 8
TOKENS = 2048
CAP = 96
COLS = 1536
N_SEQ = 16


def keep_plan(key):
    base = jax.random.fold_in(key, 1)
    kept_total = jax.random.randint(jax.random.fold_in(base, 1), (IMAGES, N_SEQ), TOK_DEV // 4, CAP + 1)
    busiest = jax.random.randint(jax.random.fold_in(base, 2), (IMAGES, 1), 0, N_SEQ)
    kept_total = jnp.where(jnp.arange(N_SEQ)[None, :] == busiest, CAP, kept_total)
    ranking = jax.random.randint(jax.random.fold_in(base, 3), (IMAGES, N_SEQ, TOK_DEV), 0, 2 ** 22) * TOK_DEV + jnp.arange(TOK_DEV)[None, None, :]
    ordering = jnp.argsort(ranking, axis=-1)
    chosen = ordering[:, :, :CAP]
    slot_live = jnp.arange(CAP)[None, None, :] < kept_total[:, :, None]
    chosen = jnp.sort(jnp.where(slot_live, chosen, TOK_DEV), axis=-1)
    chosen = jnp.where(slot_live, chosen, 0)
    return (kept_total.astype(jnp.int32), chosen.reshape(IMAGES, N_SEQ * CAP).astype(jnp.int32))


def key_field(key, salt):
    field = jax.random.normal(jax.random.fold_in(key, salt), (IMAGES, TOKENS, COLS), jnp.float32)
    return jnp.clip(field, -6.0, 6.0)


def draw_keep_count(key, part):
    kept_total, chosen = keep_plan(key)
    return kept_total


def draw_keep_index(key, part):
    kept_total, chosen = keep_plan(key)
    return chosen


def draw_enc_key(key, part):
    field = key_field(key, 200)
    return field.astype(jnp.bfloat16)


def draw_enc_query(key, part):
    own = jax.random.fold_in(key, 5)
    query = jnp.clip(jax.random.normal(own, (IMAGES, TOKENS, COLS), jnp.float32), -6.0, 6.0)
    return query.astype(jnp.bfloat16)


def draw_dec_key(key, part):
    field = key_field(key, 100)
    return field.astype(jnp.bfloat16)


def draw_dec_query(key, part):
    own = jax.random.fold_in(key, 7)
    query = jnp.clip(jax.random.normal(own, (IMAGES, TOKENS, COLS), jnp.float32), -6.0, 6.0)
    return query.astype(jnp.bfloat16)


def place_ends(values, key, least, high):
    extent = values.shape
    place = [jax.random.randint(jax.random.fold_in(key, axis), (), 0, extent[axis]) for axis in range(len(extent))]
    values = values.at[tuple(place)].set(least)
    longest = extent.index(max(extent))
    place[longest] = (place[longest] + 1) % extent[longest]
    return values.at[tuple(place)].set(high)


def block_levels(key, extent, pieces, smallest, largest):
    gain = 1.0
    for dim, shards_of in pieces:
        draws = jax.random.uniform(jax.random.fold_in(jax.random.fold_in(key, 6), dim), (shards_of,), jnp.float32, smallest / len(pieces), largest / len(pieces))
        gain = gain * jnp.repeat(jnp.exp(draws), extent[dim] // shards_of).reshape((-1,) + (1,) * (len(extent) - 1 - dim))
    return gain


def gaussian(rng, extent, scale, bound, pieces=(), kind=jnp.bfloat16):
    values = scale * jax.random.normal(rng, extent, jnp.float32)
    if pieces:
        values = values * block_levels(rng, extent, pieces, -0.22, 0.18)
    return jnp.clip(values, -bound, bound).astype(kind)


def setup_inputs(seed: int = 0) -> dict:
    arg_keys = jax.random.split(jax.random.key(seed), 14)
    enc_query = draw_enc_query(jax.random.fold_in(arg_keys[13], 71), 0)
    enc_key = draw_enc_key(jax.random.fold_in(arg_keys[13], 71), 0)
    enc_value = gaussian(arg_keys[2], (IMAGES, TOKENS, COLS), 1.0, 6.0, ((0, 8), (1, 16), (2, 4)))
    keep_index = draw_keep_index(jax.random.fold_in(arg_keys[13], 71), 0)
    keep_count = draw_keep_count(jax.random.fold_in(arg_keys[13], 71), 0)
    text_key = gaussian(arg_keys[5], (IMAGES, TXT, COLS), 1.0, 6.0, ((0, 8), (2, 4)))
    text_value = gaussian(arg_keys[6], (IMAGES, TXT, COLS), 1.0, 6.0, ((0, 8), (2, 4)))
    dec_query = draw_dec_query(jax.random.fold_in(arg_keys[13], 71), 0)
    dec_key = draw_dec_key(jax.random.fold_in(arg_keys[13], 71), 0)
    mask_value = gaussian(arg_keys[9], (COLS,), 1.0, 5.0, ((0, 4),))
    norm_gain = jnp.clip(1.0 + 0.15 * jax.random.normal(arg_keys[10], (COLS,), jnp.float32), 0.25, 1.75).astype(jnp.bfloat16)
    target = gaussian(arg_keys[11], (IMAGES, TOKENS, COLS), 1.0, 6.0, ((0, 8), (1, 16), (2, 4)))
    timesteps = place_ends(jax.random.randint(arg_keys[12], (IMAGES,), 0, 1000), jax.random.fold_in(arg_keys[12], 1), 0, 999).astype(jnp.int32)
    return {"enc_query": enc_query, "enc_key": enc_key, "enc_value": enc_value, "keep_index": keep_index, "keep_count": keep_count, "text_key": text_key, "text_value": text_value, "dec_query": dec_query, "dec_key": dec_key, "mask_value": mask_value, "norm_gain": norm_gain, "target": target, "timesteps": timesteps}


def head_attention(query_rows, key_rows, value_rows, key_live):
    scores = jnp.dot(query_rows, key_rows.T, preferred_element_type=jnp.float32) * HEAD_DIM ** (-0.5)
    scores = jnp.where(key_live[None, :], scores, -1e+30)
    row_max = lax.optimization_barrier(jnp.max(scores, axis=1, keepdims=True))
    weights = jnp.exp(scores - row_max)
    row_sum = lax.optimization_barrier(jnp.sum(weights, axis=1, keepdims=True))
    return jnp.dot(weights.astype(jnp.bfloat16), value_rows, preferred_element_type=jnp.float32) / row_sum

def attention(query_rows, key_rows, value_rows, key_live):
    rows_q = query_rows.shape[0]
    rows_k = key_rows.shape[0]
    query_heads = query_rows.reshape(rows_q, HEADS, HEAD_DIM).transpose(1, 0, 2)
    key_heads = key_rows.reshape(rows_k, HEADS, HEAD_DIM).transpose(1, 0, 2)
    value_heads = value_rows.reshape(rows_k, HEADS, HEAD_DIM).transpose(1, 0, 2)
    result = lax.map(lambda group: head_attention(group[0], group[1], group[2], key_live), (query_heads, key_heads, value_heads))
    return result.transpose(1, 0, 2).reshape(rows_q, HEADS * HEAD_DIM)

def one_image(enc_query, enc_key, enc_value, keep_index, keep_count, text_key, text_value, dec_query, dec_key, mask_value):
    slot_ids = jnp.arange(CAP, dtype=jnp.int32)
    slot_live = (slot_ids[None, :] < keep_count[:, None]).reshape(-1)
    block_base = jnp.arange(N_SEQ, dtype=jnp.int32)[:, None] * TOK_DEV
    position = (block_base + keep_index.reshape(N_SEQ, CAP).astype(jnp.int32)).reshape(-1).astype(jnp.int32)
    kept_query = enc_query[position]
    key_rows = jnp.concatenate([text_key, enc_key[position]], axis=0)
    value_rows = jnp.concatenate([text_value, enc_value[position]], axis=0)
    enc_live = jnp.concatenate([jnp.ones((TXT,), bool), slot_live], axis=0)
    enc_out = attention(kept_query, key_rows, value_rows, enc_live).astype(jnp.bfloat16)
    target_pos = jnp.where(slot_live, position, TOKENS).astype(jnp.int32)
    filled = jnp.broadcast_to(mask_value, (TOKENS, HEADS * HEAD_DIM))
    filled = filled.at[target_pos].set(enc_out, mode='drop')
    dec_keys = jnp.concatenate([text_key, dec_key], axis=0)
    dec_values = jnp.concatenate([text_value, filled], axis=0)
    all_live = jnp.ones((TXT + TOKENS,), bool)
    return attention(dec_query, dec_keys, dec_values, all_live)

def reference(enc_query, enc_key, enc_value, keep_index, keep_count, text_key, text_value, dec_query, dec_key, mask_value, norm_gain, target, timesteps):

    def per_image(group):
        return one_image(group[0], group[1], group[2], group[3], group[4], group[5], group[6], group[7], group[8], mask_value)
    dec_att = lax.map(per_image, (enc_query, enc_key, enc_value, keep_index, keep_count, text_key, text_value, dec_query, dec_key))
    mean_square = lax.optimization_barrier(jnp.mean(dec_att * dec_att, axis=-1, keepdims=True))
    normalized = dec_att * lax.rsqrt(mean_square + 1e-06) * norm_gain.astype(jnp.float32)
    loss_weight = 1.0 / (0.1 + timesteps.astype(jnp.float32) / 999.0)
    error = (normalized - target.astype(jnp.float32)) ** 2
    total_loss = jnp.sum(loss_weight[:, None, None] * error) / (IMAGES * TOKENS * HEADS * HEAD_DIM)
    return (normalized.astype(jnp.bfloat16), total_loss)
```

```python
import functools

import jax
import jax.numpy as jnp
from jax import lax
from jax.experimental import pallas as pl
from jax.experimental.pallas import tpu as pltpu
from jax.sharding import PartitionSpec as P

HEAD_DIM = 64
LANES = 128
DEAD = 1024.0
DEAD_EDGE = 512.0
VMEM_BYTES = 48 * 1024 * 1024


def params():
    return pltpu.CompilerParams(vmem_limit_bytes=VMEM_BYTES)


def vmem(count):
    return [pl.BlockSpec(memory_space=pltpu.VMEM)] * count


def one_hot_dot(table, rows):
    return lax.dot_general(
        table, rows, (((1,), (0,)), ((), ())), preferred_element_type=jnp.float32
    )


def pack_kernel(
    count_ref, index_ref, eq_ref, ek_ref, ev_ref, dq_ref, dk_ref, tk_ref, tv_ref, mask_ref, send_ref, text_ref
):
    tokens, cols = eq_ref.shape[1:]
    slots = index_ref.shape[1]
    heads = cols // HEAD_DIM
    half = tokens // 2
    spare = tokens - slots
    total = count_ref[0, 0]
    index = jnp.broadcast_to(index_ref[...].astype(jnp.float32), (tokens, slots))
    index = jnp.transpose(index)
    token = lax.broadcasted_iota(jnp.int32, (slots, tokens), 1).astype(jnp.float32)
    slot = lax.broadcasted_iota(jnp.int32, (slots, tokens), 0)
    live = slot < total
    match_live = jnp.where(live & (token == index), 1.0, 0.0)
    match_fill = jnp.where(token == jnp.where(live, index, index[0:1, :]), 1.0, 0.0)
    kept = jnp.sum(match_live, axis=0, keepdims=True)
    kept_slot = jnp.sum(match_live * slot.astype(jnp.float32), axis=0, keepdims=True)
    row = lax.broadcasted_iota(jnp.int32, (tokens, tokens), 0)
    col = lax.broadcasted_iota(jnp.int32, (tokens, tokens), 1)
    before = jnp.where(row < col, 1.0, 0.0).astype(jnp.bfloat16)
    left = jnp.broadcast_to(1.0 - kept, (16, tokens)).astype(jnp.bfloat16)
    rank = one_hot_dot(left, before)[0:1, :]
    place = jnp.where(kept > 0.5, kept_slot, total.astype(jnp.float32) + rank)
    order = jnp.where(row.astype(jnp.float32) == place, 1.0, 0.0).astype(jnp.bfloat16)

    scale = HEAD_DIM ** (-0.5)
    match_live = match_live.astype(jnp.bfloat16)
    match_fill = match_fill.astype(jnp.bfloat16)
    query = one_hot_dot(match_live, eq_ref[0]) * scale
    slot_wide = lax.broadcasted_iota(jnp.int32, (slots, cols), 0)
    query = jnp.where(slot_wide < total, query, DEAD)
    key = one_hot_dot(match_fill, ek_ref[0])
    value = one_hot_dot(match_live, ev_ref[0])
    dec_key = one_hot_dot(order, dk_ref[0])
    dec_query = dq_ref[0].astype(jnp.float32) * scale
    text_key = tk_ref[0].astype(jnp.float32)
    text_value = tv_ref[0].astype(jnp.float32)
    mask_row = jnp.broadcast_to(mask_ref[...].astype(jnp.float32), (16, cols))

    def low(block, head):
        tile = block[:, (head // 2) * LANES : (head // 2 + 1) * LANES]
        return tile if head % 2 == 0 else pltpu.roll(tile, HEAD_DIM, 1)

    def high(block, head):
        tile = block[:, (head // 2) * LANES : (head // 2 + 1) * LANES]
        return tile if head % 2 == 1 else pltpu.roll(tile, HEAD_DIM, 1)

    def join(first, second):
        lane = lax.broadcasted_iota(jnp.int32, first.shape, 1)
        return jnp.where(lane < HEAD_DIM, first, second).astype(jnp.bfloat16)

    for head in range(heads):
        kept_tile = join(low(value, head), high(key, head))
        query_high = high(query, head)
        dec_low = low(dec_key, head)
        dq_low = low(dec_query, head)
        dq_high = high(dec_query, head)
        for core in range(2):
            first = core * half
            dest = 2 * head + core
            send_ref[dest, 0:slots, :] = kept_tile
            send_ref[dest, slots : 2 * slots, :] = join(dec_low[0:slots], query_high)
            send_ref[dest, 2 * slots : slots + tokens, :] = join(
                dec_low[slots:tokens], dq_high[first : first + spare]
            )
            rest = (half - spare) // 2
            send_ref[dest, slots + tokens : slots + tokens + rest, :] = join(
                dq_low[first + spare : first + spare + rest],
                dq_high[first + spare + rest : first + half],
            )
        text_ref[head, 0:tokens, :] = join(low(text_value, head), high(text_key, head))
        text_ref[head, tokens : 2 * tokens, :] = join(low(text_key, head), high(text_value, head))
        text_ref[head, 2 * tokens : 2 * tokens + 16, :] = low(mask_row, head).astype(jnp.bfloat16)


def softmax_rows(query, key_ref, value_ref):
    scores = lax.dot_general(
        query, key_ref[...], (((1,), (1,)), ((), ())), preferred_element_type=jnp.float32
    )
    peak = jnp.max(scores, axis=1, keepdims=True)
    weights = jnp.exp(scores - peak).astype(jnp.bfloat16)
    sums = lax.dot_general(
        weights, value_ref[...], (((1,), (0,)), ((), ())), preferred_element_type=jnp.float32
    )
    return sums / pltpu.roll(sums, HEAD_DIM, 1)


def attend_kernel(
    blocks, slots, tokens, recv_ref, text_ref, out_ref, ek_ref, ev_ref, dk_ref, dv_ref, eq_ref, dq_ref
):
    half = tokens // 2
    spare = tokens - slots
    rest = (half - spare) // 2
    head = jnp.minimum(lax.axis_index("seq") // 2, text_ref.shape[0] - 1)
    text = text_ref[head]
    text_first = text[0:tokens]
    text_second = text[tokens : 2 * tokens]
    mask_row = text[2 * tokens : 2 * tokens + 1].astype(jnp.float32)

    def lane_of(rows):
        return lax.broadcasted_iota(jnp.int32, (rows, LANES), 1)

    def with_ones(tile):
        return jnp.where(lane_of(tile.shape[0]) < HEAD_DIM, tile.astype(jnp.float32), 1.0).astype(jnp.bfloat16)

    ek_ref[0:tokens, :] = text_first
    ev_ref[0:tokens, :] = with_ones(text_first)
    dk_ref[0:tokens, :] = text_second
    dv_ref[0:tokens, :] = with_ones(text_first)
    for block in range(blocks):
        kept = recv_ref[block, 0:slots, :]
        mixed = recv_ref[block, slots : 2 * slots, :].astype(jnp.float32)
        tail = recv_ref[block, 2 * slots : slots + tokens, :].astype(jnp.float32)
        last = recv_ref[block, slots + tokens : slots + tokens + rest, :].astype(jnp.float32)
        base = tokens + block * slots
        low_slot = lane_of(slots) < HEAD_DIM
        ek_ref[base : base + slots, :] = kept
        ev_ref[base : base + slots, :] = jnp.where(
            low_slot, kept.astype(jnp.float32), jnp.where(mixed < DEAD_EDGE, 1.0, 0.0)
        ).astype(jnp.bfloat16)
        eq_ref[block * slots : block * slots + slots, :] = jnp.where(low_slot, 0.0, mixed).astype(jnp.bfloat16)
        base = tokens + block * tokens
        dk_ref[base : base + slots, :] = mixed.astype(jnp.bfloat16)
        dk_ref[base + slots : base + tokens, :] = tail.astype(jnp.bfloat16)
        base = block * half
        dq_ref[base : base + spare, :] = jnp.where(
            lane_of(spare) < HEAD_DIM, pltpu.roll(tail, HEAD_DIM, 1), 0.0
        ).astype(jnp.bfloat16)
        low_rest = lane_of(rest) < HEAD_DIM
        dq_ref[base + spare : base + spare + rest, :] = jnp.where(low_rest, last, 0.0).astype(jnp.bfloat16)
        dq_ref[base + spare + rest : base + half, :] = jnp.where(
            low_rest, pltpu.roll(last, HEAD_DIM, 1), 0.0
        ).astype(jnp.bfloat16)

    enc_group = 2
    enc_rows = enc_group * slots

    def encode(step, carry):
        first = pl.multiple_of(step * enc_rows, enc_rows)
        found = softmax_rows(eq_ref[pl.ds(first, enc_rows), :], ek_ref, ev_ref)
        for inner in range(enc_group):
            block = step * enc_group + inner
            mixed = recv_ref[block, slots : 2 * slots, :].astype(jnp.float32)
            live = pltpu.roll(mixed, HEAD_DIM, 1) < DEAD_EDGE
            rows = jnp.where(live, found[inner * slots : (inner + 1) * slots], mask_row)
            base = pl.multiple_of(tokens + block * tokens, tokens)
            dv_ref[pl.ds(base, slots), :] = jnp.where(
                lane_of(slots) < HEAD_DIM, rows, 1.0
            ).astype(jnp.bfloat16)
            dv_ref[pl.ds(base + slots, spare), :] = jnp.where(
                lane_of(spare) < HEAD_DIM, mask_row, 1.0
            ).astype(jnp.bfloat16)
        return carry

    lax.fori_loop(0, blocks // enc_group, encode, 0)

    dec_group = 4
    dec_rows = dec_group * half

    def decode(step, carry):
        first = pl.multiple_of(step * dec_rows, dec_rows)
        found = softmax_rows(dq_ref[pl.ds(first, dec_rows), :], dk_ref, dv_ref)
        for inner in range(dec_group):
            rows = found[inner * half : (inner + 1) * half]
            out_ref[step * dec_group + inner] = jnp.where(
                lane_of(half // 2) < HEAD_DIM,
                rows[0 : half // 2],
                pltpu.roll(rows[half // 2 :], HEAD_DIM, 1),
            ).astype(jnp.bfloat16)
        return carry

    lax.fori_loop(0, blocks // dec_group, decode, 0)


def sums_kernel(got_ref, gain_ref, target_ref, att_ref, sums_ref):
    tokens, cols = att_ref.shape
    half = tokens // 2
    quarter = half // 2
    lane = lax.broadcasted_iota(jnp.int32, (quarter, LANES), 1)
    low = lane < HEAD_DIM
    for core in range(2):
        for tile in range(cols // LANES):
            even = got_ref[4 * tile + core].astype(jnp.float32)
            odd = got_ref[4 * tile + 2 + core].astype(jnp.float32)
            span = slice(tile * LANES, (tile + 1) * LANES)
            first = core * half
            att_ref[first : first + quarter, span] = jnp.where(low, even, pltpu.roll(odd, HEAD_DIM, 1))
            att_ref[first + quarter : first + half, span] = jnp.where(low, pltpu.roll(even, HEAD_DIM, 1), odd)
    att = att_ref[...]
    gained = att * gain_ref[...].astype(jnp.float32)
    target = target_ref[0].astype(jnp.float32)
    lane = lax.broadcasted_iota(jnp.int32, (tokens, LANES), 1)

    def over(block):
        return jnp.sum(block, axis=1, keepdims=True)

    table = jnp.where(
        lane == 0,
        over(att * att),
        jnp.where(lane == 1, over(gained * gained), jnp.where(lane == 2, over(gained * target), over(target * target))),
    )
    sums_ref[...] = jnp.transpose(table)[0:8, :]


def finish_kernel(count, steps_ref, att_ref, gain_ref, *refs):
    *parts, out_ref, loss_ref = refs
    tokens, cols = att_ref.shape
    total_cols = cols * count
    if count == 4:
        sums = (parts[0][...] + parts[1][...]) + (parts[2][...] + parts[3][...])
    else:
        sums = functools.reduce(lambda a, b: a + b, [part[...] for part in parts])
    square = sums[0:1, :]
    factor = lax.rsqrt(square / total_cols + 1e-06)
    error = factor * factor * sums[1:2, :] - 2.0 * factor * sums[2:3, :] + sums[3:4, :]
    weight = 1.0 / (0.1 + jnp.full((1, 1), steps_ref[0], jnp.int32).astype(jnp.float32) / 999.0)
    loss_ref[...] = jnp.broadcast_to(weight * jnp.sum(error, axis=1, keepdims=True), loss_ref.shape)
    column = jnp.transpose(jnp.broadcast_to(factor, (tokens, tokens)))[:, 0:1]
    out_ref[0] = (att_ref[...] * column * gain_ref[...].astype(jnp.float32)).astype(jnp.bfloat16)


def from_partners(part, axis, size):
    return [part] + [
        lax.ppermute(part, axis, [(source, source ^ apart) for source in range(size)]) for apart in range(1, size)
    ]


def tree_sum(parts):
    while len(parts) > 1:
        parts = [parts[place] + parts[place + 1] for place in range(0, len(parts), 2)]
    return parts[0]


def local(
    enc_query,
    enc_key,
    enc_value,
    keep_index,
    keep_count,
    text_key,
    text_value,
    dec_query,
    dec_key,
    mask_value,
    norm_gain,
    target,
    timesteps,
):
    images, seq, heads = (lax.axis_size(name) for name in ("dp", "seq", "head"))
    tokens, cols = enc_query.shape[1:]
    slots = keep_index.shape[1]
    local_heads = cols // HEAD_DIM
    packed = slots + tokens + (tokens // 2 - (tokens - slots)) // 2
    bf16, f32 = jnp.bfloat16, jnp.float32
    gain = norm_gain.reshape(1, cols)

    send, text = pl.pallas_call(
        pack_kernel,
        out_shape=(
            jax.ShapeDtypeStruct((seq, packed, LANES), bf16),
            jax.ShapeDtypeStruct((local_heads, 2 * tokens + 16, LANES), bf16),
        ),
        in_specs=[pl.BlockSpec(memory_space=pltpu.SMEM)] + vmem(9),
        out_specs=tuple(vmem(2)),
        compiler_params=params(),
        name="pack",
    )(
        keep_count,
        keep_index,
        enc_query,
        enc_key,
        enc_value,
        dec_query,
        dec_key,
        text_key,
        text_value,
        mask_value.reshape(1, cols),
    )
    recv = lax.all_to_all(send, "seq", 0, 0, tiled=True)
    out = pl.pallas_call(
        functools.partial(attend_kernel, seq, slots, tokens),
        out_shape=jax.ShapeDtypeStruct((seq, tokens // 4, LANES), bf16),
        in_specs=vmem(2),
        out_specs=vmem(1)[0],
        scratch_shapes=[
            pltpu.VMEM((tokens + seq * slots, LANES), bf16),
            pltpu.VMEM((tokens + seq * slots, LANES), bf16),
            pltpu.VMEM((tokens + seq * tokens, LANES), bf16),
            pltpu.VMEM((tokens + seq * tokens, LANES), bf16),
            pltpu.VMEM((seq * slots, LANES), bf16),
            pltpu.VMEM((seq * tokens // 2, LANES), bf16),
        ],
        compiler_params=params(),
        name="attend",
    )(recv, text)
    got = lax.all_to_all(out, "seq", 0, 0, tiled=True)
    att, sums = pl.pallas_call(
        sums_kernel,
        out_shape=(
            jax.ShapeDtypeStruct((tokens, cols), f32),
            jax.ShapeDtypeStruct((8, tokens), f32),
        ),
        in_specs=vmem(3),
        out_specs=tuple(vmem(2)),
        compiler_params=params(),
        name="sums",
    )(got, gain, target)
    parts = from_partners(sums, "head", heads)
    decoded, loss = pl.pallas_call(
        functools.partial(finish_kernel, heads),
        out_shape=(
            jax.ShapeDtypeStruct((1, tokens, cols), bf16),
            jax.ShapeDtypeStruct((8, LANES), f32),
        ),
        in_specs=[pl.BlockSpec(memory_space=pltpu.SMEM)] + vmem(2 + heads),
        out_specs=tuple(vmem(2)),
        compiler_params=params(),
        name="finish",
    )(timesteps, att, gain, *parts)
    loss = tree_sum(from_partners(loss, "seq", seq))
    loss = tree_sum(from_partners(loss, "dp", images))
    total_loss = loss[0, 0] / (images * tokens * seq * cols * heads)
    return (decoded, total_loss)


def solution(mesh):
    placed = (
        P("dp", "seq", "head"),
        P("dp", "seq", "head"),
        P("dp", "seq", "head"),
        P("dp", "seq"),
        P("dp", "seq"),
        P("dp", None, "head"),
        P("dp", None, "head"),
        P("dp", "seq", "head"),
        P("dp", "seq", "head"),
        P("head"),
        P("head"),
        P("dp", "seq", "head"),
        P("dp"),
    )
    return jax.shard_map(
        local, mesh=mesh, in_specs=placed, out_specs=(P("dp", "seq", "head"), P()), check_vma=False
    )
```

```python
import functools

import jax
import jax.numpy as jnp
from jax import lax
from jax.experimental import pallas as pl
from jax.experimental.pallas import tpu as pltpu
from jax.sharding import PartitionSpec as P

HEAD_DIM = 64
LANES = 128
DEAD = 1024.0
DEAD_EDGE = 512.0
VMEM_BYTES = 48 * 1024 * 1024


def params():
    return pltpu.CompilerParams(vmem_limit_bytes=VMEM_BYTES)


def vmem(count):
    return [pl.BlockSpec(memory_space=pltpu.VMEM)] * count


def one_hot_dot(table, rows):
    return lax.dot_general(
        table, rows, (((1,), (0,)), ((), ())), preferred_element_type=jnp.float32
    )


def pack_kernel(
    count_ref, index_hbm, eq_hbm, ek_hbm, ev_hbm, dq_hbm, dk_hbm, tk_hbm, tv_hbm, mask_hbm, send_ref, text_ref, *scratch
):
    *held, sems = scratch
    given = (index_hbm, eq_hbm, ek_hbm, ev_hbm, dq_hbm, dk_hbm, tk_hbm, tv_hbm, mask_hbm)
    copies = [
        pltpu.make_async_copy(source, place, sems.at[number])
        for number, (source, place) in enumerate(zip(given, held))
    ]
    for copy in copies:
        copy.start()
    for copy in copies:
        copy.wait()
    index_ref, eq_ref, ek_ref, ev_ref, dq_ref, dk_ref, tk_ref, tv_ref, mask_ref = held
    tokens, cols = eq_ref.shape[1:]
    slots = index_ref.shape[1]
    heads = cols // HEAD_DIM
    spare = tokens - slots
    total = count_ref[0, 0]
    index = jnp.broadcast_to(index_ref[...].astype(jnp.float32), (tokens, slots))
    index = jnp.transpose(index)
    token = lax.broadcasted_iota(jnp.int32, (slots, tokens), 1).astype(jnp.float32)
    slot = lax.broadcasted_iota(jnp.int32, (slots, tokens), 0)
    live = slot < total
    match_live = jnp.where(live & (token == index), 1.0, 0.0)
    match_fill = jnp.where(token == jnp.where(live, index, index[0:1, :]), 1.0, 0.0)
    kept = jnp.sum(match_live, axis=0, keepdims=True)
    kept_slot = jnp.sum(match_live * slot.astype(jnp.float32), axis=0, keepdims=True)
    row = lax.broadcasted_iota(jnp.int32, (tokens, tokens), 0)
    col = lax.broadcasted_iota(jnp.int32, (tokens, tokens), 1)
    before = jnp.where(row < col, 1.0, 0.0).astype(jnp.bfloat16)
    left = jnp.broadcast_to(1.0 - kept, (16, tokens)).astype(jnp.bfloat16)
    rank = one_hot_dot(left, before)[0:1, :]
    place = jnp.where(kept > 0.5, kept_slot, total.astype(jnp.float32) + rank)
    order = jnp.where(row.astype(jnp.float32) == place, 1.0, 0.0).astype(jnp.bfloat16)

    scale = HEAD_DIM ** (-0.5)
    match_live = match_live.astype(jnp.bfloat16)
    match_fill = match_fill.astype(jnp.bfloat16)
    query = one_hot_dot(match_live, eq_ref[0]) * scale
    slot_wide = lax.broadcasted_iota(jnp.int32, (slots, cols), 0)
    query = jnp.where(slot_wide < total, query, DEAD)
    key = one_hot_dot(match_fill, ek_ref[0])
    value = one_hot_dot(match_live, ev_ref[0])
    dec_key = one_hot_dot(order, dk_ref[0])
    dec_query = dq_ref[0].astype(jnp.float32) * scale
    text_key = tk_ref[0].astype(jnp.float32)
    text_value = tv_ref[0].astype(jnp.float32)
    mask_row = jnp.broadcast_to(mask_ref[...].astype(jnp.float32), (16, cols))

    def low(block, head):
        tile = block[:, (head // 2) * LANES : (head // 2 + 1) * LANES]
        return tile if head % 2 == 0 else pltpu.roll(tile, HEAD_DIM, 1)

    def high(block, head):
        tile = block[:, (head // 2) * LANES : (head // 2 + 1) * LANES]
        return tile if head % 2 == 1 else pltpu.roll(tile, HEAD_DIM, 1)

    def join(first, second):
        lane = lax.broadcasted_iota(jnp.int32, first.shape, 1)
        return jnp.where(lane < HEAD_DIM, first, second).astype(jnp.bfloat16)

    for head in range(heads):
        kept_tile = join(low(value, head), high(key, head))
        query_high = high(query, head)
        dec_low = low(dec_key, head)
        dq_low = low(dec_query, head)
        dq_high = high(dec_query, head)
        send_ref[head, 0:slots, :] = kept_tile
        send_ref[head, slots : 2 * slots, :] = join(dec_low[0:slots], query_high)
        send_ref[head, 2 * slots : slots + tokens, :] = join(dec_low[slots:tokens], dq_high[0:spare])
        rest = slots // 2
        send_ref[head, slots + tokens : slots + tokens + rest, :] = join(
            dq_low[spare : spare + rest], dq_high[spare + rest : tokens]
        )
        text_ref[head, 0:tokens, :] = join(low(text_value, head), high(text_key, head))
        text_ref[head, tokens : 2 * tokens, :] = join(low(text_key, head), high(text_value, head))
        text_ref[head, 2 * tokens : 2 * tokens + 16, :] = low(mask_row, head).astype(jnp.bfloat16)


def softmax_rows(query, key_ref, value_ref):
    scores = lax.dot_general(
        query, key_ref[...], (((1,), (1,)), ((), ())), preferred_element_type=jnp.float32
    )
    peak = jnp.max(scores, axis=1, keepdims=True)
    weights = jnp.exp(scores - peak).astype(jnp.bfloat16)
    sums = lax.dot_general(
        weights, value_ref[...], (((1,), (0,)), ((), ())), preferred_element_type=jnp.float32
    )
    return sums / pltpu.roll(sums, HEAD_DIM, 1)


def attend_kernel(
    blocks, slots, tokens, own_ref, pair_ref, text_ref, out_ref, ek_ref, ev_ref, dk_ref, dv_ref, eq_ref, dq_ref
):
    spare = tokens - slots
    rest = slots // 2
    chips = blocks // 2
    head = jnp.minimum(lax.axis_index("seq") // 2, text_ref.shape[0] - 1)
    text = text_ref[head]
    text_first = text[0:tokens]
    text_second = text[tokens : 2 * tokens]
    mask_row = text[2 * tokens : 2 * tokens + 1].astype(jnp.float32)

    def lane_of(rows):
        return lax.broadcasted_iota(jnp.int32, (rows, LANES), 1)

    def with_ones(tile):
        return jnp.where(lane_of(tile.shape[0]) < HEAD_DIM, tile.astype(jnp.float32), 1.0).astype(jnp.bfloat16)

    ek_ref[0:tokens, :] = text_first
    ev_ref[0:tokens, :] = with_ones(text_first)
    dk_ref[0:tokens, :] = text_second
    dv_ref[0:tokens, :] = with_ones(text_first)
    for block in range(blocks):
        own = block < chips
        got = own_ref.at[block] if own else pair_ref.at[block - chips]
        kept = got[0:slots, :]
        mixed = got[slots : 2 * slots, :].astype(jnp.float32)
        tail = got[2 * slots : slots + tokens, :].astype(jnp.float32)
        base = tokens + block * slots
        low_slot = lane_of(slots) < HEAD_DIM
        live = mixed < DEAD_EDGE
        ek_ref[base : base + slots, :] = kept
        ev_ref[base : base + slots, :] = jnp.where(
            low_slot, kept.astype(jnp.float32), jnp.where(live, 1.0, 0.0)
        ).astype(jnp.bfloat16)
        eq_ref[block * slots : block * slots + slots, :] = jnp.where(low_slot, 0.0, mixed).astype(jnp.bfloat16)
        base = tokens + block * tokens
        dk_ref[base : base + slots, :] = mixed.astype(jnp.bfloat16)
        dk_ref[base + slots : base + tokens, :] = tail.astype(jnp.bfloat16)
        if own:
            last = got[slots + tokens : slots + tokens + rest, :].astype(jnp.float32)
            base = block * tokens
            dq_ref[base : base + spare, :] = jnp.where(
                lane_of(spare) < HEAD_DIM, pltpu.roll(tail, HEAD_DIM, 1), 0.0
            ).astype(jnp.bfloat16)
            low_rest = lane_of(rest) < HEAD_DIM
            dq_ref[base + spare : base + spare + rest, :] = jnp.where(low_rest, last, 0.0).astype(jnp.bfloat16)
            dq_ref[base + spare + rest : base + tokens, :] = jnp.where(
                low_rest, pltpu.roll(last, HEAD_DIM, 1), 0.0
            ).astype(jnp.bfloat16)

    enc_group = 2
    enc_rows = enc_group * slots

    def encode(step, carry):
        first = pl.multiple_of(step * enc_rows, enc_rows)
        found = softmax_rows(eq_ref[pl.ds(first, enc_rows), :], ek_ref, ev_ref)
        for inner in range(enc_group):
            block = step * enc_group + inner
            mixed = eq_ref[pl.ds(first + inner * slots, slots), :].astype(jnp.float32)
            live = pltpu.roll(mixed, HEAD_DIM, 1) < DEAD_EDGE
            rows = jnp.where(live, found[inner * slots : (inner + 1) * slots], mask_row)
            base = pl.multiple_of(tokens + block * tokens, tokens)
            dv_ref[pl.ds(base, slots), :] = jnp.where(
                lane_of(slots) < HEAD_DIM, rows, 1.0
            ).astype(jnp.bfloat16)
            dv_ref[pl.ds(base + slots, spare), :] = jnp.where(
                lane_of(spare) < HEAD_DIM, mask_row, 1.0
            ).astype(jnp.bfloat16)
        return carry

    lax.fori_loop(0, blocks // enc_group, encode, 0)

    dec_group = 2
    dec_rows = dec_group * tokens

    def decode(step, carry):
        first = pl.multiple_of(step * dec_rows, dec_rows)
        found = softmax_rows(dq_ref[pl.ds(first, dec_rows), :], dk_ref, dv_ref)
        for inner in range(dec_group):
            rows = found[inner * tokens : (inner + 1) * tokens]
            out_ref[step * dec_group + inner] = jnp.where(
                lane_of(tokens // 2) < HEAD_DIM,
                rows[0 : tokens // 2],
                pltpu.roll(rows[tokens // 2 :], HEAD_DIM, 1),
            ).astype(jnp.bfloat16)
        return carry

    lax.fori_loop(0, chips // dec_group, decode, 0)


def sums_kernel(got_ref, gain_ref, target_ref, att_ref, sums_ref):
    tokens, cols = att_ref.shape
    half = tokens // 2
    low = lax.broadcasted_iota(jnp.int32, (half, LANES), 1) < HEAD_DIM
    for tile in range(cols // LANES):
        even = got_ref[2 * tile].astype(jnp.float32)
        odd = got_ref[2 * tile + 1].astype(jnp.float32)
        span = slice(tile * LANES, (tile + 1) * LANES)
        att_ref[0:half, span] = jnp.where(low, even, pltpu.roll(odd, HEAD_DIM, 1))
        att_ref[half:tokens, span] = jnp.where(low, pltpu.roll(even, HEAD_DIM, 1), odd)
    att = att_ref[...]
    gained = att * gain_ref[...].astype(jnp.float32)
    target = target_ref[0].astype(jnp.float32)
    lane = lax.broadcasted_iota(jnp.int32, (tokens, LANES), 1)

    def over(block):
        return jnp.sum(block, axis=1, keepdims=True)

    table = jnp.where(
        lane == 0,
        over(att * att),
        jnp.where(lane == 1, over(gained * gained), jnp.where(lane == 2, over(gained * target), over(target * target))),
    )
    sums_ref[...] = jnp.transpose(table)[0:8, :]


def finish_kernel(count, steps_ref, att_ref, gain_ref, sums_ref, out_ref, loss_ref):
    tokens, cols = att_ref.shape
    total_cols = cols * count
    sums = sums_ref[...]
    square = sums[0:1, :]
    factor = lax.rsqrt(square / total_cols + 1e-06)
    error = factor * factor * sums[1:2, :] - 2.0 * factor * sums[2:3, :] + sums[3:4, :]
    weight = 1.0 / (0.1 + jnp.full((1, 1), steps_ref[0], jnp.int32).astype(jnp.float32) / 999.0)
    loss_ref[...] = jnp.broadcast_to(weight * jnp.sum(error, axis=1, keepdims=True), loss_ref.shape)
    column = jnp.transpose(jnp.broadcast_to(factor, (tokens, tokens)))[:, 0:1]
    out_ref[0] = (att_ref[...] * column * gain_ref[...].astype(jnp.float32)).astype(jnp.bfloat16)


def local(
    enc_query,
    enc_key,
    enc_value,
    keep_index,
    keep_count,
    text_key,
    text_value,
    dec_query,
    dec_key,
    mask_value,
    norm_gain,
    target,
    timesteps,
):
    images, seq, heads = (lax.axis_size(name) for name in ("dp", "seq", "head"))
    tokens, cols = enc_query.shape[1:]
    slots = keep_index.shape[1]
    local_heads = cols // HEAD_DIM
    chips = seq // 2
    packed = slots + tokens + slots // 2
    same_core = [[2 * chip + core for chip in range(chips)] for core in range(2)]
    bf16, f32 = jnp.bfloat16, jnp.float32
    gain = norm_gain.reshape(1, cols)

    send, text = pl.pallas_call(
        pack_kernel,
        out_shape=(
            jax.ShapeDtypeStruct((chips, packed, LANES), bf16),
            jax.ShapeDtypeStruct((local_heads, 2 * tokens + 16, LANES), bf16),
        ),
        in_specs=[pl.BlockSpec(memory_space=pltpu.SMEM)] + [pl.BlockSpec(memory_space=pl.ANY)] * 9,
        out_specs=tuple(vmem(2)),
        scratch_shapes=[pltpu.VMEM((1, slots), jnp.int32)]
        + [pltpu.VMEM((1, tokens, cols), bf16)] * 7
        + [pltpu.VMEM((1, cols), bf16), pltpu.SemaphoreType.DMA((9,))],
        compiler_params=params(),
        name="pack",
    )(
        keep_count,
        keep_index,
        enc_query,
        enc_key,
        enc_value,
        dec_query,
        dec_key,
        text_key,
        text_value,
        mask_value.reshape(1, cols),
    )
    own = lax.all_to_all(send, "seq", 0, 0, axis_index_groups=same_core, tiled=True)
    pair = lax.ppermute(own, "seq", [(source, source ^ 1) for source in range(seq)])
    out = pl.pallas_call(
        functools.partial(attend_kernel, seq, slots, tokens),
        out_shape=jax.ShapeDtypeStruct((chips, tokens // 2, LANES), bf16),
        in_specs=vmem(3),
        out_specs=vmem(1)[0],
        scratch_shapes=[
            pltpu.VMEM((tokens + seq * slots, LANES), bf16),
            pltpu.VMEM((tokens + seq * slots, LANES), bf16),
            pltpu.VMEM((tokens + seq * tokens, LANES), bf16),
            pltpu.VMEM((tokens + seq * tokens, LANES), bf16),
            pltpu.VMEM((seq * slots, LANES), bf16),
            pltpu.VMEM((seq * tokens // 2, LANES), bf16),
        ],
        compiler_params=params(),
        name="attend",
    )(own, pair, text)
    got = lax.all_to_all(out, "seq", 0, 0, axis_index_groups=same_core, tiled=True)
    att, sums = pl.pallas_call(
        sums_kernel,
        out_shape=(
            jax.ShapeDtypeStruct((tokens, cols), f32),
            jax.ShapeDtypeStruct((8, tokens), f32),
        ),
        in_specs=vmem(3),
        out_specs=tuple(vmem(2)),
        compiler_params=params(),
        name="sums",
    )(got, gain, target)
    sums = lax.psum(sums, "head")
    decoded, loss = pl.pallas_call(
        functools.partial(finish_kernel, heads),
        out_shape=(
            jax.ShapeDtypeStruct((1, tokens, cols), bf16),
            jax.ShapeDtypeStruct((1, LANES), f32),
        ),
        in_specs=[pl.BlockSpec(memory_space=pltpu.SMEM)] + vmem(3),
        out_specs=tuple(vmem(2)),
        compiler_params=params(),
        name="finish",
    )(timesteps, att, gain, sums)
    total_loss = lax.psum(lax.psum(loss[0, 0], "seq"), "dp") / (images * tokens * seq * cols * heads)
    return (decoded, total_loss)


def solution(mesh):
    placed = (
        P("dp", "seq", "head"),
        P("dp", "seq", "head"),
        P("dp", "seq", "head"),
        P("dp", "seq"),
        P("dp", "seq"),
        P("dp", None, "head"),
        P("dp", None, "head"),
        P("dp", "seq", "head"),
        P("dp", "seq", "head"),
        P("head"),
        P("head"),
        P("dp", "seq", "head"),
        P("dp"),
    )
    return jax.shard_map(
        local, mesh=mesh, in_specs=placed, out_specs=(P("dp", "seq", "head"), P()), check_vma=False
    )
```

```python
import functools

import jax
import jax.numpy as jnp
from jax import lax
from jax.experimental import pallas as pl
from jax.experimental.pallas import tpu as pltpu
from jax.sharding import PartitionSpec as P

HEAD_DIM = 64
LANES = 128
DEAD = 1024.0
DEAD_EDGE = 512.0
MIB = 1024 * 1024


def params(mib=40):
    return pltpu.CompilerParams(vmem_limit_bytes=mib * MIB)


def vmem(count):
    return [pl.BlockSpec(memory_space=pltpu.VMEM)] * count


def one_hot_dot(table, rows):
    return lax.dot_general(
        table, rows, (((1,), (0,)), ((), ())), preferred_element_type=jnp.float32
    )


def pack_kernel(
    count_ref, index_hbm, eq_hbm, ek_hbm, ev_hbm, dq_hbm, dk_hbm, tk_hbm, tv_hbm, mask_hbm, send_ref, text_ref, *scratch
):
    *held, sems = scratch
    given = (index_hbm, eq_hbm, ek_hbm, ev_hbm, dq_hbm, dk_hbm, tk_hbm, tv_hbm, mask_hbm)
    copies = [
        pltpu.make_async_copy(source, place, sems.at[number])
        for number, (source, place) in enumerate(zip(given, held))
    ]
    for copy in copies:
        copy.start()
    for copy in copies:
        copy.wait()
    index_ref, eq_ref, ek_ref, ev_ref, dq_ref, dk_ref, tk_ref, tv_ref, mask_ref = held
    tokens, cols = eq_ref.shape[1:]
    slots = index_ref.shape[1]
    heads = cols // HEAD_DIM
    spare = tokens - slots
    total = count_ref[0, 0]
    index = jnp.broadcast_to(index_ref[...].astype(jnp.float32), (tokens, slots))
    index = jnp.transpose(index)
    token = lax.broadcasted_iota(jnp.int32, (slots, tokens), 1).astype(jnp.float32)
    slot = lax.broadcasted_iota(jnp.int32, (slots, tokens), 0)
    live = slot < total
    match_live = jnp.where(live & (token == index), 1.0, 0.0)
    match_fill = jnp.where(token == jnp.where(live, index, index[0:1, :]), 1.0, 0.0)
    kept = jnp.sum(match_live, axis=0, keepdims=True)
    kept_slot = jnp.sum(match_live * slot.astype(jnp.float32), axis=0, keepdims=True)
    row = lax.broadcasted_iota(jnp.int32, (tokens, tokens), 0)
    col = lax.broadcasted_iota(jnp.int32, (tokens, tokens), 1)
    before = jnp.where(row < col, 1.0, 0.0).astype(jnp.bfloat16)
    left = jnp.broadcast_to(1.0 - kept, (16, tokens)).astype(jnp.bfloat16)
    rank = one_hot_dot(left, before)[0:1, :]
    place = jnp.where(kept > 0.5, kept_slot, total.astype(jnp.float32) + rank)
    order = jnp.where(row.astype(jnp.float32) == place, 1.0, 0.0).astype(jnp.bfloat16)

    scale = HEAD_DIM ** (-0.5)
    match_live = match_live.astype(jnp.bfloat16)
    match_fill = match_fill.astype(jnp.bfloat16)
    query = one_hot_dot(match_live, eq_ref[0]) * scale
    slot_wide = lax.broadcasted_iota(jnp.int32, (slots, cols), 0)
    query = jnp.where(slot_wide < total, query, DEAD)
    key = one_hot_dot(match_fill, ek_ref[0])
    value = one_hot_dot(match_live, ev_ref[0])
    dec_key = one_hot_dot(order, dk_ref[0])
    dec_query = dq_ref[0].astype(jnp.float32) * scale
    text_key = tk_ref[0].astype(jnp.float32)
    text_value = tv_ref[0].astype(jnp.float32)
    mask_row = jnp.broadcast_to(mask_ref[...].astype(jnp.float32).reshape(1, cols), (16, cols))

    def low(block, head):
        tile = block[:, (head // 2) * LANES : (head // 2 + 1) * LANES]
        return tile if head % 2 == 0 else pltpu.roll(tile, HEAD_DIM, 1)

    def high(block, head):
        tile = block[:, (head // 2) * LANES : (head // 2 + 1) * LANES]
        return tile if head % 2 == 1 else pltpu.roll(tile, HEAD_DIM, 1)

    def join(first, second):
        lane = lax.broadcasted_iota(jnp.int32, first.shape, 1)
        return jnp.where(lane < HEAD_DIM, first, second).astype(jnp.bfloat16)

    for head in range(heads):
        kept_tile = join(low(value, head), high(key, head))
        query_high = high(query, head)
        dec_low = low(dec_key, head)
        dq_low = low(dec_query, head)
        dq_high = high(dec_query, head)
        send_ref[head, 0:slots, :] = kept_tile
        send_ref[head, slots : 2 * slots, :] = join(dec_low[0:slots], query_high)
        send_ref[head, 2 * slots : slots + tokens, :] = join(dec_low[slots:tokens], dq_high[0:spare])
        rest = slots // 2
        send_ref[head, slots + tokens : slots + tokens + rest, :] = join(
            dq_low[spare : spare + rest], dq_high[spare + rest : tokens]
        )
        text_ref[head, 0:tokens, :] = join(low(text_value, head), high(text_key, head))
        text_ref[head, tokens : 2 * tokens, :] = join(low(text_key, head), high(text_value, head))
        text_ref[head, 2 * tokens : 2 * tokens + 16, :] = low(mask_row, head).astype(jnp.bfloat16)


def put_scores(query, key_ref, place, peak):
    keys = key_ref.shape[0]
    largest = None
    for first in range(0, keys, 2 * LANES):
        last = min(keys, first + 2 * LANES)
        part = lax.dot_general(
            query, key_ref[first:last, :], (((1,), (1,)), ((), ())), preferred_element_type=jnp.float32
        )
        place[:, first:last] = part
        for lane in range(0, last - first, LANES):
            tile = part[:, lane : lane + LANES]
            largest = tile if largest is None else jnp.maximum(largest, tile)
    peak[...] = largest


def weigh(place, peak, value_ref):
    keys = value_ref.shape[0]
    top = jnp.max(peak[...], axis=1, keepdims=True)
    weights = jnp.exp(place[:, 0:keys] - top).astype(jnp.bfloat16)
    sums = lax.dot_general(
        weights, value_ref[...], (((1,), (0,)), ((), ())), preferred_element_type=jnp.float32
    )
    return sums / pltpu.roll(sums, HEAD_DIM, 1)


def over_tiles(tiles, rows, query_ref, key_ref, value_ref, buffers, use):
    (one, one_peak), (two, two_peak) = buffers

    def query(tile):
        return query_ref[pl.ds(pl.multiple_of(tile * rows, rows), rows), :]

    put_scores(query(0), key_ref, one, one_peak)

    def pair(step, carry):
        tile = 2 * step
        put_scores(query(tile + 1), key_ref, two, two_peak)
        use(tile, weigh(one, one_peak, value_ref))
        put_scores(query(jnp.minimum(tile + 2, tiles - 1)), key_ref, one, one_peak)
        use(tile + 1, weigh(two, two_peak, value_ref))
        return carry

    lax.fori_loop(0, tiles // 2, pair, 0)


def attend_kernel(
    blocks, slots, tokens, own_ref, pair_ref, text_ref, out_ref, ek_ref, ev_ref, dk_ref, dv_ref, eq_ref, dq_ref, found_ref, *places
):
    spare = tokens - slots
    rest = slots // 2
    chips = blocks // 2
    head = jnp.minimum(lax.axis_index("seq") // 2, text_ref.shape[0] - 1)
    text = text_ref[head]
    text_first = text[0:tokens]
    text_second = text[tokens : 2 * tokens]
    mask_row = text[2 * tokens : 2 * tokens + 1].astype(jnp.float32)

    def lane_of(rows):
        return lax.broadcasted_iota(jnp.int32, (rows, LANES), 1)

    def with_ones(tile):
        return jnp.where(lane_of(tile.shape[0]) < HEAD_DIM, tile.astype(jnp.float32), 1.0).astype(jnp.bfloat16)

    ek_ref[0:tokens, :] = text_first
    ev_ref[0:tokens, :] = with_ones(text_first)
    dk_ref[0:tokens, :] = text_second
    dv_ref[0:tokens, :] = with_ones(text_first)
    for block in range(blocks):
        own = block < chips
        got = own_ref.at[block] if own else pair_ref.at[block - chips]
        kept = got[0:slots, :]
        mixed = got[slots : 2 * slots, :].astype(jnp.float32)
        tail = got[2 * slots : slots + tokens, :].astype(jnp.float32)
        base = tokens + block * slots
        low_slot = lane_of(slots) < HEAD_DIM
        live = mixed < DEAD_EDGE
        ek_ref[base : base + slots, :] = kept
        ev_ref[base : base + slots, :] = jnp.where(
            low_slot, kept.astype(jnp.float32), jnp.where(live, 1.0, 0.0)
        ).astype(jnp.bfloat16)
        eq_ref[block * slots : block * slots + slots, :] = jnp.where(low_slot, 0.0, mixed).astype(jnp.bfloat16)
        base = tokens + block * tokens
        dk_ref[base : base + slots, :] = mixed.astype(jnp.bfloat16)
        dk_ref[base + slots : base + tokens, :] = tail.astype(jnp.bfloat16)
        if own:
            last = got[slots + tokens : slots + tokens + rest, :].astype(jnp.float32)
            base = block * tokens
            dq_ref[base : base + spare, :] = jnp.where(
                lane_of(spare) < HEAD_DIM, pltpu.roll(tail, HEAD_DIM, 1), 0.0
            ).astype(jnp.bfloat16)
            low_rest = lane_of(rest) < HEAD_DIM
            dq_ref[base + spare : base + spare + rest, :] = jnp.where(low_rest, last, 0.0).astype(jnp.bfloat16)
            dq_ref[base + spare + rest : base + tokens, :] = jnp.where(
                low_rest, pltpu.roll(last, HEAD_DIM, 1), 0.0
            ).astype(jnp.bfloat16)

    buffers = (places[0:2], places[2:4])
    rows = 2 * tokens

    def keep(tile, found):
        found_ref[pl.ds(pl.multiple_of(tile * rows, rows), rows), :] = found

    over_tiles(blocks * slots // rows, rows, eq_ref, ek_ref, ev_ref, buffers, keep)
    fill = jnp.where(lane_of(spare) < HEAD_DIM, mask_row, 1.0).astype(jnp.bfloat16)
    for block in range(blocks):
        span = slice(block * slots, (block + 1) * slots)
        live = pltpu.roll(eq_ref[span, :].astype(jnp.float32), HEAD_DIM, 1) < DEAD_EDGE
        base = tokens + block * tokens
        dv_ref[base : base + slots, :] = jnp.where(
            lane_of(slots) < HEAD_DIM, jnp.where(live, found_ref[span, :], mask_row), 1.0
        ).astype(jnp.bfloat16)
        dv_ref[base + slots : base + tokens, :] = fill

    def give(tile, found):
        half = tokens // 2
        for inner in range(2):
            first = inner * tokens
            out_ref[2 * tile + inner] = jnp.where(
                lane_of(half) < HEAD_DIM,
                found[first : first + half],
                pltpu.roll(found[first + half : first + tokens], HEAD_DIM, 1),
            ).astype(jnp.bfloat16)

    over_tiles(chips * tokens // rows, rows, dq_ref, dk_ref, dv_ref, buffers, give)


def sums_kernel(got_ref, gain_ref, target_ref, att_ref, sums_ref):
    tokens, cols = att_ref.shape
    half = tokens // 2
    low = lax.broadcasted_iota(jnp.int32, (half, LANES), 1) < HEAD_DIM
    for tile in range(cols // LANES):
        even = got_ref[2 * tile].astype(jnp.float32)
        odd = got_ref[2 * tile + 1].astype(jnp.float32)
        span = slice(tile * LANES, (tile + 1) * LANES)
        att_ref[0:half, span] = jnp.where(low, even, pltpu.roll(odd, HEAD_DIM, 1))
        att_ref[half:tokens, span] = jnp.where(low, pltpu.roll(even, HEAD_DIM, 1), odd)
    att = att_ref[...]
    gained = att * gain_ref[...].astype(jnp.float32)
    target = target_ref[0].astype(jnp.float32)
    lane = lax.broadcasted_iota(jnp.int32, (tokens, LANES), 1)

    def over(block):
        return jnp.sum(block, axis=1, keepdims=True)

    table = jnp.where(
        lane == 0,
        over(att * att),
        jnp.where(lane == 1, over(gained * gained), jnp.where(lane == 2, over(gained * target), over(target * target))),
    )
    sums_ref[...] = jnp.broadcast_to(jnp.transpose(table)[None, 0:8, :], sums_ref.shape)


def finish_kernel(steps_ref, att_ref, gain_ref, sums_ref, out_ref, loss_ref):
    tokens, cols = att_ref.shape
    total_cols = cols * sums_ref.shape[0]
    sums = jnp.sum(sums_ref[...], axis=0)
    square = sums[0:1, :]
    factor = lax.rsqrt(square / total_cols + 1e-06)
    error = factor * factor * sums[1:2, :] - 2.0 * factor * sums[2:3, :] + sums[3:4, :]
    weight = 1.0 / (0.1 + jnp.full((1, 1), steps_ref[0], jnp.int32).astype(jnp.float32) / 999.0)
    loss_ref[...] = jnp.broadcast_to(weight * jnp.sum(error, axis=1, keepdims=True), loss_ref.shape)
    column = jnp.transpose(jnp.broadcast_to(factor, (tokens, tokens)))[:, 0:1]
    out_ref[0] = (att_ref[...] * column * gain_ref[...].astype(jnp.float32)).astype(jnp.bfloat16)


def fold_kernel(count, got_ref, sum_ref):
    total = jnp.sum(got_ref[...], axis=0) / count
    if len(sum_ref.shape) == 2:
        sum_ref[...] = total[0:1, 0:1]
    else:
        sum_ref[...] = jnp.broadcast_to(total[None], sum_ref.shape)


def fold(parts, axis, out_shape, count):
    got = lax.all_to_all(parts, axis, 0, 0, tiled=True)
    return pl.pallas_call(
        functools.partial(fold_kernel, count),
        out_shape=jax.ShapeDtypeStruct(out_shape, jnp.float32),
        in_specs=vmem(1),
        out_specs=vmem(1)[0],
        compiler_params=params(),
        name="fold",
    )(got)


def local(
    enc_query,
    enc_key,
    enc_value,
    keep_index,
    keep_count,
    text_key,
    text_value,
    dec_query,
    dec_key,
    mask_value,
    norm_gain,
    target,
    timesteps,
):
    images, seq, heads = (lax.axis_size(name) for name in ("dp", "seq", "head"))
    tokens, cols = enc_query.shape[1:]
    slots = keep_index.shape[1]
    local_heads = cols // HEAD_DIM
    chips = seq // 2
    packed = slots + tokens + slots // 2
    same_core = [[2 * chip + core for chip in range(chips)] for core in range(2)]
    bf16, f32 = jnp.bfloat16, jnp.float32
    gain = norm_gain.reshape(1, cols)

    send, text = pl.pallas_call(
        pack_kernel,
        out_shape=(
            jax.ShapeDtypeStruct((chips, packed, LANES), bf16),
            jax.ShapeDtypeStruct((local_heads, 2 * tokens + 16, LANES), bf16),
        ),
        in_specs=[pl.BlockSpec(memory_space=pltpu.SMEM)] + [pl.BlockSpec(memory_space=pltpu.HBM)] * 9,
        out_specs=tuple(vmem(2)),
        scratch_shapes=[pltpu.VMEM((1, slots), jnp.int32)]
        + [pltpu.VMEM((1, tokens, cols), bf16)] * 7
        + [pltpu.VMEM((cols,), bf16), pltpu.SemaphoreType.DMA((9,))],
        compiler_params=params(60),
        name="pack",
    )(
        keep_count,
        keep_index,
        enc_query,
        enc_key,
        enc_value,
        dec_query,
        dec_key,
        text_key,
        text_value,
        mask_value,
    )
    own = lax.all_to_all(send, "seq", 0, 0, axis_index_groups=same_core, tiled=True)
    pair = lax.ppermute(own, "seq", [(source, source ^ 1) for source in range(seq)])
    out = pl.pallas_call(
        functools.partial(attend_kernel, seq, slots, tokens),
        out_shape=jax.ShapeDtypeStruct((chips, tokens // 2, LANES), bf16),
        in_specs=vmem(3),
        out_specs=vmem(1)[0],
        scratch_shapes=[
            pltpu.VMEM((tokens + seq * slots, LANES), bf16),
            pltpu.VMEM((tokens + seq * slots, LANES), bf16),
            pltpu.VMEM((tokens + seq * tokens, LANES), bf16),
            pltpu.VMEM((tokens + seq * tokens, LANES), bf16),
            pltpu.VMEM((seq * slots, LANES), bf16),
            pltpu.VMEM((seq * tokens // 2, LANES), bf16),
            pltpu.VMEM((seq * slots, LANES), f32),
        ]
        + [pltpu.VMEM((2 * tokens, tokens + seq * tokens), f32), pltpu.VMEM((2 * tokens, LANES), f32)] * 2,
        compiler_params=params(),
        name="attend",
    )(own, pair, text)
    got = lax.all_to_all(out, "seq", 0, 0, axis_index_groups=same_core, tiled=True)
    att, sums = pl.pallas_call(
        sums_kernel,
        out_shape=(
            jax.ShapeDtypeStruct((tokens, cols), f32),
            jax.ShapeDtypeStruct((heads, 8, tokens), f32),
        ),
        in_specs=vmem(3),
        out_specs=tuple(vmem(2)),
        compiler_params=params(),
        name="sums",
    )(got, gain, target)
    sums = lax.all_to_all(sums, "head", 0, 0, tiled=True)
    decoded, loss = pl.pallas_call(
        finish_kernel,
        out_shape=(
            jax.ShapeDtypeStruct((1, tokens, cols), bf16),
            jax.ShapeDtypeStruct((seq, 8, LANES), f32),
        ),
        in_specs=[pl.BlockSpec(memory_space=pltpu.SMEM)] + vmem(3),
        out_specs=tuple(vmem(2)),
        compiler_params=params(),
        name="finish",
    )(timesteps, att, gain, sums)
    loss = fold(loss, "seq", (images, 8, LANES), 1.0)
    loss = fold(loss, "dp", (1, 1), float(images * tokens * seq * cols * heads))
    total_loss = loss.reshape(())
    return (decoded, total_loss)


def solution(mesh):
    placed = (
        P("dp", "seq", "head"),
        P("dp", "seq", "head"),
        P("dp", "seq", "head"),
        P("dp", "seq"),
        P("dp", "seq"),
        P("dp", None, "head"),
        P("dp", None, "head"),
        P("dp", "seq", "head"),
        P("dp", "seq", "head"),
        P("head"),
        P("head"),
        P("dp", "seq", "head"),
        P("dp"),
    )
    return jax.shard_map(
        local, mesh=mesh, in_specs=placed, out_specs=(P("dp", "seq", "head"), P()), check_vma=False
    )
```

```python
import functools

import jax
import jax.numpy as jnp
from jax import lax
from jax.experimental import pallas as pl
from jax.experimental.pallas import tpu as pltpu
from jax.sharding import PartitionSpec as P

HEAD_DIM = 64
LANES = 128
DEAD = 1024.0
DEAD_EDGE = 512.0
MIB = 1024 * 1024


def params(mib=40):
    return pltpu.CompilerParams(vmem_limit_bytes=mib * MIB)


def vmem(count):
    return [pl.BlockSpec(memory_space=pltpu.VMEM)] * count


def one_hot_dot(table, rows):
    return lax.dot_general(
        table, rows, (((1,), (0,)), ((), ())), preferred_element_type=jnp.float32
    )


def pack_kernel(
    count_ref, index_hbm, eq_hbm, ek_hbm, ev_hbm, dq_hbm, dk_hbm, tk_hbm, tv_hbm, mask_hbm, send_ref, text_ref, *scratch
):
    *held, sems = scratch
    given = (index_hbm, eq_hbm, ek_hbm, ev_hbm, dq_hbm, dk_hbm, tk_hbm, tv_hbm, mask_hbm)
    copies = [
        pltpu.make_async_copy(source, place, sems.at[number])
        for number, (source, place) in enumerate(zip(given, held))
    ]
    for copy in copies:
        copy.start()
    copies[0].wait()
    index_ref, eq_ref, ek_ref, ev_ref, dq_ref, dk_ref, tk_ref, tv_ref, mask_ref = held
    tokens, cols = eq_ref.shape[1:]
    slots = index_ref.shape[1]
    heads = cols // HEAD_DIM
    spare = tokens - slots
    total = count_ref[0, 0]
    index = jnp.broadcast_to(index_ref[...].astype(jnp.float32), (tokens, slots))
    index = jnp.transpose(index)
    token = lax.broadcasted_iota(jnp.int32, (slots, tokens), 1).astype(jnp.float32)
    slot = lax.broadcasted_iota(jnp.int32, (slots, tokens), 0)
    live = slot < total
    match_live = jnp.where(live & (token == index), 1.0, 0.0)
    match_fill = jnp.where(token == jnp.where(live, index, index[0:1, :]), 1.0, 0.0)
    kept = jnp.sum(match_live, axis=0, keepdims=True)
    kept_slot = jnp.sum(match_live * slot.astype(jnp.float32), axis=0, keepdims=True)
    row = lax.broadcasted_iota(jnp.int32, (tokens, tokens), 0)
    col = lax.broadcasted_iota(jnp.int32, (tokens, tokens), 1)
    before = jnp.where(row < col, 1.0, 0.0).astype(jnp.bfloat16)
    left = jnp.broadcast_to(1.0 - kept, (16, tokens)).astype(jnp.bfloat16)
    rank = one_hot_dot(left, before)[0:1, :]
    place = jnp.where(kept > 0.5, kept_slot, total.astype(jnp.float32) + rank)
    order = jnp.where(row.astype(jnp.float32) == place, 1.0, 0.0).astype(jnp.bfloat16)

    for copy in copies[1:]:
        copy.wait()
    scale = HEAD_DIM ** (-0.5)
    match_live = match_live.astype(jnp.bfloat16)
    match_fill = match_fill.astype(jnp.bfloat16)
    query = one_hot_dot(match_live, eq_ref[0]) * scale
    slot_wide = lax.broadcasted_iota(jnp.int32, (slots, cols), 0)
    query = jnp.where(slot_wide < total, query, DEAD)
    key = one_hot_dot(match_fill, ek_ref[0])
    value = one_hot_dot(match_live, ev_ref[0])
    dec_key = one_hot_dot(order, dk_ref[0])
    dec_query = dq_ref[0].astype(jnp.float32) * scale
    text_key = tk_ref[0].astype(jnp.float32)
    text_value = tv_ref[0].astype(jnp.float32)
    mask_row = jnp.broadcast_to(mask_ref[...].astype(jnp.float32).reshape(1, cols), (16, cols))

    def low(block, head):
        tile = block[:, (head // 2) * LANES : (head // 2 + 1) * LANES]
        return tile if head % 2 == 0 else pltpu.roll(tile, HEAD_DIM, 1)

    def high(block, head):
        tile = block[:, (head // 2) * LANES : (head // 2 + 1) * LANES]
        return tile if head % 2 == 1 else pltpu.roll(tile, HEAD_DIM, 1)

    def join(first, second):
        lane = lax.broadcasted_iota(jnp.int32, first.shape, 1)
        return jnp.where(lane < HEAD_DIM, first, second).astype(jnp.bfloat16)

    for head in range(heads):
        kept_tile = join(low(value, head), high(key, head))
        query_high = high(query, head)
        dec_low = low(dec_key, head)
        dq_low = low(dec_query, head)
        dq_high = high(dec_query, head)
        send_ref[head, 0:slots, :] = kept_tile
        send_ref[head, slots : 2 * slots, :] = join(dec_low[0:slots], query_high)
        send_ref[head, 2 * slots : slots + tokens, :] = join(dec_low[slots:tokens], dq_high[0:spare])
        rest = slots // 2
        send_ref[head, slots + tokens : slots + tokens + rest, :] = join(
            dq_low[spare : spare + rest], dq_high[spare + rest : tokens]
        )
        text_ref[head, 0:tokens, :] = join(low(text_value, head), high(text_key, head))
        text_ref[head, tokens : 2 * tokens, :] = join(low(text_key, head), high(text_value, head))
        text_ref[head, 2 * tokens : 2 * tokens + 16, :] = low(mask_row, head).astype(jnp.bfloat16)


def put_scores(query, key_ref, place, peak):
    keys = key_ref.shape[0]
    largest = None
    for first in range(0, keys, 2 * LANES):
        last = min(keys, first + 2 * LANES)
        part = lax.dot_general(
            query, key_ref[first:last, :], (((1,), (1,)), ((), ())), preferred_element_type=jnp.float32
        )
        place[:, first:last] = part
        for lane in range(0, last - first, LANES):
            tile = part[:, lane : lane + LANES]
            largest = tile if largest is None else jnp.maximum(largest, tile)
    peak[...] = largest


def weigh(place, peak, value_ref):
    keys = value_ref.shape[0]
    top = jnp.max(peak[...], axis=1, keepdims=True)
    weights = jnp.exp(place[:, 0:keys] - top).astype(jnp.bfloat16)
    sums = lax.dot_general(
        weights, value_ref[...], (((1,), (0,)), ((), ())), preferred_element_type=jnp.float32
    )
    return sums / pltpu.roll(sums, HEAD_DIM, 1)


def over_tiles(tiles, rows, query_ref, key_ref, value_ref, buffers, use, after):
    (one, one_peak), (two, two_peak) = buffers

    def put(tile, buffer):
        put_scores(query_ref[pl.ds(pl.multiple_of(tile * rows, rows), rows), :], key_ref, *buffer)

    def pair(step, carry):
        tile = 2 * step
        put(tile + 1, buffers[1])
        use(tile, weigh(one, one_peak, value_ref))
        put(tile + 2, buffers[0])
        use(tile + 1, weigh(two, two_peak, value_ref))
        return carry

    lax.fori_loop(0, tiles // 2 - 1, pair, 0)
    put(tiles - 1, buffers[1])
    use(tiles - 2, weigh(one, one_peak, value_ref))
    after()
    use(tiles - 1, weigh(two, two_peak, value_ref))


def attend_kernel(
    blocks, slots, tokens, own_ref, pair_ref, text_ref, out_ref, ek_ref, ev_ref, dk_ref, dv_ref, eq_ref, dq_ref, found_ref, *places
):
    spare = tokens - slots
    rest = slots // 2
    chips = blocks // 2
    head = jnp.minimum(lax.axis_index("seq") // 2, text_ref.shape[0] - 1)
    text = text_ref[head]
    text_first = text[0:tokens]
    text_second = text[tokens : 2 * tokens]
    mask_row = text[2 * tokens : 2 * tokens + 1].astype(jnp.float32)

    def lane_of(rows):
        return lax.broadcasted_iota(jnp.int32, (rows, LANES), 1)

    def with_ones(tile):
        return jnp.where(lane_of(tile.shape[0]) < HEAD_DIM, tile.astype(jnp.float32), 1.0).astype(jnp.bfloat16)

    ek_ref[0:tokens, :] = text_first
    ev_ref[0:tokens, :] = with_ones(text_first)
    dk_ref[0:tokens, :] = text_second
    dv_ref[0:tokens, :] = with_ones(text_first)
    for block in range(blocks):
        own = block < chips
        got = own_ref.at[block] if own else pair_ref.at[block - chips]
        kept = got[0:slots, :]
        mixed = got[slots : 2 * slots, :].astype(jnp.float32)
        tail = got[2 * slots : slots + tokens, :].astype(jnp.float32)
        base = tokens + block * slots
        low_slot = lane_of(slots) < HEAD_DIM
        live = mixed < DEAD_EDGE
        ek_ref[base : base + slots, :] = kept
        ev_ref[base : base + slots, :] = jnp.where(
            low_slot, kept.astype(jnp.float32), jnp.where(live, 1.0, 0.0)
        ).astype(jnp.bfloat16)
        eq_ref[block * slots : block * slots + slots, :] = jnp.where(low_slot, 0.0, mixed).astype(jnp.bfloat16)
        base = tokens + block * tokens
        dk_ref[base : base + slots, :] = mixed.astype(jnp.bfloat16)
        dk_ref[base + slots : base + tokens, :] = tail.astype(jnp.bfloat16)
        if own:
            last = got[slots + tokens : slots + tokens + rest, :].astype(jnp.float32)
            base = block * tokens
            dq_ref[base : base + spare, :] = jnp.where(
                lane_of(spare) < HEAD_DIM, pltpu.roll(tail, HEAD_DIM, 1), 0.0
            ).astype(jnp.bfloat16)
            low_rest = lane_of(rest) < HEAD_DIM
            dq_ref[base + spare : base + spare + rest, :] = jnp.where(low_rest, last, 0.0).astype(jnp.bfloat16)
            dq_ref[base + spare + rest : base + tokens, :] = jnp.where(
                low_rest, pltpu.roll(last, HEAD_DIM, 1), 0.0
            ).astype(jnp.bfloat16)

    buffers = (places[0:2], places[2:4])
    rows = 2 * tokens

    def keep(tile, found):
        found_ref[pl.ds(pl.multiple_of(tile * rows, rows), rows), :] = found

    put_scores(eq_ref[0:rows, :], ek_ref, *buffers[0])
    over_tiles(
        blocks * slots // rows,
        rows,
        eq_ref,
        ek_ref,
        ev_ref,
        buffers,
        keep,
        lambda: put_scores(dq_ref[0:rows, :], dk_ref, *buffers[0]),
    )
    fill = jnp.where(lane_of(spare) < HEAD_DIM, mask_row, 1.0).astype(jnp.bfloat16)
    for block in range(blocks):
        span = slice(block * slots, (block + 1) * slots)
        live = pltpu.roll(eq_ref[span, :].astype(jnp.float32), HEAD_DIM, 1) < DEAD_EDGE
        base = tokens + block * tokens
        dv_ref[base : base + slots, :] = jnp.where(
            lane_of(slots) < HEAD_DIM, jnp.where(live, found_ref[span, :], mask_row), 1.0
        ).astype(jnp.bfloat16)
        dv_ref[base + slots : base + tokens, :] = fill

    def give(tile, found):
        half = tokens // 2
        for inner in range(2):
            first = inner * tokens
            out_ref[2 * tile + inner] = jnp.where(
                lane_of(half) < HEAD_DIM,
                found[first : first + half],
                pltpu.roll(found[first + half : first + tokens], HEAD_DIM, 1),
            ).astype(jnp.bfloat16)

    over_tiles(chips * tokens // rows, rows, dq_ref, dk_ref, dv_ref, buffers, give, lambda: None)


def sums_kernel(got_ref, gain_ref, target_ref, att_ref, sums_ref):
    tokens, cols = att_ref.shape
    half = tokens // 2
    low = lax.broadcasted_iota(jnp.int32, (half, LANES), 1) < HEAD_DIM
    for tile in range(cols // LANES):
        even = got_ref[2 * tile].astype(jnp.float32)
        odd = got_ref[2 * tile + 1].astype(jnp.float32)
        span = slice(tile * LANES, (tile + 1) * LANES)
        att_ref[0:half, span] = jnp.where(low, even, pltpu.roll(odd, HEAD_DIM, 1))
        att_ref[half:tokens, span] = jnp.where(low, pltpu.roll(even, HEAD_DIM, 1), odd)
    att = att_ref[...]
    gained = att * gain_ref[...].astype(jnp.float32)
    target = target_ref[0].astype(jnp.float32)
    lane = lax.broadcasted_iota(jnp.int32, (tokens, LANES), 1)

    def over(block):
        return jnp.sum(block, axis=1, keepdims=True)

    table = jnp.where(
        lane == 0,
        over(att * att),
        jnp.where(lane == 1, over(gained * gained), jnp.where(lane == 2, over(gained * target), over(target * target))),
    )
    sums_ref[...] = jnp.broadcast_to(jnp.transpose(table)[None, 0:8, :], sums_ref.shape)


def finish_kernel(steps_ref, att_ref, gain_ref, sums_ref, out_ref, loss_ref):
    tokens, cols = att_ref.shape
    total_cols = cols * sums_ref.shape[0]
    sums = jnp.sum(sums_ref[...], axis=0)
    square = sums[0:1, :]
    factor = lax.rsqrt(square / total_cols + 1e-06)
    error = factor * factor * sums[1:2, :] - 2.0 * factor * sums[2:3, :] + sums[3:4, :]
    weight = 1.0 / (0.1 + jnp.full((1, 1), steps_ref[0], jnp.int32).astype(jnp.float32) / 999.0)
    loss_ref[...] = jnp.broadcast_to(weight * jnp.sum(error, axis=1, keepdims=True), loss_ref.shape)
    column = jnp.transpose(jnp.broadcast_to(factor, (tokens, tokens)))[:, 0:1]
    out_ref[0] = (att_ref[...] * column * gain_ref[...].astype(jnp.float32)).astype(jnp.bfloat16)


def fold_kernel(count, got_ref, sum_ref):
    sum_ref[...] = (jnp.sum(got_ref[...], axis=0) / count)[0:1, 0:1]


def local(
    enc_query,
    enc_key,
    enc_value,
    keep_index,
    keep_count,
    text_key,
    text_value,
    dec_query,
    dec_key,
    mask_value,
    norm_gain,
    target,
    timesteps,
):
    images, seq, heads = (lax.axis_size(name) for name in ("dp", "seq", "head"))
    tokens, cols = enc_query.shape[1:]
    slots = keep_index.shape[1]
    local_heads = cols // HEAD_DIM
    chips = seq // 2
    packed = slots + tokens + slots // 2
    same_core = [[2 * chip + core for chip in range(chips)] for core in range(2)]
    bf16, f32 = jnp.bfloat16, jnp.float32
    gain = norm_gain.reshape(1, cols)

    send, text = pl.pallas_call(
        pack_kernel,
        out_shape=(
            jax.ShapeDtypeStruct((chips, packed, LANES), bf16),
            jax.ShapeDtypeStruct((local_heads, 2 * tokens + 16, LANES), bf16),
        ),
        in_specs=[pl.BlockSpec(memory_space=pltpu.SMEM)] + [pl.BlockSpec(memory_space=pltpu.HBM)] * 9,
        out_specs=tuple(vmem(2)),
        scratch_shapes=[pltpu.VMEM((1, slots), jnp.int32)]
        + [pltpu.VMEM((1, tokens, cols), bf16)] * 7
        + [pltpu.VMEM((cols,), bf16), pltpu.SemaphoreType.DMA((9,))],
        compiler_params=params(60),
        name="pack",
    )(
        keep_count,
        keep_index,
        enc_query,
        enc_key,
        enc_value,
        dec_query,
        dec_key,
        text_key,
        text_value,
        mask_value,
    )
    own = lax.all_to_all(send, "seq", 0, 0, axis_index_groups=same_core, tiled=True)
    pair = lax.ppermute(own, "seq", [(source, source ^ 1) for source in range(seq)])
    out = pl.pallas_call(
        functools.partial(attend_kernel, seq, slots, tokens),
        out_shape=jax.ShapeDtypeStruct((chips, tokens // 2, LANES), bf16),
        in_specs=vmem(3),
        out_specs=vmem(1)[0],
        scratch_shapes=[
            pltpu.VMEM((tokens + seq * slots, LANES), bf16),
            pltpu.VMEM((tokens + seq * slots, LANES), bf16),
            pltpu.VMEM((tokens + seq * tokens, LANES), bf16),
            pltpu.VMEM((tokens + seq * tokens, LANES), bf16),
            pltpu.VMEM((seq * slots, LANES), bf16),
            pltpu.VMEM((seq * tokens // 2, LANES), bf16),
            pltpu.VMEM((seq * slots, LANES), f32),
        ]
        + [pltpu.VMEM((2 * tokens, tokens + seq * tokens), f32), pltpu.VMEM((2 * tokens, LANES), f32)] * 2,
        compiler_params=params(),
        name="attend",
    )(own, pair, text)
    got = lax.all_to_all(out, "seq", 0, 0, axis_index_groups=same_core, tiled=True)
    att, sums = pl.pallas_call(
        sums_kernel,
        out_shape=(
            jax.ShapeDtypeStruct((tokens, cols), f32),
            jax.ShapeDtypeStruct((heads, 8, tokens), f32),
        ),
        in_specs=vmem(3),
        out_specs=tuple(vmem(2)),
        compiler_params=params(),
        name="sums",
    )(got, gain, target)
    sums = lax.all_to_all(sums, "head", 0, 0, tiled=True)
    decoded, loss = pl.pallas_call(
        finish_kernel,
        out_shape=(
            jax.ShapeDtypeStruct((1, tokens, cols), bf16),
            jax.ShapeDtypeStruct((images * seq, 8, LANES), f32),
        ),
        in_specs=[pl.BlockSpec(memory_space=pltpu.SMEM)] + vmem(3),
        out_specs=tuple(vmem(2)),
        compiler_params=params(),
        name="finish",
    )(timesteps, att, gain, sums)
    got = lax.all_to_all(loss, ("dp", "seq"), 0, 0, tiled=True)
    loss = pl.pallas_call(
        functools.partial(fold_kernel, float(images * tokens * seq * cols * heads)),
        out_shape=jax.ShapeDtypeStruct((1, 1), f32),
        in_specs=vmem(1),
        out_specs=vmem(1)[0],
        compiler_params=params(),
        name="fold",
    )(got)
    total_loss = loss.reshape(())
    return (decoded, total_loss)


def solution(mesh):
    placed = (
        P("dp", "seq", "head"),
        P("dp", "seq", "head"),
        P("dp", "seq", "head"),
        P("dp", "seq"),
        P("dp", "seq"),
        P("dp", None, "head"),
        P("dp", None, "head"),
        P("dp", "seq", "head"),
        P("dp", "seq", "head"),
        P("head"),
        P("head"),
        P("dp", "seq", "head"),
        P("dp"),
    )
    return jax.shard_map(
        local, mesh=mesh, in_specs=placed, out_specs=(P("dp", "seq", "head"), P()), check_vma=False
    )
```

```python
import functools

import jax
import jax.numpy as jnp
from jax import lax
from jax.experimental import pallas as pl
from jax.experimental.pallas import tpu as pltpu
from jax.sharding import PartitionSpec as P

HEAD_DIM = 64
LANES = 128
DEAD = 1024.0
DEAD_EDGE = 512.0
MIB = 1024 * 1024


def params(mib=40):
    return pltpu.CompilerParams(vmem_limit_bytes=mib * MIB)


def vmem(count):
    return [pl.BlockSpec(memory_space=pltpu.VMEM)] * count


def one_hot_dot(table, rows):
    return lax.dot_general(
        table, rows, (((1,), (0,)), ((), ())), preferred_element_type=jnp.float32
    )


def pack_kernel(
    count_ref, index_hbm, eq_hbm, ek_hbm, ev_hbm, dq_hbm, dk_hbm, tk_hbm, tv_hbm, mask_hbm, send_ref, text_ref, *scratch
):
    *held, sems = scratch
    given = (index_hbm, eq_hbm, ek_hbm, ev_hbm, dq_hbm, dk_hbm, tk_hbm, tv_hbm, mask_hbm)
    copies = [
        pltpu.make_async_copy(source, place, sems.at[number])
        for number, (source, place) in enumerate(zip(given, held))
    ]
    for copy in copies:
        copy.start()
    copies[0].wait()
    index_ref, eq_ref, ek_ref, ev_ref, dq_ref, dk_ref, tk_ref, tv_ref, mask_ref = held
    tokens, cols = eq_ref.shape[1:]
    slots = index_ref.shape[1]
    heads = cols // HEAD_DIM
    spare = tokens - slots
    total = count_ref[0, 0]
    index = jnp.broadcast_to(index_ref[...].astype(jnp.float32), (tokens, slots))
    index = jnp.transpose(index)
    token = lax.broadcasted_iota(jnp.int32, (slots, tokens), 1).astype(jnp.float32)
    slot = lax.broadcasted_iota(jnp.int32, (slots, tokens), 0)
    live = slot < total
    match_live = jnp.where(live & (token == index), 1.0, 0.0)
    match_fill = jnp.where(token == jnp.where(live, index, index[0:1, :]), 1.0, 0.0)
    kept = jnp.sum(match_live, axis=0, keepdims=True)
    kept_slot = jnp.sum(match_live * slot.astype(jnp.float32), axis=0, keepdims=True)
    row = lax.broadcasted_iota(jnp.int32, (tokens, tokens), 0)
    col = lax.broadcasted_iota(jnp.int32, (tokens, tokens), 1)
    before = jnp.where(row < col, 1.0, 0.0).astype(jnp.bfloat16)
    left = jnp.broadcast_to(1.0 - kept, (16, tokens)).astype(jnp.bfloat16)
    rank = one_hot_dot(left, before)[0:1, :]
    place = jnp.where(kept > 0.5, kept_slot, total.astype(jnp.float32) + rank)
    order = jnp.where(row.astype(jnp.float32) == place, 1.0, 0.0).astype(jnp.bfloat16)

    for copy in copies[1:]:
        copy.wait()
    scale = HEAD_DIM ** (-0.5)
    match_live = match_live.astype(jnp.bfloat16)
    match_fill = match_fill.astype(jnp.bfloat16)
    query = one_hot_dot(match_live, eq_ref[0]) * scale
    slot_wide = lax.broadcasted_iota(jnp.int32, (slots, cols), 0)
    query = jnp.where(slot_wide < total, query, DEAD)
    key = one_hot_dot(match_fill, ek_ref[0])
    value = one_hot_dot(match_live, ev_ref[0])
    dec_key = one_hot_dot(order, dk_ref[0])
    dec_query = dq_ref[0].astype(jnp.float32) * scale
    text_key = tk_ref[0].astype(jnp.float32)
    text_value = tv_ref[0].astype(jnp.float32)
    mask_row = jnp.broadcast_to(mask_ref[...].astype(jnp.float32).reshape(1, cols), (16, cols))

    def low(block, head):
        tile = block[:, (head // 2) * LANES : (head // 2 + 1) * LANES]
        return tile if head % 2 == 0 else pltpu.roll(tile, HEAD_DIM, 1)

    def high(block, head):
        tile = block[:, (head // 2) * LANES : (head // 2 + 1) * LANES]
        return tile if head % 2 == 1 else pltpu.roll(tile, HEAD_DIM, 1)

    def join(first, second):
        lane = lax.broadcasted_iota(jnp.int32, first.shape, 1)
        return jnp.where(lane < HEAD_DIM, first, second).astype(jnp.bfloat16)

    for head in range(heads):
        kept_tile = join(low(value, head), high(key, head))
        query_high = high(query, head)
        dec_low = low(dec_key, head)
        dq_low = low(dec_query, head)
        dq_high = high(dec_query, head)
        send_ref[head, 0:slots, :] = kept_tile
        send_ref[head, slots : 2 * slots, :] = join(dec_low[0:slots], query_high)
        send_ref[head, 2 * slots : slots + tokens, :] = join(dec_low[slots:tokens], dq_high[0:spare])
        rest = slots // 2
        send_ref[head, slots + tokens : slots + tokens + rest, :] = join(
            dq_low[spare : spare + rest], dq_high[spare + rest : tokens]
        )
        text_ref[head, 0:tokens, :] = join(low(text_value, head), high(text_key, head))
        text_ref[head, tokens : 2 * tokens, :] = join(low(text_key, head), high(text_value, head))
        text_ref[head, 2 * tokens : 2 * tokens + 16, :] = low(mask_row, head).astype(jnp.bfloat16)


def put_scores(query, key_ref, place, peak):
    keys = key_ref.shape[0]
    largest = None
    for first in range(0, keys, 2 * LANES):
        last = min(keys, first + 2 * LANES)
        part = lax.dot_general(
            query, key_ref[first:last, :], (((1,), (1,)), ((), ())), preferred_element_type=jnp.float32
        )
        place[:, first:last] = part
        for lane in range(0, last - first, LANES):
            tile = part[:, lane : lane + LANES]
            largest = tile if largest is None else jnp.maximum(largest, tile)
    peak[...] = largest


def weigh(place, peak, value_ref):
    keys = value_ref.shape[0]
    top = jnp.max(peak[...], axis=1, keepdims=True)
    weights = jnp.exp(place[:, 0:keys] - top).astype(jnp.bfloat16)
    sums = lax.dot_general(
        weights, value_ref[...], (((1,), (0,)), ((), ())), preferred_element_type=jnp.float32
    )
    return sums / pltpu.roll(sums, HEAD_DIM, 1)


def over_tiles(tiles, rows, query_ref, key_ref, value_ref, buffers, use, after):
    (one, one_peak), (two, two_peak) = buffers

    def put(tile, buffer):
        put_scores(query_ref[pl.ds(pl.multiple_of(tile * rows, rows), rows), :], key_ref, *buffer)

    def pair(step, carry):
        tile = 2 * step
        put(tile + 1, buffers[1])
        use(tile, weigh(one, one_peak, value_ref))
        put(tile + 2, buffers[0])
        use(tile + 1, weigh(two, two_peak, value_ref))
        return carry

    lax.fori_loop(0, tiles // 2 - 1, pair, 0)
    put(tiles - 1, buffers[1])
    use(tiles - 2, weigh(one, one_peak, value_ref))
    after()
    use(tiles - 1, weigh(two, two_peak, value_ref))


def attend_kernel(
    blocks, slots, tokens, own_ref, pair_ref, text_ref, out_ref, ek_ref, ev_ref, dk_ref, dv_ref, eq_ref, dq_ref, found_ref, *places
):
    spare = tokens - slots
    rest = slots // 2
    chips = blocks // 2
    head = jnp.minimum(lax.axis_index("seq") // 2, text_ref.shape[0] - 1)
    text = text_ref[head]
    text_first = text[0:tokens]
    text_second = text[tokens : 2 * tokens]
    mask_row = text[2 * tokens : 2 * tokens + 1].astype(jnp.float32)

    def lane_of(rows):
        return lax.broadcasted_iota(jnp.int32, (rows, LANES), 1)

    def with_ones(tile):
        return jnp.where(lane_of(tile.shape[0]) < HEAD_DIM, tile.astype(jnp.float32), 1.0).astype(jnp.bfloat16)

    ek_ref[0:tokens, :] = text_first
    ev_ref[0:tokens, :] = with_ones(text_first)
    dk_ref[0:tokens, :] = text_second
    dv_ref[0:tokens, :] = with_ones(text_first)
    for block in range(blocks):
        own = block < chips
        got = own_ref.at[block] if own else pair_ref.at[block - chips]
        kept = got[0:slots, :]
        mixed = got[slots : 2 * slots, :].astype(jnp.float32)
        tail = got[2 * slots : slots + tokens, :].astype(jnp.float32)
        base = tokens + block * slots
        low_slot = lane_of(slots) < HEAD_DIM
        live = mixed < DEAD_EDGE
        ek_ref[base : base + slots, :] = kept
        ev_ref[base : base + slots, :] = jnp.where(
            low_slot, kept.astype(jnp.float32), jnp.where(live, 1.0, 0.0)
        ).astype(jnp.bfloat16)
        eq_ref[block * slots : block * slots + slots, :] = jnp.where(low_slot, 0.0, mixed).astype(jnp.bfloat16)
        base = tokens + block * tokens
        dk_ref[base : base + slots, :] = mixed.astype(jnp.bfloat16)
        dk_ref[base + slots : base + tokens, :] = tail.astype(jnp.bfloat16)
        if own:
            last = got[slots + tokens : slots + tokens + rest, :].astype(jnp.float32)
            base = block * tokens
            dq_ref[base : base + spare, :] = jnp.where(
                lane_of(spare) < HEAD_DIM, pltpu.roll(tail, HEAD_DIM, 1), 0.0
            ).astype(jnp.bfloat16)
            low_rest = lane_of(rest) < HEAD_DIM
            dq_ref[base + spare : base + spare + rest, :] = jnp.where(low_rest, last, 0.0).astype(jnp.bfloat16)
            dq_ref[base + spare + rest : base + tokens, :] = jnp.where(
                low_rest, pltpu.roll(last, HEAD_DIM, 1), 0.0
            ).astype(jnp.bfloat16)

    buffers = (places[0:2], places[2:4])
    rows = 2 * tokens

    def keep(tile, found):
        found_ref[pl.ds(pl.multiple_of(tile * rows, rows), rows), :] = found

    put_scores(eq_ref[0:rows, :], ek_ref, *buffers[0])
    over_tiles(
        blocks * slots // rows,
        rows,
        eq_ref,
        ek_ref,
        ev_ref,
        buffers,
        keep,
        lambda: put_scores(dq_ref[0:rows, :], dk_ref, *buffers[0]),
    )
    fill = jnp.where(lane_of(spare) < HEAD_DIM, mask_row, 1.0).astype(jnp.bfloat16)
    for block in range(blocks):
        span = slice(block * slots, (block + 1) * slots)
        live = pltpu.roll(eq_ref[span, :].astype(jnp.float32), HEAD_DIM, 1) < DEAD_EDGE
        base = tokens + block * tokens
        dv_ref[base : base + slots, :] = jnp.where(
            lane_of(slots) < HEAD_DIM, jnp.where(live, found_ref[span, :], mask_row), 1.0
        ).astype(jnp.bfloat16)
        dv_ref[base + slots : base + tokens, :] = fill

    def give(tile, found):
        half = tokens // 2
        for inner in range(2):
            first = inner * tokens
            out_ref[2 * tile + inner] = jnp.where(
                lane_of(half) < HEAD_DIM,
                found[first : first + half],
                pltpu.roll(found[first + half : first + tokens], HEAD_DIM, 1),
            ).astype(jnp.bfloat16)

    over_tiles(chips * tokens // rows, rows, dq_ref, dk_ref, dv_ref, buffers, give, lambda: None)


def sums_kernel(got_ref, gain_ref, target_ref, weight_ref, att_ref, sums_ref):
    tokens, cols = att_ref.shape
    half = tokens // 2
    low = lax.broadcasted_iota(jnp.int32, (half, LANES), 1) < HEAD_DIM
    for tile in range(cols // LANES):
        even = got_ref[2 * tile].astype(jnp.float32)
        odd = got_ref[2 * tile + 1].astype(jnp.float32)
        span = slice(tile * LANES, (tile + 1) * LANES)
        att_ref[0:half, span] = jnp.where(low, even, pltpu.roll(odd, HEAD_DIM, 1))
        att_ref[half:tokens, span] = jnp.where(low, pltpu.roll(even, HEAD_DIM, 1), odd)
    att = att_ref[...]
    gained = att * gain_ref[...].astype(jnp.float32)
    target = target_ref[0].astype(jnp.float32)
    weight = 1.0 / (0.1 + jnp.full((1, 1), weight_ref[0], jnp.int32).astype(jnp.float32) / 999.0)
    lane = lax.broadcasted_iota(jnp.int32, (tokens, LANES), 1)

    def over(block):
        return jnp.sum(block, axis=1, keepdims=True)

    table = jnp.where(
        lane == 1,
        over(gained * gained),
        jnp.where(lane == 2, over(gained * target), over(target * target)),
    )
    table = jnp.where(lane == 0, over(att * att), table * weight)
    sums_ref[...] = jnp.broadcast_to(jnp.transpose(table)[None, 0:4, :], sums_ref.shape)


def finish_kernel(heads, att_ref, gain_ref, sums_ref, out_ref, loss_ref):
    tokens, cols = att_ref.shape
    images = sums_ref.shape[0] // heads
    total_cols = cols * heads
    total = None
    for image in range(images):
        sums = jnp.sum(sums_ref[image * heads : (image + 1) * heads], axis=0)
        factor = lax.rsqrt(sums[0:1, :] / total_cols + 1e-06)
        error = factor * factor * sums[1:2, :] - 2.0 * factor * sums[2:3, :] + sums[3:4, :]
        total = error if total is None else total + error
    loss_ref[...] = jnp.broadcast_to(jnp.sum(total, axis=1, keepdims=True)[None], loss_ref.shape)
    own = jnp.sum(sums_ref[pl.ds(lax.axis_index("dp") * heads, heads)], axis=0)
    factor = lax.rsqrt(own[0:1, :] / total_cols + 1e-06)
    column = jnp.transpose(jnp.broadcast_to(factor, (tokens, tokens)))[:, 0:1]
    out_ref[0] = (att_ref[...] * column * gain_ref[...].astype(jnp.float32)).astype(jnp.bfloat16)


def fold_kernel(count, got_ref, sum_ref):
    sum_ref[...] = (jnp.sum(got_ref[...], axis=0) / count)[0:1, 0:1]


def local(
    enc_query,
    enc_key,
    enc_value,
    keep_index,
    keep_count,
    text_key,
    text_value,
    dec_query,
    dec_key,
    mask_value,
    norm_gain,
    target,
    timesteps,
):
    images, seq, heads = (lax.axis_size(name) for name in ("dp", "seq", "head"))
    tokens, cols = enc_query.shape[1:]
    slots = keep_index.shape[1]
    local_heads = cols // HEAD_DIM
    chips = seq // 2
    packed = slots + tokens + slots // 2
    same_core = [[2 * chip + core for chip in range(chips)] for core in range(2)]
    bf16, f32 = jnp.bfloat16, jnp.float32
    gain = norm_gain.reshape(1, cols)

    send, text = pl.pallas_call(
        pack_kernel,
        out_shape=(
            jax.ShapeDtypeStruct((chips, packed, LANES), bf16),
            jax.ShapeDtypeStruct((local_heads, 2 * tokens + 16, LANES), bf16),
        ),
        in_specs=[pl.BlockSpec(memory_space=pltpu.SMEM)] + [pl.BlockSpec(memory_space=pltpu.HBM)] * 9,
        out_specs=tuple(vmem(2)),
        scratch_shapes=[pltpu.VMEM((1, slots), jnp.int32)]
        + [pltpu.VMEM((1, tokens, cols), bf16)] * 7
        + [pltpu.VMEM((cols,), bf16), pltpu.SemaphoreType.DMA((9,))],
        compiler_params=params(60),
        name="pack",
    )(
        keep_count,
        keep_index,
        enc_query,
        enc_key,
        enc_value,
        dec_query,
        dec_key,
        text_key,
        text_value,
        mask_value,
    )
    own = lax.all_to_all(send, "seq", 0, 0, axis_index_groups=same_core, tiled=True)
    pair = lax.ppermute(own, "seq", [(source, source ^ 1) for source in range(seq)])
    out = pl.pallas_call(
        functools.partial(attend_kernel, seq, slots, tokens),
        out_shape=jax.ShapeDtypeStruct((chips, tokens // 2, LANES), bf16),
        in_specs=vmem(3),
        out_specs=vmem(1)[0],
        scratch_shapes=[
            pltpu.VMEM((tokens + seq * slots, LANES), bf16),
            pltpu.VMEM((tokens + seq * slots, LANES), bf16),
            pltpu.VMEM((tokens + seq * tokens, LANES), bf16),
            pltpu.VMEM((tokens + seq * tokens, LANES), bf16),
            pltpu.VMEM((seq * slots, LANES), bf16),
            pltpu.VMEM((seq * tokens // 2, LANES), bf16),
            pltpu.VMEM((seq * slots, LANES), f32),
        ]
        + [pltpu.VMEM((2 * tokens, tokens + seq * tokens), f32), pltpu.VMEM((2 * tokens, LANES), f32)] * 2,
        compiler_params=params(),
        name="attend",
    )(own, pair, text)
    got = lax.all_to_all(out, "seq", 0, 0, axis_index_groups=same_core, tiled=True)
    att, sums = pl.pallas_call(
        sums_kernel,
        out_shape=(
            jax.ShapeDtypeStruct((tokens, cols), f32),
            jax.ShapeDtypeStruct((images * heads, 4, tokens), f32),
        ),
        in_specs=vmem(3) + [pl.BlockSpec(memory_space=pltpu.SMEM)],
        out_specs=tuple(vmem(2)),
        compiler_params=params(),
        name="sums",
    )(got, gain, target, timesteps)
    sums = lax.all_to_all(sums, ("dp", "head"), 0, 0, tiled=True)
    decoded, loss = pl.pallas_call(
        functools.partial(finish_kernel, heads),
        out_shape=(
            jax.ShapeDtypeStruct((1, tokens, cols), bf16),
            jax.ShapeDtypeStruct((seq, 1, LANES), f32),
        ),
        in_specs=vmem(3),
        out_specs=tuple(vmem(2)),
        compiler_params=params(),
        name="finish",
    )(att, gain, sums)
    got = lax.all_to_all(loss, "seq", 0, 0, tiled=True)
    loss = pl.pallas_call(
        functools.partial(fold_kernel, float(images * tokens * seq * cols * heads)),
        out_shape=jax.ShapeDtypeStruct((1, 1), f32),
        in_specs=vmem(1),
        out_specs=vmem(1)[0],
        compiler_params=params(),
        name="fold",
    )(got)
    total_loss = loss.reshape(())
    return (decoded, total_loss)


def solution(mesh):
    placed = (
        P("dp", "seq", "head"),
        P("dp", "seq", "head"),
        P("dp", "seq", "head"),
        P("dp", "seq"),
        P("dp", "seq"),
        P("dp", None, "head"),
        P("dp", None, "head"),
        P("dp", "seq", "head"),
        P("dp", "seq", "head"),
        P("head"),
        P("head"),
        P("dp", "seq", "head"),
        P("dp"),
    )
    return jax.shard_map(
        local, mesh=mesh, in_specs=placed, out_specs=(P("dp", "seq", "head"), P()), check_vma=False
    )
```

```python
import functools

import jax
import jax.numpy as jnp
from jax import lax
from jax.experimental import pallas as pl
from jax.experimental.pallas import tpu as pltpu
from jax.sharding import PartitionSpec as P

HEAD_DIM = 64
LANES = 128
DEAD = 1024.0
DEAD_EDGE = 512.0
MIB = 1024 * 1024


def params(mib=40):
    return pltpu.CompilerParams(vmem_limit_bytes=mib * MIB)


def vmem(count):
    return [pl.BlockSpec(memory_space=pltpu.VMEM)] * count


def one_hot_dot(table, rows):
    return lax.dot_general(
        table, rows, (((1,), (0,)), ((), ())), preferred_element_type=jnp.float32
    )


def pack_kernel(
    count_ref, index_hbm, eq_hbm, ek_hbm, ev_hbm, dq_hbm, dk_hbm, send_ref, *scratch
):
    *held, sems = scratch
    given = (index_hbm, eq_hbm, ek_hbm, ev_hbm, dq_hbm, dk_hbm)
    copies = [
        pltpu.make_async_copy(source, place, sems.at[number])
        for number, (source, place) in enumerate(zip(given, held))
    ]
    for copy in copies:
        copy.start()
    copies[0].wait()
    index_ref, eq_ref, ek_ref, ev_ref, dq_ref, dk_ref = held
    tokens, cols = eq_ref.shape[1:]
    slots = index_ref.shape[1]
    heads = cols // HEAD_DIM
    spare = tokens - slots
    total = count_ref[0, 0]
    index = jnp.broadcast_to(index_ref[...].astype(jnp.float32), (tokens, slots))
    index = jnp.transpose(index)
    token = lax.broadcasted_iota(jnp.int32, (slots, tokens), 1).astype(jnp.float32)
    slot = lax.broadcasted_iota(jnp.int32, (slots, tokens), 0)
    live = slot < total
    match_live = jnp.where(live & (token == index), 1.0, 0.0)
    match_fill = jnp.where(token == jnp.where(live, index, index[0:1, :]), 1.0, 0.0)
    kept = jnp.sum(match_live, axis=0, keepdims=True)
    kept_slot = jnp.sum(match_live * slot.astype(jnp.float32), axis=0, keepdims=True)
    row = lax.broadcasted_iota(jnp.int32, (tokens, tokens), 0)
    col = lax.broadcasted_iota(jnp.int32, (tokens, tokens), 1)
    before = jnp.where(row < col, 1.0, 0.0).astype(jnp.bfloat16)
    left = jnp.broadcast_to(1.0 - kept, (16, tokens)).astype(jnp.bfloat16)
    rank = one_hot_dot(left, before)[0:1, :]
    place = jnp.where(kept > 0.5, kept_slot, total.astype(jnp.float32) + rank)
    order = jnp.where(row.astype(jnp.float32) == place, 1.0, 0.0).astype(jnp.bfloat16)

    for copy in copies[1:]:
        copy.wait()
    scale = HEAD_DIM ** (-0.5)
    match_live = match_live.astype(jnp.bfloat16)
    match_fill = match_fill.astype(jnp.bfloat16)
    query = one_hot_dot(match_live, eq_ref[0]) * scale
    slot_wide = lax.broadcasted_iota(jnp.int32, (slots, cols), 0)
    query = jnp.where(slot_wide < total, query, DEAD)
    key = one_hot_dot(match_fill, ek_ref[0])
    value = one_hot_dot(match_live, ev_ref[0])
    dec_key = one_hot_dot(order, dk_ref[0])
    dec_query = dq_ref[0].astype(jnp.float32) * scale

    def low(block, head):
        tile = block[:, (head // 2) * LANES : (head // 2 + 1) * LANES]
        return tile if head % 2 == 0 else pltpu.roll(tile, HEAD_DIM, 1)

    def high(block, head):
        tile = block[:, (head // 2) * LANES : (head // 2 + 1) * LANES]
        return tile if head % 2 == 1 else pltpu.roll(tile, HEAD_DIM, 1)

    def join(first, second):
        lane = lax.broadcasted_iota(jnp.int32, first.shape, 1)
        return jnp.where(lane < HEAD_DIM, first, second).astype(jnp.bfloat16)

    for head in range(heads):
        kept_tile = join(low(value, head), high(key, head))
        query_high = high(query, head)
        dec_low = low(dec_key, head)
        dq_low = low(dec_query, head)
        dq_high = high(dec_query, head)
        send_ref[head, 0:slots, :] = kept_tile
        send_ref[head, slots : 2 * slots, :] = join(dec_low[0:slots], query_high)
        send_ref[head, 2 * slots : slots + tokens, :] = join(dec_low[slots:tokens], dq_high[0:spare])
        rest = slots // 2
        send_ref[head, slots + tokens : slots + tokens + rest, :] = join(
            dq_low[spare : spare + rest], dq_high[spare + rest : tokens]
        )


def put_scores(query, key_refs, place, peak):
    rows = query.shape[0]
    largest = None
    column = 0
    for key_ref in key_refs:
        keys = key_ref.shape[0]
        for first in range(0, keys, 2 * LANES):
            last = min(keys, first + 2 * LANES)
            part = lax.dot_general(
                query, key_ref[first:last, :], (((1,), (1,)), ((), ())), preferred_element_type=jnp.float32
            )
            place[0:rows, column : column + last - first] = part
            column += last - first
            for lane in range(0, last - first, LANES):
                tile = part[:, lane : lane + LANES]
                largest = tile if largest is None else jnp.maximum(largest, tile)
    peak[0:rows, :] = largest


def weigh(rows, place, peak, value_refs, earlier):
    top = jnp.max(peak[0:rows, :], axis=1, keepdims=True)
    sums = None
    if earlier is not None:
        earlier_sums, earlier_top = earlier
        top = jnp.maximum(top, earlier_top[:, 0:1])
        sums = earlier_sums * jnp.exp(earlier_top - top)
    column = 0
    for value_ref in value_refs:
        keys = value_ref.shape[0]
        weights = jnp.exp(place[0:rows, column : column + keys] - top).astype(jnp.bfloat16)
        column += keys
        part = lax.dot_general(
            weights, value_ref[...], (((1,), (0,)), ((), ())), preferred_element_type=jnp.float32
        )
        sums = part if sums is None else sums + part
    return top, sums


def run_jobs(jobs, buffers):
    def put(number):
        query, key_refs, _, _, _ = jobs[number]
        put_scores(query(), key_refs, *buffers[number % 2])

    put(0)
    for number, (query, _, value_refs, earlier, use) in enumerate(jobs):
        if number + 1 < len(jobs):
            put(number + 1)
        place, peak = buffers[number % 2]
        rows = query().shape[0]
        use(*weigh(rows, place, peak, value_refs, None if earlier is None else earlier()))


def lane_of(rows):
    return lax.broadcasted_iota(jnp.int32, (rows, LANES), 1)


def unpack(slots, tokens, got, block, first_key, first_dec, ek_ref, ev_ref, eq_ref, dk_ref):
    kept = got[0:slots, :]
    mixed = got[slots : 2 * slots, :].astype(jnp.float32)
    low = lane_of(slots) < HEAD_DIM
    base = first_key + block * slots
    ek_ref[base : base + slots, :] = kept
    ev_ref[base : base + slots, :] = jnp.where(
        low, kept.astype(jnp.float32), jnp.where(mixed < DEAD_EDGE, 1.0, 0.0)
    ).astype(jnp.bfloat16)
    eq_ref[block * slots : block * slots + slots, :] = jnp.where(low, 0.0, mixed).astype(jnp.bfloat16)
    base = first_dec + block * tokens
    dk_ref[base : base + tokens, :] = got[slots : slots + tokens, :]


def begin_kernel(
    slots,
    tokens,
    own_ref,
    text_key_ref,
    text_value_ref,
    mask_ref,
    ek_ref,
    ev_ref,
    eq_ref,
    dk_ref,
    dq_ref,
    sums_ref,
    top_ref,
    fill_ref,
    *places
):
    chips = own_ref.shape[0]
    cols = text_key_ref.shape[2]
    spare = tokens - slots
    rest = slots // 2
    head = jnp.minimum(lax.axis_index("seq") // 2, cols // HEAD_DIM - 1)
    odd = lax.rem(head, 2) == 1
    lanes = pl.ds(pl.multiple_of((head // 2) * LANES, LANES), LANES)

    def low_high(rows):
        turned = pltpu.roll(rows, HEAD_DIM, 1)
        return jnp.where(odd, turned, rows), jnp.where(odd, rows, turned)

    key_low, key_high = low_high(text_key_ref[0, :, lanes].astype(jnp.float32))
    value_low, _ = low_high(text_value_ref[0, :, lanes].astype(jnp.float32))
    mask_row = jnp.zeros((1, LANES), jnp.float32)
    whole = mask_ref[...].astype(jnp.float32).reshape(1, cols)
    for tile in range(cols // LANES):
        mask_row = jnp.where(head // 2 == tile, whole[:, tile * LANES : (tile + 1) * LANES], mask_row)
    mask_row, _ = low_high(jnp.broadcast_to(mask_row, (8, LANES)))
    low = lane_of(tokens) < HEAD_DIM
    fill_ref[...] = jnp.where(lane_of(8) < HEAD_DIM, mask_row, 1.0)
    ek_ref[0:tokens, :] = jnp.where(low, value_low, key_high).astype(jnp.bfloat16)
    ev_ref[0:tokens, :] = jnp.where(low, value_low, 1.0).astype(jnp.bfloat16)
    dk_ref[0:tokens, :] = key_low.astype(jnp.bfloat16)
    for block in range(chips):
        got = own_ref.at[block]
        unpack(slots, tokens, got, block, tokens, tokens, ek_ref, ev_ref, eq_ref, dk_ref)
        tail = got[2 * slots : slots + tokens, :].astype(jnp.float32)
        last = got[slots + tokens : slots + tokens + rest, :].astype(jnp.float32)
        base = block * tokens
        dq_ref[base : base + spare, :] = jnp.where(
            lane_of(spare) < HEAD_DIM, pltpu.roll(tail, HEAD_DIM, 1), 0.0
        ).astype(jnp.bfloat16)
        low_rest = lane_of(rest) < HEAD_DIM
        dq_ref[base + spare : base + spare + rest, :] = jnp.where(low_rest, last, 0.0).astype(jnp.bfloat16)
        dq_ref[base + spare + rest : base + tokens, :] = jnp.where(
            low_rest, pltpu.roll(last, HEAD_DIM, 1), 0.0
        ).astype(jnp.bfloat16)

    rows = chips // 2 * slots

    def job(tile):
        span = slice(tile * rows, (tile + 1) * rows)

        def use(top, sums):
            sums_ref[span, :] = sums
            top_ref[span, :] = jnp.broadcast_to(top, (rows, LANES))

        return (lambda: eq_ref[span, :], [ek_ref], [ev_ref], None, use)

    run_jobs([job(tile) for tile in range(2)], (places[0:2], places[2:4]))


def attend_kernel(
    slots,
    tokens,
    pair_ref,
    ek_ref,
    ev_ref,
    eq_ref,
    dk_ref,
    dq_ref,
    sums_ref,
    top_ref,
    fill_ref,
    out_ref,
    pair_ek_ref,
    pair_ev_ref,
    pair_eq_ref,
    pair_dk_ref,
    dv_ref,
    *places
):
    chips = pair_ref.shape[0]
    spare = tokens - slots
    for block in range(chips):
        unpack(
            slots, tokens, pair_ref.at[block], block, 0, 0, pair_ek_ref, pair_ev_ref, pair_eq_ref, pair_dk_ref
        )
    dv_ref[0:tokens, :] = ev_ref[0:tokens, :]
    mask_row = fill_ref[0:1, :]
    fill = jnp.broadcast_to(mask_row, (spare, LANES)).astype(jnp.bfloat16)
    group = chips // 2
    rows = group * slots

    def encode(tile, query_ref, first_block, key_refs, value_refs, earlier):
        span = slice(tile * rows, (tile + 1) * rows)

        def use(top, sums):
            found = sums / pltpu.roll(sums, HEAD_DIM, 1)
            for inner in range(group):
                mixed = query_ref[tile * rows + inner * slots : tile * rows + (inner + 1) * slots, :]
                live = pltpu.roll(mixed.astype(jnp.float32), HEAD_DIM, 1) < DEAD_EDGE
                base = tokens + (first_block + tile * group + inner) * tokens
                dv_ref[base : base + slots, :] = jnp.where(
                    (lane_of(slots) < HEAD_DIM) & live, found[inner * slots : (inner + 1) * slots, :], mask_row
                ).astype(jnp.bfloat16)
                dv_ref[base + slots : base + tokens, :] = fill

        before = (lambda: (sums_ref[span, :], top_ref[span, :])) if earlier else None
        return (lambda: query_ref[span, :], key_refs, value_refs, before, use)

    dec_group = 2
    dec_rows = dec_group * tokens
    half = tokens // 2

    def decode(tile):
        def use(top, sums):
            found = sums / pltpu.roll(sums, HEAD_DIM, 1)
            for inner in range(dec_group):
                first = inner * tokens
                out_ref[tile * dec_group + inner] = jnp.where(
                    lane_of(half) < HEAD_DIM,
                    found[first : first + half],
                    pltpu.roll(found[first + half : first + tokens], HEAD_DIM, 1),
                ).astype(jnp.bfloat16)

        span = slice(tile * dec_rows, (tile + 1) * dec_rows)
        return (lambda: dq_ref[span, :], [dk_ref, pair_dk_ref], [dv_ref], None, use)

    jobs = [encode(tile, eq_ref, 0, [pair_ek_ref], [pair_ev_ref], True) for tile in range(2)]
    jobs += [
        encode(tile, pair_eq_ref, chips, [ek_ref, pair_ek_ref], [ev_ref, pair_ev_ref], False) for tile in range(2)
    ]
    jobs += [decode(tile) for tile in range(chips // dec_group)]
    run_jobs(jobs, (places[0:2], places[2:4]))


def sums_kernel(got_ref, gain_ref, target_ref, weight_ref, att_ref, sums_ref):
    tokens, cols = att_ref.shape
    half = tokens // 2
    low = lax.broadcasted_iota(jnp.int32, (half, LANES), 1) < HEAD_DIM
    for tile in range(cols // LANES):
        even = got_ref[2 * tile].astype(jnp.float32)
        odd = got_ref[2 * tile + 1].astype(jnp.float32)
        span = slice(tile * LANES, (tile + 1) * LANES)
        att_ref[0:half, span] = jnp.where(low, even, pltpu.roll(odd, HEAD_DIM, 1))
        att_ref[half:tokens, span] = jnp.where(low, pltpu.roll(even, HEAD_DIM, 1), odd)
    att = att_ref[...]
    gained = att * gain_ref[...].astype(jnp.float32)
    target = target_ref[0].astype(jnp.float32)
    weight = 1.0 / (0.1 + jnp.full((1, 1), weight_ref[0], jnp.int32).astype(jnp.float32) / 999.0)
    lane = lax.broadcasted_iota(jnp.int32, (tokens, LANES), 1)

    def over(block):
        return jnp.sum(block, axis=1, keepdims=True)

    table = jnp.where(
        lane == 1,
        over(gained * gained),
        jnp.where(lane == 2, over(gained * target), over(target * target)),
    )
    table = jnp.where(lane == 0, over(att * att), table * weight)
    sums_ref[...] = jnp.broadcast_to(jnp.transpose(table)[None, 0:4, :], sums_ref.shape)


def finish_kernel(heads, att_ref, gain_ref, sums_ref, out_ref, loss_ref):
    tokens, cols = att_ref.shape
    images = sums_ref.shape[0] // heads
    total_cols = cols * heads
    total = None
    for image in range(images):
        sums = jnp.sum(sums_ref[image * heads : (image + 1) * heads], axis=0)
        factor = lax.rsqrt(sums[0:1, :] / total_cols + 1e-06)
        error = factor * factor * sums[1:2, :] - 2.0 * factor * sums[2:3, :] + sums[3:4, :]
        total = error if total is None else total + error
    loss_ref[...] = jnp.broadcast_to(jnp.sum(total, axis=1, keepdims=True)[None], loss_ref.shape)
    own = jnp.sum(sums_ref[pl.ds(lax.axis_index("dp") * heads, heads)], axis=0)
    factor = lax.rsqrt(own[0:1, :] / total_cols + 1e-06)
    column = jnp.transpose(jnp.broadcast_to(factor, (tokens, tokens)))[:, 0:1]
    out_ref[0] = (att_ref[...] * column * gain_ref[...].astype(jnp.float32)).astype(jnp.bfloat16)


def fold_kernel(count, got_ref, sum_ref):
    sum_ref[...] = (jnp.sum(got_ref[...], axis=0) / count)[0:1, 0:1]


def local(
    enc_query,
    enc_key,
    enc_value,
    keep_index,
    keep_count,
    text_key,
    text_value,
    dec_query,
    dec_key,
    mask_value,
    norm_gain,
    target,
    timesteps,
):
    images, seq, heads = (lax.axis_size(name) for name in ("dp", "seq", "head"))
    tokens, cols = enc_query.shape[1:]
    slots = keep_index.shape[1]
    local_heads = cols // HEAD_DIM
    chips = seq // 2
    packed = slots + tokens + slots // 2
    same_core = [[2 * chip + core for chip in range(chips)] for core in range(2)]
    bf16, f32 = jnp.bfloat16, jnp.float32
    gain = norm_gain.reshape(1, cols)

    send = pl.pallas_call(
        pack_kernel,
        out_shape=jax.ShapeDtypeStruct((chips, packed, LANES), bf16),
        in_specs=[pl.BlockSpec(memory_space=pltpu.SMEM)] + [pl.BlockSpec(memory_space=pltpu.HBM)] * 6,
        out_specs=vmem(1)[0],
        scratch_shapes=[pltpu.VMEM((1, slots), jnp.int32)]
        + [pltpu.VMEM((1, tokens, cols), bf16)] * 5
        + [pltpu.SemaphoreType.DMA((6,))],
        compiler_params=params(60),
        name="pack",
    )(keep_count, keep_index, enc_query, enc_key, enc_value, dec_query, dec_key)
    own = lax.all_to_all(send, "seq", 0, 0, axis_index_groups=same_core, tiled=True)
    pair = lax.ppermute(own, "seq", [(source, source ^ 1) for source in range(seq)])
    kept_own = chips * slots
    dec_own = chips * tokens
    begun = pl.pallas_call(
        functools.partial(begin_kernel, slots, tokens),
        out_shape=(
            jax.ShapeDtypeStruct((tokens + kept_own, LANES), bf16),
            jax.ShapeDtypeStruct((tokens + kept_own, LANES), bf16),
            jax.ShapeDtypeStruct((kept_own, LANES), bf16),
            jax.ShapeDtypeStruct((tokens + dec_own, LANES), bf16),
            jax.ShapeDtypeStruct((dec_own, LANES), bf16),
            jax.ShapeDtypeStruct((kept_own, LANES), f32),
            jax.ShapeDtypeStruct((kept_own, LANES), f32),
            jax.ShapeDtypeStruct((8, LANES), f32),
        ),
        in_specs=vmem(4),
        out_specs=tuple(vmem(8)),
        scratch_shapes=[
            pltpu.VMEM((kept_own // 2, tokens + kept_own), f32),
            pltpu.VMEM((kept_own // 2, LANES), f32),
        ]
        * 2,
        compiler_params=params(),
        cost_estimate=pl.CostEstimate(
            flops=4 * kept_own * (tokens + kept_own) * LANES,
            bytes_accessed=8 * MIB,
            transcendentals=kept_own * (tokens + kept_own),
        ),
        name="begin",
    )(own, text_key, text_value, mask_value)
    out = pl.pallas_call(
        functools.partial(attend_kernel, slots, tokens),
        out_shape=jax.ShapeDtypeStruct((chips, tokens // 2, LANES), bf16),
        in_specs=vmem(9),
        out_specs=vmem(1)[0],
        scratch_shapes=[
            pltpu.VMEM((kept_own, LANES), bf16),
            pltpu.VMEM((kept_own, LANES), bf16),
            pltpu.VMEM((kept_own, LANES), bf16),
            pltpu.VMEM((dec_own, LANES), bf16),
            pltpu.VMEM((tokens + 2 * dec_own, LANES), bf16),
        ]
        + [
            pltpu.VMEM((kept_own // 2, tokens + 2 * dec_own), f32),
            pltpu.VMEM((kept_own // 2, LANES), f32),
        ]
        * 2,
        compiler_params=params(),
        name="attend",
    )(pair, *begun)
    got = lax.all_to_all(out, "seq", 0, 0, axis_index_groups=same_core, tiled=True)
    att, sums = pl.pallas_call(
        sums_kernel,
        out_shape=(
            jax.ShapeDtypeStruct((tokens, cols), f32),
            jax.ShapeDtypeStruct((images * heads, 4, tokens), f32),
        ),
        in_specs=vmem(3) + [pl.BlockSpec(memory_space=pltpu.SMEM)],
        out_specs=tuple(vmem(2)),
        compiler_params=params(),
        name="sums",
    )(got, gain, target, timesteps)
    sums = lax.all_to_all(sums, ("dp", "head"), 0, 0, tiled=True)
    decoded, loss = pl.pallas_call(
        functools.partial(finish_kernel, heads),
        out_shape=(
            jax.ShapeDtypeStruct((1, tokens, cols), bf16),
            jax.ShapeDtypeStruct((seq, 1, LANES), f32),
        ),
        in_specs=vmem(3),
        out_specs=tuple(vmem(2)),
        compiler_params=params(),
        name="finish",
    )(att, gain, sums)
    got = lax.all_to_all(loss, "seq", 0, 0, tiled=True)
    loss = pl.pallas_call(
        functools.partial(fold_kernel, float(images * tokens * seq * cols * heads)),
        out_shape=jax.ShapeDtypeStruct((1, 1), f32),
        in_specs=vmem(1),
        out_specs=vmem(1)[0],
        compiler_params=params(),
        name="fold",
    )(got)
    total_loss = loss.reshape(())
    return (decoded, total_loss)


def solution(mesh):
    placed = (
        P("dp", "seq", "head"),
        P("dp", "seq", "head"),
        P("dp", "seq", "head"),
        P("dp", "seq"),
        P("dp", "seq"),
        P("dp", None, "head"),
        P("dp", None, "head"),
        P("dp", "seq", "head"),
        P("dp", "seq", "head"),
        P("head"),
        P("head"),
        P("dp", "seq", "head"),
        P("dp"),
    )
    return jax.shard_map(
        local, mesh=mesh, in_specs=placed, out_specs=(P("dp", "seq", "head"), P()), check_vma=False
    )
```

```python
import functools

import jax
import jax.numpy as jnp
from jax import lax
from jax.experimental import pallas as pl
from jax.experimental.pallas import tpu as pltpu
from jax.sharding import PartitionSpec as P

HEAD_DIM = 64
LANES = 128
DEAD = 1024.0
DEAD_EDGE = 512.0
MIB = 1024 * 1024


def params(mib=40):
    return pltpu.CompilerParams(vmem_limit_bytes=mib * MIB)


def vmem(count):
    return [pl.BlockSpec(memory_space=pltpu.VMEM)] * count


def one_hot_dot(table, rows):
    return lax.dot_general(
        table, rows, (((1,), (0,)), ((), ())), preferred_element_type=jnp.float32
    )


def pack_kernel(
    count_ref, index_hbm, eq_hbm, ek_hbm, ev_hbm, dq_hbm, dk_hbm, send_ref, *scratch
):
    *held, packed_ref, sems, out_sems = scratch
    given = (index_hbm, eq_hbm, ek_hbm, ev_hbm, dq_hbm, dk_hbm)
    copies = [
        pltpu.make_async_copy(source, place, sems.at[number])
        for number, (source, place) in enumerate(zip(given, held))
    ]
    for copy in copies:
        copy.start()
    copies[0].wait()
    index_ref, eq_ref, ek_ref, ev_ref, dq_ref, dk_ref = held
    tokens, cols = eq_ref.shape[1:]
    slots = index_ref.shape[1]
    heads = cols // HEAD_DIM
    spare = tokens - slots
    total = count_ref[0, 0]
    index = jnp.broadcast_to(index_ref[...].astype(jnp.float32), (tokens, slots))
    index = jnp.transpose(index)
    token = lax.broadcasted_iota(jnp.int32, (slots, tokens), 1).astype(jnp.float32)
    slot = lax.broadcasted_iota(jnp.int32, (slots, tokens), 0)
    live = slot < total
    match_live = jnp.where(live & (token == index), 1.0, 0.0)
    match_fill = jnp.where(token == jnp.where(live, index, index[0:1, :]), 1.0, 0.0)
    kept = jnp.sum(match_live, axis=0, keepdims=True)
    kept_slot = jnp.sum(match_live * slot.astype(jnp.float32), axis=0, keepdims=True)
    row = lax.broadcasted_iota(jnp.int32, (tokens, tokens), 0)
    col = lax.broadcasted_iota(jnp.int32, (tokens, tokens), 1)
    before = jnp.where(row < col, 1.0, 0.0).astype(jnp.bfloat16)
    left = jnp.broadcast_to(1.0 - kept, (16, tokens)).astype(jnp.bfloat16)
    rank = one_hot_dot(left, before)[0:1, :]
    place = jnp.where(kept > 0.5, kept_slot, total.astype(jnp.float32) + rank)
    order = jnp.where(row.astype(jnp.float32) == place, 1.0, 0.0).astype(jnp.bfloat16)

    for copy in copies[1:]:
        copy.wait()
    scale = HEAD_DIM ** (-0.5)
    match_live = match_live.astype(jnp.bfloat16)
    match_fill = match_fill.astype(jnp.bfloat16)
    query = one_hot_dot(match_live, eq_ref[0]) * scale
    slot_wide = lax.broadcasted_iota(jnp.int32, (slots, cols), 0)
    query = jnp.where(slot_wide < total, query, DEAD)
    key = one_hot_dot(match_fill, ek_ref[0])
    value = one_hot_dot(match_live, ev_ref[0])
    dec_key = one_hot_dot(order, dk_ref[0])
    dec_query = dq_ref[0].astype(jnp.float32) * scale

    def low(block, head):
        tile = block[:, (head // 2) * LANES : (head // 2 + 1) * LANES]
        return tile if head % 2 == 0 else pltpu.roll(tile, HEAD_DIM, 1)

    def high(block, head):
        tile = block[:, (head // 2) * LANES : (head // 2 + 1) * LANES]
        return tile if head % 2 == 1 else pltpu.roll(tile, HEAD_DIM, 1)

    def join(first, second):
        lane = lax.broadcasted_iota(jnp.int32, first.shape, 1)
        return jnp.where(lane < HEAD_DIM, first, second).astype(jnp.bfloat16)

    given_out = []
    for head in range(heads):
        dq_high = high(dec_query, head)
        dec_low = low(dec_key, head)
        packed_ref[head, 0:slots, :] = join(low(value, head), high(key, head))
        packed_ref[head, slots : 2 * slots, :] = join(dec_low[0:slots], high(query, head))
        packed_ref[head, 2 * slots : slots + tokens, :] = join(dec_low[slots:tokens], dq_high[0:spare])
        rest = slots // 2
        packed_ref[head, slots + tokens : slots + tokens + rest, :] = join(
            low(dec_query, head)[spare : spare + rest], dq_high[spare + rest : tokens]
        )
        copy = pltpu.make_async_copy(packed_ref.at[head], send_ref.at[head], out_sems.at[head])
        copy.start()
        given_out.append(copy)
    for copy in given_out:
        copy.wait()


def put_scores(query, key_refs, place, peak):
    rows = query.shape[0]
    largest = None
    column = 0
    for key_ref in key_refs:
        keys = key_ref.shape[0]
        for first in range(0, keys, 2 * LANES):
            last = min(keys, first + 2 * LANES)
            part = lax.dot_general(
                query, key_ref[first:last, :], (((1,), (1,)), ((), ())), preferred_element_type=jnp.float32
            )
            place[0:rows, column : column + last - first] = part
            column += last - first
            for lane in range(0, last - first, LANES):
                tile = part[:, lane : lane + LANES]
                largest = tile if largest is None else jnp.maximum(largest, tile)
    peak[0:rows, :] = largest


def weigh(rows, place, peak, value_refs, earlier):
    top = jnp.max(peak[0:rows, :], axis=1, keepdims=True)
    sums = None
    if earlier is not None:
        earlier_sums, earlier_top = earlier
        top = jnp.maximum(top, earlier_top[:, 0:1])
        sums = earlier_sums * jnp.exp(earlier_top - top)
    column = 0
    for value_ref in value_refs:
        keys = value_ref.shape[0]
        weights = jnp.exp(place[0:rows, column : column + keys] - top).astype(jnp.bfloat16)
        column += keys
        part = lax.dot_general(
            weights, value_ref[...], (((1,), (0,)), ((), ())), preferred_element_type=jnp.float32
        )
        sums = part if sums is None else sums + part
    return top, sums


def run_jobs(jobs, buffers):
    def put(number):
        query, key_refs, _, _, _ = jobs[number]
        put_scores(query(), key_refs, *buffers[number % 2])

    put(0)
    for number, (query, _, value_refs, earlier, use) in enumerate(jobs):
        if number + 1 < len(jobs):
            put(number + 1)
        place, peak = buffers[number % 2]
        rows = query().shape[0]
        use(*weigh(rows, place, peak, value_refs, None if earlier is None else earlier()))


def lane_of(rows):
    return lax.broadcasted_iota(jnp.int32, (rows, LANES), 1)


def unpack(slots, tokens, got, block, first_key, first_dec, ek_ref, ev_ref, eq_ref, dk_ref):
    kept = got[0:slots, :]
    mixed = got[slots : 2 * slots, :].astype(jnp.float32)
    low = lane_of(slots) < HEAD_DIM
    base = first_key + block * slots
    ek_ref[base : base + slots, :] = kept
    ev_ref[base : base + slots, :] = jnp.where(
        low, kept.astype(jnp.float32), jnp.where(mixed < DEAD_EDGE, 1.0, 0.0)
    ).astype(jnp.bfloat16)
    eq_ref[block * slots : block * slots + slots, :] = jnp.where(low, 0.0, mixed).astype(jnp.bfloat16)
    base = first_dec + block * tokens
    dk_ref[base : base + tokens, :] = got[slots : slots + tokens, :]


def begin_kernel(
    slots,
    tokens,
    own_ref,
    text_key_ref,
    text_value_ref,
    mask_ref,
    ek_ref,
    ev_ref,
    eq_ref,
    dk_ref,
    dq_ref,
    sums_ref,
    top_ref,
    fill_ref,
    *places
):
    chips = own_ref.shape[0]
    cols = text_key_ref.shape[2]
    spare = tokens - slots
    rest = slots // 2
    head = jnp.minimum(lax.axis_index("seq") // 2, cols // HEAD_DIM - 1)
    odd = lax.rem(head, 2) == 1
    lanes = pl.ds(pl.multiple_of((head // 2) * LANES, LANES), LANES)

    def low_high(rows):
        turned = pltpu.roll(rows, HEAD_DIM, 1)
        return jnp.where(odd, turned, rows), jnp.where(odd, rows, turned)

    key_low, key_high = low_high(text_key_ref[0, :, lanes].astype(jnp.float32))
    value_low, _ = low_high(text_value_ref[0, :, lanes].astype(jnp.float32))
    mask_row = jnp.zeros((1, LANES), jnp.float32)
    whole = mask_ref[...].astype(jnp.float32).reshape(1, cols)
    for tile in range(cols // LANES):
        mask_row = jnp.where(head // 2 == tile, whole[:, tile * LANES : (tile + 1) * LANES], mask_row)
    mask_row, _ = low_high(jnp.broadcast_to(mask_row, (8, LANES)))
    low = lane_of(tokens) < HEAD_DIM
    fill_ref[...] = jnp.where(lane_of(8) < HEAD_DIM, mask_row, 1.0)
    ek_ref[0:tokens, :] = jnp.where(low, value_low, key_high).astype(jnp.bfloat16)
    ev_ref[0:tokens, :] = jnp.where(low, value_low, 1.0).astype(jnp.bfloat16)
    dk_ref[0:tokens, :] = key_low.astype(jnp.bfloat16)
    for block in range(chips):
        got = own_ref.at[block]
        unpack(slots, tokens, got, block, tokens, tokens, ek_ref, ev_ref, eq_ref, dk_ref)
        tail = got[2 * slots : slots + tokens, :].astype(jnp.float32)
        last = got[slots + tokens : slots + tokens + rest, :].astype(jnp.float32)
        base = block * tokens
        dq_ref[base : base + spare, :] = jnp.where(
            lane_of(spare) < HEAD_DIM, pltpu.roll(tail, HEAD_DIM, 1), 0.0
        ).astype(jnp.bfloat16)
        low_rest = lane_of(rest) < HEAD_DIM
        dq_ref[base + spare : base + spare + rest, :] = jnp.where(low_rest, last, 0.0).astype(jnp.bfloat16)
        dq_ref[base + spare + rest : base + tokens, :] = jnp.where(
            low_rest, pltpu.roll(last, HEAD_DIM, 1), 0.0
        ).astype(jnp.bfloat16)

    rows = chips // 2 * slots

    def job(tile):
        span = slice(tile * rows, (tile + 1) * rows)

        def use(top, sums):
            sums_ref[span, :] = sums
            top_ref[span, :] = jnp.broadcast_to(top, (rows, LANES))

        return (lambda: eq_ref[span, :], [ek_ref], [ev_ref], None, use)

    run_jobs([job(tile) for tile in range(2)], (places[0:2], places[2:4]))


def attend_kernel(
    slots,
    tokens,
    pair_ref,
    ek_ref,
    ev_ref,
    eq_ref,
    dk_ref,
    dq_ref,
    sums_ref,
    top_ref,
    fill_ref,
    out_ref,
    pair_ek_ref,
    pair_ev_ref,
    pair_eq_ref,
    pair_dk_ref,
    dv_ref,
    *places
):
    chips = pair_ref.shape[0]
    spare = tokens - slots
    for block in range(chips):
        unpack(
            slots, tokens, pair_ref.at[block], block, 0, 0, pair_ek_ref, pair_ev_ref, pair_eq_ref, pair_dk_ref
        )
    dv_ref[0:tokens, :] = ev_ref[0:tokens, :]
    mask_row = fill_ref[0:1, :]
    fill = jnp.broadcast_to(mask_row, (spare, LANES)).astype(jnp.bfloat16)
    group = chips // 2
    rows = group * slots

    def encode(tile, query_ref, first_block, key_refs, value_refs, earlier):
        span = slice(tile * rows, (tile + 1) * rows)

        def use(top, sums):
            found = sums / pltpu.roll(sums, HEAD_DIM, 1)
            for inner in range(group):
                mixed = query_ref[tile * rows + inner * slots : tile * rows + (inner + 1) * slots, :]
                live = pltpu.roll(mixed.astype(jnp.float32), HEAD_DIM, 1) < DEAD_EDGE
                base = tokens + (first_block + tile * group + inner) * tokens
                dv_ref[base : base + slots, :] = jnp.where(
                    (lane_of(slots) < HEAD_DIM) & live, found[inner * slots : (inner + 1) * slots, :], mask_row
                ).astype(jnp.bfloat16)
                dv_ref[base + slots : base + tokens, :] = fill

        before = (lambda: (sums_ref[span, :], top_ref[span, :])) if earlier else None
        return (lambda: query_ref[span, :], key_refs, value_refs, before, use)

    dec_group = 4
    dec_rows = dec_group * tokens
    half = tokens // 2

    def decode(tile):
        def use(top, sums):
            found = sums / pltpu.roll(sums, HEAD_DIM, 1)
            for inner in range(dec_group):
                first = inner * tokens
                out_ref[tile * dec_group + inner] = jnp.where(
                    lane_of(half) < HEAD_DIM,
                    found[first : first + half],
                    pltpu.roll(found[first + half : first + tokens], HEAD_DIM, 1),
                ).astype(jnp.bfloat16)

        span = slice(tile * dec_rows, (tile + 1) * dec_rows)
        return (lambda: dq_ref[span, :], [dk_ref, pair_dk_ref], [dv_ref], None, use)

    jobs = [encode(tile, eq_ref, 0, [pair_ek_ref], [pair_ev_ref], True) for tile in range(2)]
    jobs += [
        encode(tile, pair_eq_ref, chips, [ek_ref, pair_ek_ref], [ev_ref, pair_ev_ref], False) for tile in range(2)
    ]
    jobs += [decode(tile) for tile in range(chips // dec_group)]
    run_jobs(jobs, (places[0:2], places[2:4]))


def sums_kernel(got_ref, gain_ref, target_ref, weight_ref, att_ref, sums_ref):
    tokens, cols = att_ref.shape
    half = tokens // 2
    low = lax.broadcasted_iota(jnp.int32, (half, LANES), 1) < HEAD_DIM
    for tile in range(cols // LANES):
        even = got_ref[2 * tile].astype(jnp.float32)
        odd = got_ref[2 * tile + 1].astype(jnp.float32)
        span = slice(tile * LANES, (tile + 1) * LANES)
        att_ref[0:half, span] = jnp.where(low, even, pltpu.roll(odd, HEAD_DIM, 1))
        att_ref[half:tokens, span] = jnp.where(low, pltpu.roll(even, HEAD_DIM, 1), odd)
    att = att_ref[...]
    gained = att * gain_ref[...].astype(jnp.float32)
    target = target_ref[0].astype(jnp.float32)
    weight = 1.0 / (0.1 + jnp.full((1, 1), weight_ref[0], jnp.int32).astype(jnp.float32) / 999.0)
    lane = lax.broadcasted_iota(jnp.int32, (tokens, LANES), 1)

    def over(block):
        return jnp.sum(block, axis=1, keepdims=True)

    table = jnp.where(
        lane == 1,
        over(gained * gained),
        jnp.where(lane == 2, over(gained * target), over(target * target)),
    )
    table = jnp.where(lane == 0, over(att * att), table * weight)
    sums_ref[...] = jnp.broadcast_to(jnp.transpose(table)[None, 0:4, :], sums_ref.shape)


def loss_kernel(heads, total_cols, sums_ref, loss_ref):
    total = None
    for image in range(sums_ref.shape[0] // heads):
        sums = jnp.sum(sums_ref[image * heads : (image + 1) * heads], axis=0)
        factor = lax.rsqrt(sums[0:1, :] / total_cols + 1e-06)
        error = factor * factor * sums[1:2, :] - 2.0 * factor * sums[2:3, :] + sums[3:4, :]
        total = error if total is None else total + error
    loss_ref[...] = jnp.broadcast_to(jnp.sum(total, axis=1, keepdims=True)[None], loss_ref.shape)


def norm_kernel(heads, total_cols, att_ref, gain_ref, sums_ref, out_ref):
    tokens = att_ref.shape[0]
    own = jnp.sum(sums_ref[pl.ds(lax.axis_index("dp") * heads, heads)], axis=0)
    factor = lax.rsqrt(own[0:1, :] / total_cols + 1e-06)
    column = jnp.transpose(jnp.broadcast_to(factor, (tokens, tokens)))[:, 0:1]
    out_ref[0] = (att_ref[...] * column * gain_ref[...].astype(jnp.float32)).astype(jnp.bfloat16)


def fold_kernel(count, got_ref, sum_ref):
    sum_ref[...] = (jnp.sum(got_ref[...], axis=0) / count)[0:1, 0:1]


def local(
    enc_query,
    enc_key,
    enc_value,
    keep_index,
    keep_count,
    text_key,
    text_value,
    dec_query,
    dec_key,
    mask_value,
    norm_gain,
    target,
    timesteps,
):
    images, seq, heads = (lax.axis_size(name) for name in ("dp", "seq", "head"))
    tokens, cols = enc_query.shape[1:]
    slots = keep_index.shape[1]
    local_heads = cols // HEAD_DIM
    chips = seq // 2
    packed = slots + tokens + slots // 2
    same_core = [[2 * chip + core for chip in range(chips)] for core in range(2)]
    bf16, f32 = jnp.bfloat16, jnp.float32
    gain = norm_gain.reshape(1, cols)

    send = pl.pallas_call(
        pack_kernel,
        out_shape=jax.ShapeDtypeStruct((chips, packed, LANES), bf16),
        in_specs=[pl.BlockSpec(memory_space=pltpu.SMEM)] + [pl.BlockSpec(memory_space=pltpu.HBM)] * 6,
        out_specs=pl.BlockSpec(memory_space=pltpu.HBM),
        scratch_shapes=[pltpu.VMEM((1, slots), jnp.int32)]
        + [pltpu.VMEM((1, tokens, cols), bf16)] * 5
        + [
            pltpu.VMEM((local_heads, packed, LANES), bf16),
            pltpu.SemaphoreType.DMA((6,)),
            pltpu.SemaphoreType.DMA((local_heads,)),
        ],
        compiler_params=params(60),
        name="pack",
    )(keep_count, keep_index, enc_query, enc_key, enc_value, dec_query, dec_key)
    own = lax.all_to_all(send, "seq", 0, 0, axis_index_groups=same_core, tiled=True)
    pair = lax.ppermute(own, "seq", [(source, source ^ 1) for source in range(seq)])
    kept_own = chips * slots
    dec_own = chips * tokens
    begun = pl.pallas_call(
        functools.partial(begin_kernel, slots, tokens),
        out_shape=(
            jax.ShapeDtypeStruct((tokens + kept_own, LANES), bf16),
            jax.ShapeDtypeStruct((tokens + kept_own, LANES), bf16),
            jax.ShapeDtypeStruct((kept_own, LANES), bf16),
            jax.ShapeDtypeStruct((tokens + dec_own, LANES), bf16),
            jax.ShapeDtypeStruct((dec_own, LANES), bf16),
            jax.ShapeDtypeStruct((kept_own, LANES), f32),
            jax.ShapeDtypeStruct((kept_own, LANES), f32),
            jax.ShapeDtypeStruct((8, LANES), f32),
        ),
        in_specs=vmem(4),
        out_specs=tuple(vmem(8)),
        scratch_shapes=[
            pltpu.VMEM((kept_own // 2, tokens + kept_own), f32),
            pltpu.VMEM((kept_own // 2, LANES), f32),
        ]
        * 2,
        compiler_params=params(),
        cost_estimate=pl.CostEstimate(
            flops=4 * kept_own * (tokens + kept_own) * LANES,
            bytes_accessed=8 * MIB,
            transcendentals=kept_own * (tokens + kept_own),
        ),
        name="begin",
    )(own, text_key, text_value, mask_value)
    out = pl.pallas_call(
        functools.partial(attend_kernel, slots, tokens),
        out_shape=jax.ShapeDtypeStruct((chips, tokens // 2, LANES), bf16),
        in_specs=vmem(9),
        out_specs=vmem(1)[0],
        scratch_shapes=[
            pltpu.VMEM((kept_own, LANES), bf16),
            pltpu.VMEM((kept_own, LANES), bf16),
            pltpu.VMEM((kept_own, LANES), bf16),
            pltpu.VMEM((dec_own, LANES), bf16),
            pltpu.VMEM((tokens + 2 * dec_own, LANES), bf16),
        ]
        + [
            pltpu.VMEM((dec_own // 2, tokens + 2 * dec_own), f32),
            pltpu.VMEM((dec_own // 2, LANES), f32),
        ]
        * 2,
        compiler_params=params(),
        name="attend",
    )(pair, *begun)
    got = lax.all_to_all(out, "seq", 0, 0, axis_index_groups=same_core, tiled=True)
    att, sums = pl.pallas_call(
        sums_kernel,
        out_shape=(
            jax.ShapeDtypeStruct((tokens, cols), f32),
            jax.ShapeDtypeStruct((images * heads, 4, tokens), f32),
        ),
        in_specs=vmem(3) + [pl.BlockSpec(memory_space=pltpu.SMEM)],
        out_specs=tuple(vmem(2)),
        compiler_params=params(),
        name="sums",
    )(got, gain, target, timesteps)
    sums = lax.all_to_all(sums, ("dp", "head"), 0, 0, tiled=True)
    loss = pl.pallas_call(
        functools.partial(loss_kernel, heads, cols * heads),
        out_shape=jax.ShapeDtypeStruct((seq, 1, LANES), f32),
        in_specs=vmem(1),
        out_specs=vmem(1)[0],
        compiler_params=params(),
        name="loss",
    )(sums)
    got = lax.all_to_all(loss, "seq", 0, 0, tiled=True)
    decoded = pl.pallas_call(
        functools.partial(norm_kernel, heads, cols * heads),
        out_shape=jax.ShapeDtypeStruct((1, tokens, cols), bf16),
        in_specs=vmem(3),
        out_specs=vmem(1)[0],
        compiler_params=params(),
        cost_estimate=pl.CostEstimate(flops=4 * tokens * cols, bytes_accessed=8 * tokens * cols, transcendentals=tokens),
        name="norm",
    )(att, gain, sums)
    loss = pl.pallas_call(
        functools.partial(fold_kernel, float(images * tokens * seq * cols * heads)),
        out_shape=jax.ShapeDtypeStruct((1, 1), f32),
        in_specs=vmem(1),
        out_specs=vmem(1)[0],
        compiler_params=params(),
        name="fold",
    )(got)
    total_loss = loss.reshape(())
    return (decoded, total_loss)


def solution(mesh):
    placed = (
        P("dp", "seq", "head"),
        P("dp", "seq", "head"),
        P("dp", "seq", "head"),
        P("dp", "seq"),
        P("dp", "seq"),
        P("dp", None, "head"),
        P("dp", None, "head"),
        P("dp", "seq", "head"),
        P("dp", "seq", "head"),
        P("head"),
        P("head"),
        P("dp", "seq", "head"),
        P("dp"),
    )
    return jax.shard_map(
        local, mesh=mesh, in_specs=placed, out_specs=(P("dp", "seq", "head"), P()), check_vma=False
    )
```

```python
import functools

import jax
import jax.numpy as jnp
from jax import lax
from jax.experimental import pallas as pl
from jax.experimental.pallas import tpu as pltpu
from jax.sharding import PartitionSpec as P

HEAD_DIM = 64
LANES = 128
DEAD = 1024.0
DEAD_EDGE = 512.0
MIB = 1024 * 1024


def params(mib=40):
    return pltpu.CompilerParams(vmem_limit_bytes=mib * MIB)


def vmem(count):
    return [pl.BlockSpec(memory_space=pltpu.VMEM)] * count


def one_hot_dot(table, rows):
    return lax.dot_general(
        table, rows, (((1,), (0,)), ((), ())), preferred_element_type=jnp.float32
    )


def pack_kernel(
    count_ref, index_hbm, eq_hbm, ek_hbm, ev_hbm, dq_hbm, dk_hbm, send_ref, *scratch
):
    *held, sems = scratch
    given = (index_hbm, eq_hbm, ek_hbm, ev_hbm, dq_hbm, dk_hbm)
    copies = [
        pltpu.make_async_copy(source, place, sems.at[number])
        for number, (source, place) in enumerate(zip(given, held))
    ]
    for copy in copies:
        copy.start()
    copies[0].wait()
    index_ref, eq_ref, ek_ref, ev_ref, dq_ref, dk_ref = held
    tokens, cols = eq_ref.shape[1:]
    slots = index_ref.shape[1]
    heads = cols // HEAD_DIM
    spare = tokens - slots
    total = count_ref[0, 0]
    index = jnp.broadcast_to(index_ref[...].astype(jnp.float32), (tokens, slots))
    index = jnp.transpose(index)
    token = lax.broadcasted_iota(jnp.int32, (slots, tokens), 1).astype(jnp.float32)
    slot = lax.broadcasted_iota(jnp.int32, (slots, tokens), 0)
    live = slot < total
    match_live = jnp.where(live & (token == index), 1.0, 0.0)
    match_fill = jnp.where(token == jnp.where(live, index, index[0:1, :]), 1.0, 0.0)
    kept = jnp.sum(match_live, axis=0, keepdims=True)
    kept_slot = jnp.sum(match_live * slot.astype(jnp.float32), axis=0, keepdims=True)
    row = lax.broadcasted_iota(jnp.int32, (tokens, tokens), 0)
    col = lax.broadcasted_iota(jnp.int32, (tokens, tokens), 1)
    before = jnp.where(row < col, 1.0, 0.0).astype(jnp.bfloat16)
    left = jnp.broadcast_to(1.0 - kept, (16, tokens)).astype(jnp.bfloat16)
    rank = one_hot_dot(left, before)[0:1, :]
    place = jnp.where(kept > 0.5, kept_slot, total.astype(jnp.float32) + rank)
    order = jnp.where(row.astype(jnp.float32) == place, 1.0, 0.0).astype(jnp.bfloat16)

    for copy in copies[1:]:
        copy.wait()
    scale = HEAD_DIM ** (-0.5)
    match_live = match_live.astype(jnp.bfloat16)
    match_fill = match_fill.astype(jnp.bfloat16)
    query = one_hot_dot(match_live, eq_ref[0]) * scale
    slot_wide = lax.broadcasted_iota(jnp.int32, (slots, cols), 0)
    query = jnp.where(slot_wide < total, query, DEAD)
    key = one_hot_dot(match_fill, ek_ref[0])
    value = one_hot_dot(match_live, ev_ref[0])
    dec_key = one_hot_dot(order, dk_ref[0])
    dec_query = dq_ref[0].astype(jnp.float32) * scale

    def low(block, head):
        tile = block[:, (head // 2) * LANES : (head // 2 + 1) * LANES]
        return tile if head % 2 == 0 else pltpu.roll(tile, HEAD_DIM, 1)

    def high(block, head):
        tile = block[:, (head // 2) * LANES : (head // 2 + 1) * LANES]
        return tile if head % 2 == 1 else pltpu.roll(tile, HEAD_DIM, 1)

    def join(first, second):
        lane = lax.broadcasted_iota(jnp.int32, first.shape, 1)
        return jnp.where(lane < HEAD_DIM, first, second).astype(jnp.bfloat16)

    for head in range(heads):
        kept_tile = join(low(value, head), high(key, head))
        query_high = high(query, head)
        dec_low = low(dec_key, head)
        dq_low = low(dec_query, head)
        dq_high = high(dec_query, head)
        send_ref[head, 0:slots, :] = kept_tile
        send_ref[head, slots : 2 * slots, :] = join(dec_low[0:slots], query_high)
        send_ref[head, 2 * slots : slots + tokens, :] = join(dec_low[slots:tokens], dq_high[0:spare])
        rest = slots // 2
        send_ref[head, slots + tokens : slots + tokens + rest, :] = join(
            dq_low[spare : spare + rest], dq_high[spare + rest : tokens]
        )


def put_scores(query, key_refs, place, peak):
    rows = query.shape[0]
    largest = None
    column = 0
    for key_ref in key_refs:
        keys = key_ref.shape[0]
        for first in range(0, keys, 2 * LANES):
            last = min(keys, first + 2 * LANES)
            part = lax.dot_general(
                query, key_ref[first:last, :], (((1,), (1,)), ((), ())), preferred_element_type=jnp.float32
            )
            place[0:rows, column : column + last - first] = part
            column += last - first
            for lane in range(0, last - first, LANES):
                tile = part[:, lane : lane + LANES]
                largest = tile if largest is None else jnp.maximum(largest, tile)
    peak[0:rows, :] = largest


def weigh(rows, place, peak, value_refs, earlier):
    top = jnp.max(peak[0:rows, :], axis=1, keepdims=True)
    sums = None
    if earlier is not None:
        earlier_sums, earlier_top = earlier
        top = jnp.maximum(top, earlier_top[:, 0:1])
        sums = earlier_sums * jnp.exp(earlier_top - top)
    column = 0
    for value_ref in value_refs:
        keys = value_ref.shape[0]
        weights = jnp.exp(place[0:rows, column : column + keys] - top).astype(jnp.bfloat16)
        column += keys
        part = lax.dot_general(
            weights, value_ref[...], (((1,), (0,)), ((), ())), preferred_element_type=jnp.float32
        )
        sums = part if sums is None else sums + part
    return top, sums


def run_jobs(jobs, buffers):
    def put(number):
        query, key_refs, _, _, _ = jobs[number]
        put_scores(query(), key_refs, *buffers[number % 2])

    put(0)
    for number, (query, _, value_refs, earlier, use) in enumerate(jobs):
        if number + 1 < len(jobs):
            put(number + 1)
        place, peak = buffers[number % 2]
        rows = query().shape[0]
        use(*weigh(rows, place, peak, value_refs, None if earlier is None else earlier()))


def lane_of(rows):
    return lax.broadcasted_iota(jnp.int32, (rows, LANES), 1)


def unpack(slots, tokens, got, block, first_key, first_dec, ek_ref, ev_ref, eq_ref, dk_ref):
    kept = got[0:slots, :]
    mixed = got[slots : 2 * slots, :].astype(jnp.float32)
    low = lane_of(slots) < HEAD_DIM
    base = first_key + block * slots
    ek_ref[base : base + slots, :] = kept
    ev_ref[base : base + slots, :] = jnp.where(
        low, kept.astype(jnp.float32), jnp.where(mixed < DEAD_EDGE, 1.0, 0.0)
    ).astype(jnp.bfloat16)
    eq_ref[block * slots : block * slots + slots, :] = jnp.where(low, 0.0, mixed).astype(jnp.bfloat16)
    base = first_dec + block * tokens
    dk_ref[base : base + tokens, :] = got[slots : slots + tokens, :]


def begin_kernel(
    slots,
    tokens,
    own_ref,
    text_key_ref,
    text_value_ref,
    mask_ref,
    gain_ref,
    steps_ref,
    ek_ref,
    ev_ref,
    eq_ref,
    dk_ref,
    dq_ref,
    sums_ref,
    top_ref,
    fill_ref,
    weight_ref,
    wide_gain_ref,
    *places
):
    chips = own_ref.shape[0]
    cols = text_key_ref.shape[2]
    spare = tokens - slots
    rest = slots // 2
    head = jnp.minimum(lax.axis_index("seq") // 2, cols // HEAD_DIM - 1)
    odd = lax.rem(head, 2) == 1
    lanes = pl.ds(pl.multiple_of((head // 2) * LANES, LANES), LANES)

    def low_high(rows):
        turned = pltpu.roll(rows, HEAD_DIM, 1)
        return jnp.where(odd, turned, rows), jnp.where(odd, rows, turned)

    key_low, key_high = low_high(text_key_ref[0, :, lanes].astype(jnp.float32))
    value_low, _ = low_high(text_value_ref[0, :, lanes].astype(jnp.float32))
    mask_row = jnp.zeros((1, LANES), jnp.float32)
    whole = mask_ref[...].astype(jnp.float32).reshape(1, cols)
    for tile in range(cols // LANES):
        mask_row = jnp.where(head // 2 == tile, whole[:, tile * LANES : (tile + 1) * LANES], mask_row)
    mask_row, _ = low_high(jnp.broadcast_to(mask_row, (8, LANES)))
    steps = jnp.full((8, LANES), steps_ref[0], jnp.int32).astype(jnp.float32)
    weight_ref[...] = 1.0 / (0.1 + steps / 999.0)
    wide_gain_ref[...] = jnp.broadcast_to(gain_ref[...].astype(jnp.float32).reshape(1, cols), (8, cols))
    low = lane_of(tokens) < HEAD_DIM
    fill_ref[...] = jnp.where(lane_of(8) < HEAD_DIM, mask_row, 1.0)
    ek_ref[0:tokens, :] = jnp.where(low, value_low, key_high).astype(jnp.bfloat16)
    ev_ref[0:tokens, :] = jnp.where(low, value_low, 1.0).astype(jnp.bfloat16)
    dk_ref[0:tokens, :] = key_low.astype(jnp.bfloat16)
    for block in range(chips):
        got = own_ref.at[block]
        unpack(slots, tokens, got, block, tokens, tokens, ek_ref, ev_ref, eq_ref, dk_ref)
        tail = got[2 * slots : slots + tokens, :].astype(jnp.float32)
        last = got[slots + tokens : slots + tokens + rest, :].astype(jnp.float32)
        base = block * tokens
        dq_ref[base : base + spare, :] = jnp.where(
            lane_of(spare) < HEAD_DIM, pltpu.roll(tail, HEAD_DIM, 1), 0.0
        ).astype(jnp.bfloat16)
        low_rest = lane_of(rest) < HEAD_DIM
        dq_ref[base + spare : base + spare + rest, :] = jnp.where(low_rest, last, 0.0).astype(jnp.bfloat16)
        dq_ref[base + spare + rest : base + tokens, :] = jnp.where(
            low_rest, pltpu.roll(last, HEAD_DIM, 1), 0.0
        ).astype(jnp.bfloat16)

    rows = chips // 2 * slots

    def job(tile):
        span = slice(tile * rows, (tile + 1) * rows)

        def use(top, sums):
            sums_ref[span, :] = sums
            top_ref[span, :] = jnp.broadcast_to(top, (rows, LANES))

        return (lambda: eq_ref[span, :], [ek_ref], [ev_ref], None, use)

    run_jobs([job(tile) for tile in range(2)], (places[0:2], places[2:4]))


def attend_kernel(
    slots,
    tokens,
    pair_ref,
    ek_ref,
    ev_ref,
    eq_ref,
    dk_ref,
    dq_ref,
    sums_ref,
    top_ref,
    fill_ref,
    out_ref,
    pair_ek_ref,
    pair_ev_ref,
    pair_eq_ref,
    pair_dk_ref,
    dv_ref,
    *places
):
    chips = pair_ref.shape[0]
    spare = tokens - slots
    for block in range(chips):
        unpack(
            slots, tokens, pair_ref.at[block], block, 0, 0, pair_ek_ref, pair_ev_ref, pair_eq_ref, pair_dk_ref
        )
    dv_ref[0:tokens, :] = ev_ref[0:tokens, :]
    mask_row = fill_ref[0:1, :]
    fill = jnp.broadcast_to(mask_row, (spare, LANES)).astype(jnp.bfloat16)
    group = chips // 2
    rows = group * slots

    def encode(tile, query_ref, first_block, key_refs, value_refs, earlier):
        span = slice(tile * rows, (tile + 1) * rows)

        def use(top, sums):
            found = sums / pltpu.roll(sums, HEAD_DIM, 1)
            for inner in range(group):
                mixed = query_ref[tile * rows + inner * slots : tile * rows + (inner + 1) * slots, :]
                live = pltpu.roll(mixed.astype(jnp.float32), HEAD_DIM, 1) < DEAD_EDGE
                base = tokens + (first_block + tile * group + inner) * tokens
                dv_ref[base : base + slots, :] = jnp.where(
                    (lane_of(slots) < HEAD_DIM) & live, found[inner * slots : (inner + 1) * slots, :], mask_row
                ).astype(jnp.bfloat16)
                dv_ref[base + slots : base + tokens, :] = fill

        before = (lambda: (sums_ref[span, :], top_ref[span, :])) if earlier else None
        return (lambda: query_ref[span, :], key_refs, value_refs, before, use)

    dec_group = 2
    dec_rows = dec_group * tokens
    half = tokens // 2

    def decode(tile):
        def use(top, sums):
            found = sums / pltpu.roll(sums, HEAD_DIM, 1)
            for inner in range(dec_group):
                first = inner * tokens
                out_ref[tile * dec_group + inner] = jnp.where(
                    lane_of(half) < HEAD_DIM,
                    found[first : first + half],
                    pltpu.roll(found[first + half : first + tokens], HEAD_DIM, 1),
                ).astype(jnp.bfloat16)

        span = slice(tile * dec_rows, (tile + 1) * dec_rows)
        return (lambda: dq_ref[span, :], [dk_ref, pair_dk_ref], [dv_ref], None, use)

    jobs = [encode(tile, eq_ref, 0, [pair_ek_ref], [pair_ev_ref], True) for tile in range(2)]
    jobs += [
        encode(tile, pair_eq_ref, chips, [ek_ref, pair_ek_ref], [ev_ref, pair_ev_ref], False) for tile in range(2)
    ]
    jobs += [decode(tile) for tile in range(chips // dec_group)]
    run_jobs(jobs, (places[0:2], places[2:4]))


def sums_kernel(got_ref, gain_ref, target_ref, weight_ref, att_ref, sums_ref):
    tokens, cols = att_ref.shape
    half = tokens // 2
    low = lax.broadcasted_iota(jnp.int32, (half, LANES), 1) < HEAD_DIM
    for tile in range(cols // LANES):
        even = got_ref[2 * tile].astype(jnp.float32)
        odd = got_ref[2 * tile + 1].astype(jnp.float32)
        span = slice(tile * LANES, (tile + 1) * LANES)
        att_ref[0:half, span] = jnp.where(low, even, pltpu.roll(odd, HEAD_DIM, 1))
        att_ref[half:tokens, span] = jnp.where(low, pltpu.roll(even, HEAD_DIM, 1), odd)
    att = att_ref[...]
    gained = att * gain_ref[0:1, :]
    target = target_ref[0].astype(jnp.float32)
    weight = weight_ref[0:1, :]
    lane = lax.broadcasted_iota(jnp.int32, (tokens, LANES), 1)

    def over(block):
        return jnp.sum(block, axis=1, keepdims=True)

    table = jnp.where(
        lane == 1,
        over(gained * gained),
        jnp.where(lane == 2, over(gained * target), over(target * target)),
    )
    table = jnp.where(lane == 0, over(att * att), table * weight)
    sums_ref[...] = jnp.broadcast_to(jnp.transpose(table)[None, 0:4, :], sums_ref.shape)


def loss_kernel(heads, total_cols, sums_ref, loss_ref):
    total = None
    for image in range(sums_ref.shape[0] // heads):
        sums = jnp.sum(sums_ref[image * heads : (image + 1) * heads], axis=0)
        factor = lax.rsqrt(sums[0:1, :] / total_cols + 1e-06)
        error = factor * factor * sums[1:2, :] - 2.0 * factor * sums[2:3, :] + sums[3:4, :]
        total = error if total is None else total + error
    loss_ref[...] = jnp.broadcast_to(jnp.sum(total, axis=1, keepdims=True)[None], loss_ref.shape)


def finish_kernel(heads, count, att_ref, gain_ref, sums_ref, got_ref, out_ref, loss_ref):
    tokens, cols = att_ref.shape
    loss_ref[...] = (jnp.sum(got_ref[...], axis=0) / count)[0:1, 0:1]
    own = jnp.sum(sums_ref[pl.ds(lax.axis_index("dp") * heads, heads)], axis=0)
    factor = lax.rsqrt(own[0:1, :] / (cols * heads) + 1e-06)
    column = jnp.transpose(jnp.broadcast_to(factor, (tokens, tokens)))[:, 0:1]
    out_ref[0] = (att_ref[...] * column * gain_ref[0:1, :]).astype(jnp.bfloat16)


def local(
    enc_query,
    enc_key,
    enc_value,
    keep_index,
    keep_count,
    text_key,
    text_value,
    dec_query,
    dec_key,
    mask_value,
    norm_gain,
    target,
    timesteps,
):
    images, seq, heads = (lax.axis_size(name) for name in ("dp", "seq", "head"))
    tokens, cols = enc_query.shape[1:]
    slots = keep_index.shape[1]
    local_heads = cols // HEAD_DIM
    chips = seq // 2
    packed = slots + tokens + slots // 2
    same_core = [[2 * chip + core for chip in range(chips)] for core in range(2)]
    bf16, f32 = jnp.bfloat16, jnp.float32

    send = pl.pallas_call(
        pack_kernel,
        out_shape=jax.ShapeDtypeStruct((chips, packed, LANES), bf16),
        in_specs=[pl.BlockSpec(memory_space=pltpu.SMEM)] + [pl.BlockSpec(memory_space=pltpu.HBM)] * 6,
        out_specs=vmem(1)[0],
        scratch_shapes=[pltpu.VMEM((1, slots), jnp.int32)]
        + [pltpu.VMEM((1, tokens, cols), bf16)] * 5
        + [pltpu.SemaphoreType.DMA((6,))],
        compiler_params=params(60),
        name="pack",
    )(keep_count, keep_index, enc_query, enc_key, enc_value, dec_query, dec_key)
    own = lax.all_to_all(send, "seq", 0, 0, axis_index_groups=same_core, tiled=True)
    pair = lax.ppermute(own, "seq", [(source, source ^ 1) for source in range(seq)])
    kept_own = chips * slots
    dec_own = chips * tokens
    *begun, weight, gain = pl.pallas_call(
        functools.partial(begin_kernel, slots, tokens),
        out_shape=(
            jax.ShapeDtypeStruct((tokens + kept_own, LANES), bf16),
            jax.ShapeDtypeStruct((tokens + kept_own, LANES), bf16),
            jax.ShapeDtypeStruct((kept_own, LANES), bf16),
            jax.ShapeDtypeStruct((tokens + dec_own, LANES), bf16),
            jax.ShapeDtypeStruct((dec_own, LANES), bf16),
            jax.ShapeDtypeStruct((kept_own, LANES), f32),
            jax.ShapeDtypeStruct((kept_own, LANES), f32),
            jax.ShapeDtypeStruct((8, LANES), f32),
            jax.ShapeDtypeStruct((8, LANES), f32),
            jax.ShapeDtypeStruct((8, cols), f32),
        ),
        in_specs=vmem(5) + [pl.BlockSpec(memory_space=pltpu.SMEM)],
        out_specs=tuple(vmem(10)),
        scratch_shapes=[
            pltpu.VMEM((kept_own // 2, tokens + kept_own), f32),
            pltpu.VMEM((kept_own // 2, LANES), f32),
        ]
        * 2,
        compiler_params=params(),
        cost_estimate=pl.CostEstimate(
            flops=4 * kept_own * (tokens + kept_own) * LANES,
            bytes_accessed=8 * MIB,
            transcendentals=kept_own * (tokens + kept_own),
        ),
        name="begin",
    )(own, text_key, text_value, mask_value, norm_gain, timesteps)
    out = pl.pallas_call(
        functools.partial(attend_kernel, slots, tokens),
        out_shape=jax.ShapeDtypeStruct((chips, tokens // 2, LANES), bf16),
        in_specs=vmem(9),
        out_specs=vmem(1)[0],
        scratch_shapes=[
            pltpu.VMEM((kept_own, LANES), bf16),
            pltpu.VMEM((kept_own, LANES), bf16),
            pltpu.VMEM((kept_own, LANES), bf16),
            pltpu.VMEM((dec_own, LANES), bf16),
            pltpu.VMEM((tokens + 2 * dec_own, LANES), bf16),
        ]
        + [
            pltpu.VMEM((kept_own // 2, tokens + 2 * dec_own), f32),
            pltpu.VMEM((kept_own // 2, LANES), f32),
        ]
        * 2,
        compiler_params=params(),
        name="attend",
    )(pair, *begun)
    got = lax.all_to_all(out, "seq", 0, 0, axis_index_groups=same_core, tiled=True)
    att, sums = pl.pallas_call(
        sums_kernel,
        out_shape=(
            jax.ShapeDtypeStruct((tokens, cols), f32),
            jax.ShapeDtypeStruct((images * heads, 4, tokens), f32),
        ),
        in_specs=vmem(4),
        out_specs=tuple(vmem(2)),
        compiler_params=params(),
        name="sums",
    )(got, gain, target, weight)
    sums = lax.all_to_all(sums, ("dp", "head"), 0, 0, tiled=True)
    loss = pl.pallas_call(
        functools.partial(loss_kernel, heads, cols * heads),
        out_shape=jax.ShapeDtypeStruct((seq, 1, LANES), f32),
        in_specs=vmem(1),
        out_specs=vmem(1)[0],
        compiler_params=params(),
        name="loss",
    )(sums)
    got = lax.all_to_all(loss, "seq", 0, 0, tiled=True)
    decoded, loss = pl.pallas_call(
        functools.partial(finish_kernel, heads, float(images * tokens * seq * cols * heads)),
        out_shape=(
            jax.ShapeDtypeStruct((1, tokens, cols), bf16),
            jax.ShapeDtypeStruct((1, 1), f32),
        ),
        in_specs=vmem(4),
        out_specs=tuple(vmem(2)),
        compiler_params=params(),
        name="finish",
    )(att, gain, sums, got)
    total_loss = loss.reshape(())
    return (decoded, total_loss)


def solution(mesh):
    placed = (
        P("dp", "seq", "head"),
        P("dp", "seq", "head"),
        P("dp", "seq", "head"),
        P("dp", "seq"),
        P("dp", "seq"),
        P("dp", None, "head"),
        P("dp", None, "head"),
        P("dp", "seq", "head"),
        P("dp", "seq", "head"),
        P("head"),
        P("head"),
        P("dp", "seq", "head"),
        P("dp"),
    )
    return jax.shard_map(
        local, mesh=mesh, in_specs=placed, out_specs=(P("dp", "seq", "head"), P()), check_vma=False
    )
```

```python
import functools

import jax
import jax.numpy as jnp
from jax import lax
from jax.experimental import pallas as pl
from jax.experimental.pallas import tpu as pltpu
from jax.sharding import PartitionSpec as P

HEAD_DIM = 64
LANES = 128
DEAD = 1024.0
DEAD_EDGE = 512.0
MIB = 1024 * 1024


def params(mib=40):
    return pltpu.CompilerParams(vmem_limit_bytes=mib * MIB)


def vmem(count):
    return [pl.BlockSpec(memory_space=pltpu.VMEM)] * count


def one_hot_dot(table, rows):
    return lax.dot_general(
        table, rows, (((1,), (0,)), ((), ())), preferred_element_type=jnp.float32
    )


def pack_kernel(
    count_hbm, index_hbm, eq_hbm, ek_hbm, ev_hbm, dq_hbm, dk_hbm, send_ref, *scratch
):
    *held, sems = scratch
    given = (count_hbm, index_hbm, eq_hbm, ek_hbm, ev_hbm, dq_hbm, dk_hbm)
    copies = [
        pltpu.make_async_copy(source, place, sems.at[number])
        for number, (source, place) in enumerate(zip(given, held))
    ]
    for copy in copies:
        copy.start()
    copies[0].wait()
    copies[1].wait()
    count_ref, index_ref, eq_ref, ek_ref, ev_ref, dq_ref, dk_ref = held
    tokens, cols = eq_ref.shape[1:]
    slots = index_ref.shape[1]
    heads = cols // HEAD_DIM
    spare = tokens - slots
    total = count_ref[0, 0]
    index = jnp.broadcast_to(index_ref[...].astype(jnp.float32), (tokens, slots))
    index = jnp.transpose(index)
    token = lax.broadcasted_iota(jnp.int32, (slots, tokens), 1).astype(jnp.float32)
    slot = lax.broadcasted_iota(jnp.int32, (slots, tokens), 0)
    live = slot < total
    match_live = jnp.where(live & (token == index), 1.0, 0.0)
    match_fill = jnp.where(token == jnp.where(live, index, index[0:1, :]), 1.0, 0.0)
    kept = jnp.sum(match_live, axis=0, keepdims=True)
    kept_slot = jnp.sum(match_live * slot.astype(jnp.float32), axis=0, keepdims=True)
    row = lax.broadcasted_iota(jnp.int32, (tokens, tokens), 0)
    col = lax.broadcasted_iota(jnp.int32, (tokens, tokens), 1)
    before = jnp.where(row < col, 1.0, 0.0).astype(jnp.bfloat16)
    left = jnp.broadcast_to(1.0 - kept, (16, tokens)).astype(jnp.bfloat16)
    rank = one_hot_dot(left, before)[0:1, :]
    place = jnp.where(kept > 0.5, kept_slot, total.astype(jnp.float32) + rank)
    order = jnp.where(row.astype(jnp.float32) == place, 1.0, 0.0).astype(jnp.bfloat16)

    for copy in copies[2:]:
        copy.wait()
    scale = HEAD_DIM ** (-0.5)
    match_live = match_live.astype(jnp.bfloat16)
    match_fill = match_fill.astype(jnp.bfloat16)
    query = one_hot_dot(match_live, eq_ref[0]) * scale
    slot_wide = lax.broadcasted_iota(jnp.int32, (slots, cols), 0)
    query = jnp.where(slot_wide < total, query, DEAD)
    key = one_hot_dot(match_fill, ek_ref[0])
    value = one_hot_dot(match_live, ev_ref[0])
    dec_key = one_hot_dot(order, dk_ref[0])
    dec_query = dq_ref[0].astype(jnp.float32) * scale

    def low(block, head):
        tile = block[:, (head // 2) * LANES : (head // 2 + 1) * LANES]
        return tile if head % 2 == 0 else pltpu.roll(tile, HEAD_DIM, 1)

    def high(block, head):
        tile = block[:, (head // 2) * LANES : (head // 2 + 1) * LANES]
        return tile if head % 2 == 1 else pltpu.roll(tile, HEAD_DIM, 1)

    def join(first, second):
        lane = lax.broadcasted_iota(jnp.int32, first.shape, 1)
        return jnp.where(lane < HEAD_DIM, first, second).astype(jnp.bfloat16)

    for head in range(heads):
        kept_tile = join(low(value, head), high(key, head))
        query_high = high(query, head)
        dec_low = low(dec_key, head)
        dq_low = low(dec_query, head)
        dq_high = high(dec_query, head)
        send_ref[head, 0:slots, :] = kept_tile
        send_ref[head, slots : 2 * slots, :] = join(dec_low[0:slots], query_high)
        send_ref[head, 2 * slots : slots + tokens, :] = join(dec_low[slots:tokens], dq_high[0:spare])
        rest = slots // 2
        send_ref[head, slots + tokens : slots + tokens + rest, :] = join(
            dq_low[spare : spare + rest], dq_high[spare + rest : tokens]
        )


def put_scores(query, key_refs, place, peak):
    rows = query.shape[0]
    largest = None
    column = 0
    for key_ref in key_refs:
        keys = key_ref.shape[0]
        for first in range(0, keys, 2 * LANES):
            last = min(keys, first + 2 * LANES)
            part = lax.dot_general(
                query, key_ref[first:last, :], (((1,), (1,)), ((), ())), preferred_element_type=jnp.float32
            )
            place[0:rows, column : column + last - first] = part
            column += last - first
            for lane in range(0, last - first, LANES):
                tile = part[:, lane : lane + LANES]
                largest = tile if largest is None else jnp.maximum(largest, tile)
    peak[0:rows, :] = largest


def weigh(rows, place, peak, value_refs, earlier):
    top = jnp.max(peak[0:rows, :], axis=1, keepdims=True)
    sums = None
    if earlier is not None:
        earlier_sums, earlier_top = earlier
        top = jnp.maximum(top, earlier_top[:, 0:1])
        sums = earlier_sums * jnp.exp(earlier_top - top)
    column = 0
    for value_ref in value_refs:
        keys = value_ref.shape[0]
        weights = jnp.exp(place[0:rows, column : column + keys] - top).astype(jnp.bfloat16)
        column += keys
        part = lax.dot_general(
            weights, value_ref[...], (((1,), (0,)), ((), ())), preferred_element_type=jnp.float32
        )
        sums = part if sums is None else sums + part
    return top, sums


def run_jobs(jobs, buffers):
    def put(number):
        query, key_refs, _, _, _ = jobs[number]
        put_scores(query(), key_refs, *buffers[number % 2])

    put(0)
    for number, (query, _, value_refs, earlier, use) in enumerate(jobs):
        if number + 1 < len(jobs):
            put(number + 1)
        place, peak = buffers[number % 2]
        rows = query().shape[0]
        use(*weigh(rows, place, peak, value_refs, None if earlier is None else earlier()))


def lane_of(rows):
    return lax.broadcasted_iota(jnp.int32, (rows, LANES), 1)


def unpack(slots, tokens, got, block, first_key, first_dec, ek_ref, ev_ref, eq_ref, dk_ref):
    kept = got[0:slots, :]
    mixed = got[slots : 2 * slots, :].astype(jnp.float32)
    low = lane_of(slots) < HEAD_DIM
    base = first_key + block * slots
    ek_ref[base : base + slots, :] = kept
    ev_ref[base : base + slots, :] = jnp.where(
        low, kept.astype(jnp.float32), jnp.where(mixed < DEAD_EDGE, 1.0, 0.0)
    ).astype(jnp.bfloat16)
    eq_ref[block * slots : block * slots + slots, :] = jnp.where(low, 0.0, mixed).astype(jnp.bfloat16)
    base = first_dec + block * tokens
    dk_ref[base : base + tokens, :] = got[slots : slots + tokens, :]


def begin_kernel(
    slots,
    tokens,
    own_ref,
    text_key_ref,
    text_value_ref,
    mask_ref,
    gain_ref,
    steps_hbm,
    ek_ref,
    ev_ref,
    eq_ref,
    dk_ref,
    dq_ref,
    sums_ref,
    top_ref,
    fill_ref,
    weight_ref,
    wide_gain_ref,
    steps_ref,
    steps_sem,
    *places
):
    steps_copy = pltpu.make_async_copy(steps_hbm, steps_ref, steps_sem)
    steps_copy.start()
    chips = own_ref.shape[0]
    cols = text_key_ref.shape[2]
    spare = tokens - slots
    rest = slots // 2
    head = jnp.minimum(lax.axis_index("seq") // 2, cols // HEAD_DIM - 1)
    odd = lax.rem(head, 2) == 1
    lanes = pl.ds(pl.multiple_of((head // 2) * LANES, LANES), LANES)

    def low_high(rows):
        turned = pltpu.roll(rows, HEAD_DIM, 1)
        return jnp.where(odd, turned, rows), jnp.where(odd, rows, turned)

    key_low, key_high = low_high(text_key_ref[0, :, lanes].astype(jnp.float32))
    value_low, _ = low_high(text_value_ref[0, :, lanes].astype(jnp.float32))
    mask_row = jnp.zeros((1, LANES), jnp.float32)
    whole = mask_ref[...].astype(jnp.float32).reshape(1, cols)
    for tile in range(cols // LANES):
        mask_row = jnp.where(head // 2 == tile, whole[:, tile * LANES : (tile + 1) * LANES], mask_row)
    mask_row, _ = low_high(jnp.broadcast_to(mask_row, (8, LANES)))
    wide_gain_ref[...] = jnp.broadcast_to(gain_ref[...].astype(jnp.float32).reshape(1, cols), (8, cols))
    low = lane_of(tokens) < HEAD_DIM
    fill_ref[...] = jnp.where(lane_of(8) < HEAD_DIM, mask_row, 1.0)
    ek_ref[0:tokens, :] = jnp.where(low, value_low, key_high).astype(jnp.bfloat16)
    ev_ref[0:tokens, :] = jnp.where(low, value_low, 1.0).astype(jnp.bfloat16)
    dk_ref[0:tokens, :] = key_low.astype(jnp.bfloat16)
    for block in range(chips):
        got = own_ref.at[block]
        unpack(slots, tokens, got, block, tokens, tokens, ek_ref, ev_ref, eq_ref, dk_ref)
        tail = got[2 * slots : slots + tokens, :].astype(jnp.float32)
        last = got[slots + tokens : slots + tokens + rest, :].astype(jnp.float32)
        base = block * tokens
        dq_ref[base : base + spare, :] = jnp.where(
            lane_of(spare) < HEAD_DIM, pltpu.roll(tail, HEAD_DIM, 1), 0.0
        ).astype(jnp.bfloat16)
        low_rest = lane_of(rest) < HEAD_DIM
        dq_ref[base + spare : base + spare + rest, :] = jnp.where(low_rest, last, 0.0).astype(jnp.bfloat16)
        dq_ref[base + spare + rest : base + tokens, :] = jnp.where(
            low_rest, pltpu.roll(last, HEAD_DIM, 1), 0.0
        ).astype(jnp.bfloat16)

    rows = chips // 2 * slots

    def job(tile):
        span = slice(tile * rows, (tile + 1) * rows)

        def use(top, sums):
            sums_ref[span, :] = sums
            top_ref[span, :] = jnp.broadcast_to(top, (rows, LANES))

        return (lambda: eq_ref[span, :], [ek_ref], [ev_ref], None, use)

    run_jobs([job(tile) for tile in range(2)], (places[0:2], places[2:4]))
    steps_copy.wait()
    steps = jnp.full((8, LANES), steps_ref[0], jnp.int32).astype(jnp.float32)
    weight_ref[...] = 1.0 / (0.1 + steps / 999.0)


def attend_kernel(
    slots,
    tokens,
    pair_ref,
    ek_ref,
    ev_ref,
    eq_ref,
    dk_ref,
    dq_ref,
    sums_ref,
    top_ref,
    fill_ref,
    out_ref,
    pair_ek_ref,
    pair_ev_ref,
    pair_eq_ref,
    pair_dk_ref,
    dv_ref,
    *places
):
    chips = pair_ref.shape[0]
    spare = tokens - slots
    for block in range(chips):
        unpack(
            slots, tokens, pair_ref.at[block], block, 0, 0, pair_ek_ref, pair_ev_ref, pair_eq_ref, pair_dk_ref
        )
    dv_ref[0:tokens, :] = ev_ref[0:tokens, :]
    mask_row = fill_ref[0:1, :]
    fill = jnp.broadcast_to(mask_row, (spare, LANES)).astype(jnp.bfloat16)
    group = chips // 2
    rows = group * slots

    def encode(tile, query_ref, first_block, key_refs, value_refs, earlier):
        span = slice(tile * rows, (tile + 1) * rows)

        def use(top, sums):
            found = sums / pltpu.roll(sums, HEAD_DIM, 1)
            for inner in range(group):
                mixed = query_ref[tile * rows + inner * slots : tile * rows + (inner + 1) * slots, :]
                live = pltpu.roll(mixed.astype(jnp.float32), HEAD_DIM, 1) < DEAD_EDGE
                base = tokens + (first_block + tile * group + inner) * tokens
                dv_ref[base : base + slots, :] = jnp.where(
                    (lane_of(slots) < HEAD_DIM) & live, found[inner * slots : (inner + 1) * slots, :], mask_row
                ).astype(jnp.bfloat16)
                dv_ref[base + slots : base + tokens, :] = fill

        before = (lambda: (sums_ref[span, :], top_ref[span, :])) if earlier else None
        return (lambda: query_ref[span, :], key_refs, value_refs, before, use)

    dec_group = 2
    dec_rows = dec_group * tokens
    half = tokens // 2

    def decode(tile):
        def use(top, sums):
            found = sums / pltpu.roll(sums, HEAD_DIM, 1)
            for inner in range(dec_group):
                first = inner * tokens
                out_ref[tile * dec_group + inner] = jnp.where(
                    lane_of(half) < HEAD_DIM,
                    found[first : first + half],
                    pltpu.roll(found[first + half : first + tokens], HEAD_DIM, 1),
                ).astype(jnp.bfloat16)

        span = slice(tile * dec_rows, (tile + 1) * dec_rows)
        return (lambda: dq_ref[span, :], [dk_ref, pair_dk_ref], [dv_ref], None, use)

    jobs = [encode(tile, eq_ref, 0, [pair_ek_ref], [pair_ev_ref], True) for tile in range(2)]
    jobs += [
        encode(tile, pair_eq_ref, chips, [ek_ref, pair_ek_ref], [ev_ref, pair_ev_ref], False) for tile in range(2)
    ]
    jobs += [decode(tile) for tile in range(chips // dec_group)]
    run_jobs(jobs, (places[0:2], places[2:4]))


def sums_kernel(got_ref, gain_ref, target_ref, weight_ref, att_ref, sums_ref):
    tokens, cols = att_ref.shape
    half = tokens // 2
    low = lax.broadcasted_iota(jnp.int32, (half, LANES), 1) < HEAD_DIM
    for tile in range(cols // LANES):
        even = got_ref[2 * tile].astype(jnp.float32)
        odd = got_ref[2 * tile + 1].astype(jnp.float32)
        span = slice(tile * LANES, (tile + 1) * LANES)
        att_ref[0:half, span] = jnp.where(low, even, pltpu.roll(odd, HEAD_DIM, 1))
        att_ref[half:tokens, span] = jnp.where(low, pltpu.roll(even, HEAD_DIM, 1), odd)
    att = att_ref[...]
    gained = att * gain_ref[0:1, :]
    target = target_ref[0].astype(jnp.float32)
    weight = weight_ref[0:1, :]
    lane = lax.broadcasted_iota(jnp.int32, (tokens, LANES), 1)

    def over(block):
        return jnp.sum(block, axis=1, keepdims=True)

    table = jnp.where(
        lane == 1,
        over(gained * gained),
        jnp.where(lane == 2, over(gained * target), over(target * target)),
    )
    table = jnp.where(lane == 0, over(att * att), table * weight)
    sums_ref[...] = jnp.broadcast_to(jnp.transpose(table)[None, 0:4, :], sums_ref.shape)


def loss_kernel(heads, total_cols, sums_ref, loss_ref):
    total = None
    for image in range(sums_ref.shape[0] // heads):
        sums = jnp.sum(sums_ref[image * heads : (image + 1) * heads], axis=0)
        factor = lax.rsqrt(sums[0:1, :] / total_cols + 1e-06)
        error = factor * factor * sums[1:2, :] - 2.0 * factor * sums[2:3, :] + sums[3:4, :]
        total = error if total is None else total + error
    loss_ref[...] = jnp.broadcast_to(jnp.sum(total, axis=1, keepdims=True)[None], loss_ref.shape)


def finish_kernel(heads, count, att_ref, gain_ref, sums_ref, got_ref, out_ref, loss_ref):
    tokens, cols = att_ref.shape
    loss_ref[...] = (jnp.sum(got_ref[...], axis=0) / count)[0:1, 0:1]
    own = jnp.sum(sums_ref[pl.ds(lax.axis_index("dp") * heads, heads)], axis=0)
    factor = lax.rsqrt(own[0:1, :] / (cols * heads) + 1e-06)
    column = jnp.transpose(jnp.broadcast_to(factor, (tokens, tokens)))[:, 0:1]
    out_ref[0] = (att_ref[...] * column * gain_ref[0:1, :]).astype(jnp.bfloat16)


def local(
    enc_query,
    enc_key,
    enc_value,
    keep_index,
    keep_count,
    text_key,
    text_value,
    dec_query,
    dec_key,
    mask_value,
    norm_gain,
    target,
    timesteps,
):
    images, seq, heads = (lax.axis_size(name) for name in ("dp", "seq", "head"))
    tokens, cols = enc_query.shape[1:]
    slots = keep_index.shape[1]
    local_heads = cols // HEAD_DIM
    chips = seq // 2
    packed = slots + tokens + slots // 2
    same_core = [[2 * chip + core for chip in range(chips)] for core in range(2)]
    bf16, f32 = jnp.bfloat16, jnp.float32

    send = pl.pallas_call(
        pack_kernel,
        out_shape=jax.ShapeDtypeStruct((chips, packed, LANES), bf16),
        in_specs=[pl.BlockSpec(memory_space=pltpu.HBM)] * 7,
        out_specs=vmem(1)[0],
        scratch_shapes=[pltpu.SMEM((1, 1), jnp.int32), pltpu.VMEM((1, slots), jnp.int32)]
        + [pltpu.VMEM((1, tokens, cols), bf16)] * 5
        + [pltpu.SemaphoreType.DMA((7,))],
        compiler_params=params(60),
        name="pack",
    )(keep_count, keep_index, enc_query, enc_key, enc_value, dec_query, dec_key)
    own = lax.all_to_all(send, "seq", 0, 0, axis_index_groups=same_core, tiled=True)
    pair = lax.ppermute(own, "seq", [(source, source ^ 1) for source in range(seq)])
    kept_own = chips * slots
    dec_own = chips * tokens
    *begun, weight, gain = pl.pallas_call(
        functools.partial(begin_kernel, slots, tokens),
        out_shape=(
            jax.ShapeDtypeStruct((tokens + kept_own, LANES), bf16),
            jax.ShapeDtypeStruct((tokens + kept_own, LANES), bf16),
            jax.ShapeDtypeStruct((kept_own, LANES), bf16),
            jax.ShapeDtypeStruct((tokens + dec_own, LANES), bf16),
            jax.ShapeDtypeStruct((dec_own, LANES), bf16),
            jax.ShapeDtypeStruct((kept_own, LANES), f32),
            jax.ShapeDtypeStruct((kept_own, LANES), f32),
            jax.ShapeDtypeStruct((8, LANES), f32),
            jax.ShapeDtypeStruct((8, LANES), f32),
            jax.ShapeDtypeStruct((8, cols), f32),
        ),
        in_specs=vmem(5) + [pl.BlockSpec(memory_space=pltpu.HBM)],
        out_specs=tuple(vmem(10)),
        scratch_shapes=[pltpu.SMEM((1,), jnp.int32), pltpu.SemaphoreType.DMA]
        + [
            pltpu.VMEM((kept_own // 2, tokens + kept_own), f32),
            pltpu.VMEM((kept_own // 2, LANES), f32),
        ]
        * 2,
        compiler_params=params(),
        cost_estimate=pl.CostEstimate(
            flops=4 * kept_own * (tokens + kept_own) * LANES,
            bytes_accessed=8 * MIB,
            transcendentals=kept_own * (tokens + kept_own),
        ),
        name="begin",
    )(own, text_key, text_value, mask_value, norm_gain, timesteps)
    out = pl.pallas_call(
        functools.partial(attend_kernel, slots, tokens),
        out_shape=jax.ShapeDtypeStruct((chips, tokens // 2, LANES), bf16),
        in_specs=vmem(9),
        out_specs=vmem(1)[0],
        scratch_shapes=[
            pltpu.VMEM((kept_own, LANES), bf16),
            pltpu.VMEM((kept_own, LANES), bf16),
            pltpu.VMEM((kept_own, LANES), bf16),
            pltpu.VMEM((dec_own, LANES), bf16),
            pltpu.VMEM((tokens + 2 * dec_own, LANES), bf16),
        ]
        + [
            pltpu.VMEM((kept_own // 2, tokens + 2 * dec_own), f32),
            pltpu.VMEM((kept_own // 2, LANES), f32),
        ]
        * 2,
        compiler_params=params(),
        name="attend",
    )(pair, *begun)
    got = lax.all_to_all(out, "seq", 0, 0, axis_index_groups=same_core, tiled=True)
    att, sums = pl.pallas_call(
        sums_kernel,
        out_shape=(
            jax.ShapeDtypeStruct((tokens, cols), f32),
            jax.ShapeDtypeStruct((images * heads, 4, tokens), f32),
        ),
        in_specs=vmem(4),
        out_specs=tuple(vmem(2)),
        compiler_params=params(),
        name="sums",
    )(got, gain, target, weight)
    sums = lax.all_to_all(sums, ("dp", "head"), 0, 0, tiled=True)
    loss = pl.pallas_call(
        functools.partial(loss_kernel, heads, cols * heads),
        out_shape=jax.ShapeDtypeStruct((seq, 1, LANES), f32),
        in_specs=vmem(1),
        out_specs=vmem(1)[0],
        compiler_params=params(),
        name="loss",
    )(sums)
    got = lax.all_to_all(loss, "seq", 0, 0, tiled=True)
    decoded, loss = pl.pallas_call(
        functools.partial(finish_kernel, heads, float(images * tokens * seq * cols * heads)),
        out_shape=(
            jax.ShapeDtypeStruct((1, tokens, cols), bf16),
            jax.ShapeDtypeStruct((1, 1), f32),
        ),
        in_specs=vmem(4),
        out_specs=tuple(vmem(2)),
        compiler_params=params(),
        name="finish",
    )(att, gain, sums, got)
    total_loss = loss.reshape(())
    return (decoded, total_loss)


def solution(mesh):
    placed = (
        P("dp", "seq", "head"),
        P("dp", "seq", "head"),
        P("dp", "seq", "head"),
        P("dp", "seq"),
        P("dp", "seq"),
        P("dp", None, "head"),
        P("dp", None, "head"),
        P("dp", "seq", "head"),
        P("dp", "seq", "head"),
        P("head"),
        P("head"),
        P("dp", "seq", "head"),
        P("dp"),
    )
    return jax.shard_map(
        local, mesh=mesh, in_specs=placed, out_specs=(P("dp", "seq", "head"), P()), check_vma=False
    )
```

```python
import functools

import jax
import jax.numpy as jnp
from jax import lax
from jax.experimental import pallas as pl
from jax.experimental.pallas import tpu as pltpu
from jax.sharding import PartitionSpec as P

HEAD_DIM = 64
LANES = 128
DEAD = 1024.0
DEAD_EDGE = 512.0
MIB = 1024 * 1024


def params(mib=40):
    return pltpu.CompilerParams(vmem_limit_bytes=mib * MIB)


def vmem(count):
    return [pl.BlockSpec(memory_space=pltpu.VMEM)] * count


def one_hot_dot(table, rows):
    return lax.dot_general(
        table, rows, (((1,), (0,)), ((), ())), preferred_element_type=jnp.float32
    )


def pack_kernel(
    index_hbm, eq_hbm, ek_hbm, ev_hbm, dq_hbm, dk_hbm, send_ref, *scratch
):
    *held, sems = scratch
    given = (index_hbm, eq_hbm, ek_hbm, ev_hbm, dq_hbm, dk_hbm)
    copies = [
        pltpu.make_async_copy(source, place, sems.at[number])
        for number, (source, place) in enumerate(zip(given, held))
    ]
    for copy in copies:
        copy.start()
    copies[0].wait()
    index_ref, eq_ref, ek_ref, ev_ref, dq_ref, dk_ref = held
    tokens, cols = eq_ref.shape[1:]
    slots = index_ref.shape[1]
    heads = cols // HEAD_DIM
    spare = tokens - slots
    index = jnp.broadcast_to(index_ref[...].astype(jnp.float32), (tokens, slots))
    index = jnp.transpose(index)
    token = lax.broadcasted_iota(jnp.int32, (slots, tokens), 1).astype(jnp.float32)
    slot = lax.broadcasted_iota(jnp.int32, (slots, tokens), 0)
    live = (slot == 0) | (index > 0.5)
    match_live = jnp.where(live & (token == index), 1.0, 0.0)
    match_fill = jnp.where(token == jnp.where(live, index, index[0:1, :]), 1.0, 0.0)
    kept = jnp.sum(match_live, axis=0, keepdims=True)
    kept_slot = jnp.sum(match_live * slot.astype(jnp.float32), axis=0, keepdims=True)
    row = lax.broadcasted_iota(jnp.int32, (tokens, tokens), 0)
    col = lax.broadcasted_iota(jnp.int32, (tokens, tokens), 1)
    before = jnp.where(row < col, 1.0, 0.0).astype(jnp.bfloat16)
    left = jnp.broadcast_to(1.0 - kept, (16, tokens)).astype(jnp.bfloat16)
    rank = one_hot_dot(left, before)[0:1, :]
    place = jnp.where(kept > 0.5, kept_slot, jnp.sum(kept, axis=1, keepdims=True) + rank)
    order = jnp.where(row.astype(jnp.float32) == place, 1.0, 0.0).astype(jnp.bfloat16)

    for copy in copies[1:]:
        copy.wait()
    scale = HEAD_DIM ** (-0.5)
    match_live = match_live.astype(jnp.bfloat16)
    match_fill = match_fill.astype(jnp.bfloat16)
    query = one_hot_dot(match_live, eq_ref[0]) * scale
    dead = jnp.where(live, 0.0, DEAD)
    query = query + jnp.concatenate([dead] * (cols // tokens), axis=1)
    key = one_hot_dot(match_fill, ek_ref[0])
    value = one_hot_dot(match_live, ev_ref[0])
    dec_key = one_hot_dot(order, dk_ref[0])
    dec_query = dq_ref[0].astype(jnp.float32) * scale

    def low(block, head):
        tile = block[:, (head // 2) * LANES : (head // 2 + 1) * LANES]
        return tile if head % 2 == 0 else pltpu.roll(tile, HEAD_DIM, 1)

    def high(block, head):
        tile = block[:, (head // 2) * LANES : (head // 2 + 1) * LANES]
        return tile if head % 2 == 1 else pltpu.roll(tile, HEAD_DIM, 1)

    def join(first, second):
        lane = lax.broadcasted_iota(jnp.int32, first.shape, 1)
        return jnp.where(lane < HEAD_DIM, first, second).astype(jnp.bfloat16)

    for head in range(heads):
        kept_tile = join(low(value, head), high(key, head))
        query_high = high(query, head)
        dec_low = low(dec_key, head)
        dq_low = low(dec_query, head)
        dq_high = high(dec_query, head)
        send_ref[head, 0:slots, :] = kept_tile
        send_ref[head, slots : 2 * slots, :] = join(dec_low[0:slots], query_high)
        send_ref[head, 2 * slots : slots + tokens, :] = join(dec_low[slots:tokens], dq_high[0:spare])
        rest = slots // 2
        send_ref[head, slots + tokens : slots + tokens + rest, :] = join(
            dq_low[spare : spare + rest], dq_high[spare + rest : tokens]
        )


def put_scores(query, key_refs, place, peak):
    rows = query.shape[0]
    largest = None
    column = 0
    for key_ref in key_refs:
        keys = key_ref.shape[0]
        for first in range(0, keys, 2 * LANES):
            last = min(keys, first + 2 * LANES)
            part = lax.dot_general(
                query, key_ref[first:last, :], (((1,), (1,)), ((), ())), preferred_element_type=jnp.float32
            )
            place[0:rows, column : column + last - first] = part
            column += last - first
            for lane in range(0, last - first, LANES):
                tile = part[:, lane : lane + LANES]
                largest = tile if largest is None else jnp.maximum(largest, tile)
    peak[0:rows, :] = largest


def weigh(rows, place, peak, value_refs, earlier):
    top = jnp.max(peak[0:rows, :], axis=1, keepdims=True)
    sums = None
    if earlier is not None:
        earlier_sums, earlier_top = earlier
        top = jnp.maximum(top, earlier_top[:, 0:1])
        sums = earlier_sums * jnp.exp(earlier_top - top)
    column = 0
    for value_ref in value_refs:
        keys = value_ref.shape[0]
        weights = jnp.exp(place[0:rows, column : column + keys] - top).astype(jnp.bfloat16)
        column += keys
        part = lax.dot_general(
            weights, value_ref[...], (((1,), (0,)), ((), ())), preferred_element_type=jnp.float32
        )
        sums = part if sums is None else sums + part
    return top, sums


def run_jobs(jobs, buffers):
    def put(number):
        query, key_refs, _, _, _ = jobs[number]
        put_scores(query(), key_refs, *buffers[number % 2])

    put(0)
    for number, (query, _, value_refs, earlier, use) in enumerate(jobs):
        if number + 1 < len(jobs):
            put(number + 1)
        place, peak = buffers[number % 2]
        rows = query().shape[0]
        use(*weigh(rows, place, peak, value_refs, None if earlier is None else earlier()))


def lane_of(rows):
    return lax.broadcasted_iota(jnp.int32, (rows, LANES), 1)


def unpack(slots, tokens, got, block, first_key, first_dec, ek_ref, ev_ref, eq_ref, dk_ref):
    kept = got[0:slots, :]
    mixed = got[slots : 2 * slots, :].astype(jnp.float32)
    low = lane_of(slots) < HEAD_DIM
    base = first_key + block * slots
    ek_ref[base : base + slots, :] = kept
    ev_ref[base : base + slots, :] = jnp.where(
        low, kept.astype(jnp.float32), jnp.where(mixed < DEAD_EDGE, 1.0, 0.0)
    ).astype(jnp.bfloat16)
    eq_ref[block * slots : block * slots + slots, :] = jnp.where(low, 0.0, mixed).astype(jnp.bfloat16)
    base = first_dec + block * tokens
    dk_ref[base : base + tokens, :] = got[slots : slots + tokens, :]


def begin_kernel(
    slots,
    tokens,
    own_ref,
    text_key_ref,
    text_value_ref,
    mask_ref,
    gain_ref,
    steps_ref,
    ek_ref,
    ev_ref,
    eq_ref,
    dk_ref,
    dq_ref,
    sums_ref,
    top_ref,
    fill_ref,
    weight_ref,
    wide_gain_ref,
    *places
):
    chips = own_ref.shape[0]
    cols = text_key_ref.shape[2]
    spare = tokens - slots
    rest = slots // 2
    head = jnp.minimum(lax.axis_index("seq") // 2, cols // HEAD_DIM - 1)
    odd = lax.rem(head, 2) == 1
    lanes = pl.ds(pl.multiple_of((head // 2) * LANES, LANES), LANES)

    def low_high(rows):
        turned = pltpu.roll(rows, HEAD_DIM, 1)
        return jnp.where(odd, turned, rows), jnp.where(odd, rows, turned)

    key_low, key_high = low_high(text_key_ref[0, :, lanes].astype(jnp.float32))
    value_low, _ = low_high(text_value_ref[0, :, lanes].astype(jnp.float32))
    mask_row = jnp.zeros((1, LANES), jnp.float32)
    whole = mask_ref[...].astype(jnp.float32).reshape(1, cols)
    for tile in range(cols // LANES):
        mask_row = jnp.where(head // 2 == tile, whole[:, tile * LANES : (tile + 1) * LANES], mask_row)
    mask_row, _ = low_high(jnp.broadcast_to(mask_row, (8, LANES)))
    steps = jnp.full((8, LANES), steps_ref[0], jnp.int32).astype(jnp.float32)
    weight_ref[...] = 1.0 / (0.1 + steps / 999.0)
    wide_gain_ref[...] = jnp.broadcast_to(gain_ref[...].astype(jnp.float32).reshape(1, cols), (8, cols))
    low = lane_of(tokens) < HEAD_DIM
    fill_ref[...] = jnp.where(lane_of(8) < HEAD_DIM, mask_row, 1.0)
    ek_ref[0:tokens, :] = jnp.where(low, value_low, key_high).astype(jnp.bfloat16)
    ev_ref[0:tokens, :] = jnp.where(low, value_low, 1.0).astype(jnp.bfloat16)
    dk_ref[0:tokens, :] = key_low.astype(jnp.bfloat16)
    for block in range(chips):
        got = own_ref.at[block]
        unpack(slots, tokens, got, block, tokens, tokens, ek_ref, ev_ref, eq_ref, dk_ref)
        tail = got[2 * slots : slots + tokens, :].astype(jnp.float32)
        last = got[slots + tokens : slots + tokens + rest, :].astype(jnp.float32)
        base = block * tokens
        dq_ref[base : base + spare, :] = jnp.where(
            lane_of(spare) < HEAD_DIM, pltpu.roll(tail, HEAD_DIM, 1), 0.0
        ).astype(jnp.bfloat16)
        low_rest = lane_of(rest) < HEAD_DIM
        dq_ref[base + spare : base + spare + rest, :] = jnp.where(low_rest, last, 0.0).astype(jnp.bfloat16)
        dq_ref[base + spare + rest : base + tokens, :] = jnp.where(
            low_rest, pltpu.roll(last, HEAD_DIM, 1), 0.0
        ).astype(jnp.bfloat16)

    rows = chips // 2 * slots

    def job(tile):
        span = slice(tile * rows, (tile + 1) * rows)

        def use(top, sums):
            sums_ref[span, :] = sums
            top_ref[span, :] = jnp.broadcast_to(top, (rows, LANES))

        return (lambda: eq_ref[span, :], [ek_ref], [ev_ref], None, use)

    run_jobs([job(tile) for tile in range(2)], (places[0:2], places[2:4]))


def attend_kernel(
    slots,
    tokens,
    pair_ref,
    ek_ref,
    ev_ref,
    eq_ref,
    dk_ref,
    dq_ref,
    sums_ref,
    top_ref,
    fill_ref,
    out_ref,
    pair_ek_ref,
    pair_ev_ref,
    pair_eq_ref,
    pair_dk_ref,
    dv_ref,
    *places
):
    chips = pair_ref.shape[0]
    spare = tokens - slots
    for block in range(chips):
        unpack(
            slots, tokens, pair_ref.at[block], block, 0, 0, pair_ek_ref, pair_ev_ref, pair_eq_ref, pair_dk_ref
        )
    dv_ref[0:tokens, :] = ev_ref[0:tokens, :]
    mask_row = fill_ref[0:1, :]
    fill = jnp.broadcast_to(mask_row, (spare, LANES)).astype(jnp.bfloat16)
    group = chips // 2
    rows = group * slots

    def encode(tile, query_ref, first_block, key_refs, value_refs, earlier):
        span = slice(tile * rows, (tile + 1) * rows)

        def use(top, sums):
            found = sums / pltpu.roll(sums, HEAD_DIM, 1)
            for inner in range(group):
                mixed = query_ref[tile * rows + inner * slots : tile * rows + (inner + 1) * slots, :]
                live = pltpu.roll(mixed.astype(jnp.float32), HEAD_DIM, 1) < DEAD_EDGE
                base = tokens + (first_block + tile * group + inner) * tokens
                dv_ref[base : base + slots, :] = jnp.where(
                    (lane_of(slots) < HEAD_DIM) & live, found[inner * slots : (inner + 1) * slots, :], mask_row
                ).astype(jnp.bfloat16)
                dv_ref[base + slots : base + tokens, :] = fill

        before = (lambda: (sums_ref[span, :], top_ref[span, :])) if earlier else None
        return (lambda: query_ref[span, :], key_refs, value_refs, before, use)

    dec_group = 2
    dec_rows = dec_group * tokens
    half = tokens // 2

    def decode(tile):
        def use(top, sums):
            found = sums / pltpu.roll(sums, HEAD_DIM, 1)
            for inner in range(dec_group):
                first = inner * tokens
                out_ref[tile * dec_group + inner] = jnp.where(
                    lane_of(half) < HEAD_DIM,
                    found[first : first + half],
                    pltpu.roll(found[first + half : first + tokens], HEAD_DIM, 1),
                ).astype(jnp.bfloat16)

        span = slice(tile * dec_rows, (tile + 1) * dec_rows)
        return (lambda: dq_ref[span, :], [dk_ref, pair_dk_ref], [dv_ref], None, use)

    jobs = [encode(tile, eq_ref, 0, [pair_ek_ref], [pair_ev_ref], True) for tile in range(2)]
    jobs += [
        encode(tile, pair_eq_ref, chips, [ek_ref, pair_ek_ref], [ev_ref, pair_ev_ref], False) for tile in range(2)
    ]
    jobs += [decode(tile) for tile in range(chips // dec_group)]
    run_jobs(jobs, (places[0:2], places[2:4]))


def sums_kernel(got_ref, gain_ref, target_ref, weight_ref, att_ref, sums_ref):
    tokens, cols = att_ref.shape
    half = tokens // 2
    low = lax.broadcasted_iota(jnp.int32, (half, LANES), 1) < HEAD_DIM
    for tile in range(cols // LANES):
        even = got_ref[2 * tile].astype(jnp.float32)
        odd = got_ref[2 * tile + 1].astype(jnp.float32)
        span = slice(tile * LANES, (tile + 1) * LANES)
        att_ref[0:half, span] = jnp.where(low, even, pltpu.roll(odd, HEAD_DIM, 1))
        att_ref[half:tokens, span] = jnp.where(low, pltpu.roll(even, HEAD_DIM, 1), odd)
    att = att_ref[...]
    gained = att * gain_ref[0:1, :]
    target = target_ref[0].astype(jnp.float32)
    weight = weight_ref[0:1, :]
    lane = lax.broadcasted_iota(jnp.int32, (tokens, LANES), 1)

    def over(block):
        return jnp.sum(block, axis=1, keepdims=True)

    table = jnp.where(
        lane == 1,
        over(gained * gained),
        jnp.where(lane == 2, over(gained * target), over(target * target)),
    )
    table = jnp.where(lane == 0, over(att * att), table * weight)
    sums_ref[...] = jnp.broadcast_to(jnp.transpose(table)[None, 0:4, :], sums_ref.shape)


def loss_kernel(heads, total_cols, sums_ref, loss_ref):
    total = None
    for image in range(sums_ref.shape[0] // heads):
        sums = jnp.sum(sums_ref[image * heads : (image + 1) * heads], axis=0)
        factor = lax.rsqrt(sums[0:1, :] / total_cols + 1e-06)
        error = factor * factor * sums[1:2, :] - 2.0 * factor * sums[2:3, :] + sums[3:4, :]
        total = error if total is None else total + error
    loss_ref[...] = jnp.broadcast_to(jnp.sum(total, axis=1, keepdims=True)[None], loss_ref.shape)


def finish_kernel(heads, count, att_ref, gain_ref, sums_ref, got_ref, out_ref, loss_ref):
    tokens, cols = att_ref.shape
    loss_ref[...] = (jnp.sum(got_ref[...], axis=0) / count)[0:1, 0:1]
    own = jnp.sum(sums_ref[pl.ds(lax.axis_index("dp") * heads, heads)], axis=0)
    factor = lax.rsqrt(own[0:1, :] / (cols * heads) + 1e-06)
    column = jnp.transpose(jnp.broadcast_to(factor, (tokens, tokens)))[:, 0:1]
    out_ref[0] = (att_ref[...] * column * gain_ref[0:1, :]).astype(jnp.bfloat16)


def local(
    enc_query,
    enc_key,
    enc_value,
    keep_index,
    keep_count,
    text_key,
    text_value,
    dec_query,
    dec_key,
    mask_value,
    norm_gain,
    target,
    timesteps,
):
    images, seq, heads = (lax.axis_size(name) for name in ("dp", "seq", "head"))
    tokens, cols = enc_query.shape[1:]
    slots = keep_index.shape[1]
    local_heads = cols // HEAD_DIM
    chips = seq // 2
    packed = slots + tokens + slots // 2
    same_core = [[2 * chip + core for chip in range(chips)] for core in range(2)]
    bf16, f32 = jnp.bfloat16, jnp.float32

    send = pl.pallas_call(
        pack_kernel,
        out_shape=jax.ShapeDtypeStruct((chips, packed, LANES), bf16),
        in_specs=[pl.BlockSpec(memory_space=pltpu.HBM)] * 6,
        out_specs=vmem(1)[0],
        scratch_shapes=[pltpu.VMEM((1, slots), jnp.int32)]
        + [pltpu.VMEM((1, tokens, cols), bf16)] * 5
        + [pltpu.SemaphoreType.DMA((6,))],
        compiler_params=params(60),
        name="pack",
    )(keep_index, enc_query, enc_key, enc_value, dec_query, dec_key)
    own = lax.all_to_all(send, "seq", 0, 0, axis_index_groups=same_core, tiled=True)
    pair = lax.ppermute(own, "seq", [(source, source ^ 1) for source in range(seq)])
    kept_own = chips * slots
    dec_own = chips * tokens
    *begun, weight, gain = pl.pallas_call(
        functools.partial(begin_kernel, slots, tokens),
        out_shape=(
            jax.ShapeDtypeStruct((tokens + kept_own, LANES), bf16),
            jax.ShapeDtypeStruct((tokens + kept_own, LANES), bf16),
            jax.ShapeDtypeStruct((kept_own, LANES), bf16),
            jax.ShapeDtypeStruct((tokens + dec_own, LANES), bf16),
            jax.ShapeDtypeStruct((dec_own, LANES), bf16),
            jax.ShapeDtypeStruct((kept_own, LANES), f32),
            jax.ShapeDtypeStruct((kept_own, LANES), f32),
            jax.ShapeDtypeStruct((8, LANES), f32),
            jax.ShapeDtypeStruct((8, LANES), f32),
            jax.ShapeDtypeStruct((8, cols), f32),
        ),
        in_specs=vmem(5) + [pl.BlockSpec(memory_space=pltpu.SMEM)],
        out_specs=tuple(vmem(10)),
        scratch_shapes=[
            pltpu.VMEM((kept_own // 2, tokens + kept_own), f32),
            pltpu.VMEM((kept_own // 2, LANES), f32),
        ]
        * 2,
        compiler_params=params(),
        cost_estimate=pl.CostEstimate(
            flops=4 * kept_own * (tokens + kept_own) * LANES,
            bytes_accessed=8 * MIB,
            transcendentals=kept_own * (tokens + kept_own),
        ),
        name="begin",
    )(own, text_key, text_value, mask_value, norm_gain, timesteps)
    out = pl.pallas_call(
        functools.partial(attend_kernel, slots, tokens),
        out_shape=jax.ShapeDtypeStruct((chips, tokens // 2, LANES), bf16),
        in_specs=vmem(9),
        out_specs=vmem(1)[0],
        scratch_shapes=[
            pltpu.VMEM((kept_own, LANES), bf16),
            pltpu.VMEM((kept_own, LANES), bf16),
            pltpu.VMEM((kept_own, LANES), bf16),
            pltpu.VMEM((dec_own, LANES), bf16),
            pltpu.VMEM((tokens + 2 * dec_own, LANES), bf16),
        ]
        + [
            pltpu.VMEM((kept_own // 2, tokens + 2 * dec_own), f32),
            pltpu.VMEM((kept_own // 2, LANES), f32),
        ]
        * 2,
        compiler_params=params(),
        name="attend",
    )(pair, *begun)
    got = lax.all_to_all(out, "seq", 0, 0, axis_index_groups=same_core, tiled=True)
    att, sums = pl.pallas_call(
        sums_kernel,
        out_shape=(
            jax.ShapeDtypeStruct((tokens, cols), f32),
            jax.ShapeDtypeStruct((images * heads, 4, tokens), f32),
        ),
        in_specs=vmem(4),
        out_specs=tuple(vmem(2)),
        compiler_params=params(),
        name="sums",
    )(got, gain, target, weight)
    sums = lax.all_to_all(sums, ("dp", "head"), 0, 0, tiled=True)
    loss = pl.pallas_call(
        functools.partial(loss_kernel, heads, cols * heads),
        out_shape=jax.ShapeDtypeStruct((seq, 1, LANES), f32),
        in_specs=vmem(1),
        out_specs=vmem(1)[0],
        compiler_params=params(),
        name="loss",
    )(sums)
    got = lax.all_to_all(loss, "seq", 0, 0, tiled=True)
    decoded, loss = pl.pallas_call(
        functools.partial(finish_kernel, heads, float(images * tokens * seq * cols * heads)),
        out_shape=(
            jax.ShapeDtypeStruct((1, tokens, cols), bf16),
            jax.ShapeDtypeStruct((1, 1), f32),
        ),
        in_specs=vmem(4),
        out_specs=tuple(vmem(2)),
        compiler_params=params(),
        name="finish",
    )(att, gain, sums, got)
    total_loss = loss.reshape(())
    return (decoded, total_loss)


def solution(mesh):
    placed = (
        P("dp", "seq", "head"),
        P("dp", "seq", "head"),
        P("dp", "seq", "head"),
        P("dp", "seq"),
        P("dp", "seq"),
        P("dp", None, "head"),
        P("dp", None, "head"),
        P("dp", "seq", "head"),
        P("dp", "seq", "head"),
        P("head"),
        P("head"),
        P("dp", "seq", "head"),
        P("dp"),
    )
    return jax.shard_map(
        local, mesh=mesh, in_specs=placed, out_specs=(P("dp", "seq", "head"), P()), check_vma=False
    )
```

```python
import functools

import jax
import jax.numpy as jnp
from jax import lax
from jax.experimental import pallas as pl
from jax.experimental.pallas import tpu as pltpu
from jax.sharding import PartitionSpec as P

HEAD_DIM = 64
LANES = 128
DEAD = 1024.0
DEAD_EDGE = 512.0
MIB = 1024 * 1024


def params(mib=40):
    return pltpu.CompilerParams(vmem_limit_bytes=mib * MIB)


def vmem(count):
    return [pl.BlockSpec(memory_space=pltpu.VMEM)] * count


def one_hot_dot(table, rows):
    return lax.dot_general(
        table, rows, (((1,), (0,)), ((), ())), preferred_element_type=jnp.float32
    )


def pack_kernel(
    index_hbm, eq_hbm, ek_hbm, ev_hbm, dq_hbm, dk_hbm, send_ref, *scratch
):
    *held, sems = scratch
    given = (index_hbm, eq_hbm, ek_hbm, ev_hbm, dq_hbm, dk_hbm)
    copies = [
        pltpu.make_async_copy(source, place, sems.at[number])
        for number, (source, place) in enumerate(zip(given, held))
    ]
    for copy in copies:
        copy.start()
    copies[0].wait()
    index_ref, eq_ref, ek_ref, ev_ref, dq_ref, dk_ref = held
    tokens, cols = eq_ref.shape[1:]
    slots = index_ref.shape[1]
    heads = cols // HEAD_DIM
    spare = tokens - slots
    index = jnp.broadcast_to(index_ref[...].astype(jnp.float32), (tokens, slots))
    index = jnp.transpose(index)
    token = lax.broadcasted_iota(jnp.int32, (slots, tokens), 1).astype(jnp.float32)
    slot = lax.broadcasted_iota(jnp.int32, (slots, tokens), 0)
    live = (slot == 0) | (index > 0.5)
    match_live = jnp.where(live & (token == index), 1.0, 0.0)
    match_fill = jnp.where(token == jnp.where(live, index, index[0:1, :]), 1.0, 0.0)
    kept = jnp.sum(match_live, axis=0, keepdims=True)
    kept_slot = jnp.sum(match_live * slot.astype(jnp.float32), axis=0, keepdims=True)
    row = lax.broadcasted_iota(jnp.int32, (tokens, tokens), 0)
    col = lax.broadcasted_iota(jnp.int32, (tokens, tokens), 1)
    before = jnp.where(row < col, 1.0, 0.0).astype(jnp.bfloat16)
    left = jnp.broadcast_to(1.0 - kept, (16, tokens)).astype(jnp.bfloat16)
    rank = one_hot_dot(left, before)[0:1, :]
    place = jnp.where(kept > 0.5, kept_slot, jnp.sum(kept, axis=1, keepdims=True) + rank)
    order = jnp.where(row.astype(jnp.float32) == place, 1.0, 0.0).astype(jnp.bfloat16)

    for copy in copies[1:]:
        copy.wait()
    scale = HEAD_DIM ** (-0.5)
    match_live = match_live.astype(jnp.bfloat16)
    match_fill = match_fill.astype(jnp.bfloat16)
    query = one_hot_dot(match_live, eq_ref[0]) * scale
    dead = jnp.where(live, 0.0, DEAD)
    query = query + jnp.concatenate([dead] * (cols // tokens), axis=1)
    key = one_hot_dot(match_fill, ek_ref[0])
    value = one_hot_dot(match_live, ev_ref[0])
    dec_key = one_hot_dot(order, dk_ref[0])
    dec_query = dq_ref[0].astype(jnp.float32) * scale

    def low(block, head):
        tile = block[:, (head // 2) * LANES : (head // 2 + 1) * LANES]
        return tile if head % 2 == 0 else pltpu.roll(tile, HEAD_DIM, 1)

    def high(block, head):
        tile = block[:, (head // 2) * LANES : (head // 2 + 1) * LANES]
        return tile if head % 2 == 1 else pltpu.roll(tile, HEAD_DIM, 1)

    def join(first, second):
        lane = lax.broadcasted_iota(jnp.int32, first.shape, 1)
        return jnp.where(lane < HEAD_DIM, first, second).astype(jnp.bfloat16)

    for head in range(heads):
        kept_tile = join(low(value, head), high(key, head))
        query_high = high(query, head)
        dec_low = low(dec_key, head)
        dq_low = low(dec_query, head)
        dq_high = high(dec_query, head)
        send_ref[head, 0:slots, :] = kept_tile
        send_ref[head, slots : 2 * slots, :] = join(dec_low[0:slots], query_high)
        send_ref[head, 2 * slots : slots + tokens, :] = join(dec_low[slots:tokens], dq_high[0:spare])
        rest = slots // 2
        send_ref[head, slots + tokens : slots + tokens + rest, :] = join(
            dq_low[spare : spare + rest], dq_high[spare + rest : tokens]
        )


def put_scores(query, key_refs, place, peak):
    rows = query.shape[0]
    largest = None
    column = 0
    for key_ref in key_refs:
        keys = key_ref.shape[0]
        for first in range(0, keys, 2 * LANES):
            last = min(keys, first + 2 * LANES)
            part = lax.dot_general(
                query, key_ref[first:last, :], (((1,), (1,)), ((), ())), preferred_element_type=jnp.float32
            )
            place[0:rows, column : column + last - first] = part
            column += last - first
            for lane in range(0, last - first, LANES):
                tile = part[:, lane : lane + LANES]
                largest = tile if largest is None else jnp.maximum(largest, tile)
    peak[0:rows, :] = largest


def weigh(rows, place, peak, value_refs, earlier):
    top = jnp.max(peak[0:rows, :], axis=1, keepdims=True)
    sums = None
    if earlier is not None:
        earlier_sums, earlier_top = earlier
        top = jnp.maximum(top, earlier_top[:, 0:1])
        sums = earlier_sums * jnp.exp(earlier_top - top)
    column = 0
    for value_ref in value_refs:
        keys = value_ref.shape[0]
        weights = jnp.exp(place[0:rows, column : column + keys] - top).astype(jnp.bfloat16)
        column += keys
        part = lax.dot_general(
            weights, value_ref[...], (((1,), (0,)), ((), ())), preferred_element_type=jnp.float32
        )
        sums = part if sums is None else sums + part
    return top, sums


def run_jobs(jobs, buffers):
    def put(number):
        query, key_refs, _, _, _ = jobs[number]
        put_scores(query(), key_refs, *buffers[number % 2])

    put(0)
    for number, (query, _, value_refs, earlier, use) in enumerate(jobs):
        if number + 1 < len(jobs):
            put(number + 1)
        place, peak = buffers[number % 2]
        rows = query().shape[0]
        use(*weigh(rows, place, peak, value_refs, None if earlier is None else earlier()))


def lane_of(rows):
    return lax.broadcasted_iota(jnp.int32, (rows, LANES), 1)


def unpack(slots, tokens, got, block, first_key, first_dec, ek_ref, ev_ref, eq_ref, dk_ref):
    kept = got[0:slots, :]
    mixed = got[slots : 2 * slots, :].astype(jnp.float32)
    low = lane_of(slots) < HEAD_DIM
    base = first_key + block * slots
    ek_ref[base : base + slots, :] = kept
    ev_ref[base : base + slots, :] = jnp.where(
        low, kept.astype(jnp.float32), jnp.where(mixed < DEAD_EDGE, 1.0, 0.0)
    ).astype(jnp.bfloat16)
    eq_ref[block * slots : block * slots + slots, :] = jnp.where(low, 0.0, mixed).astype(jnp.bfloat16)
    base = first_dec + block * tokens
    dk_ref[base : base + tokens, :] = got[slots : slots + tokens, :]


def begin_kernel(
    slots,
    tokens,
    own_ref,
    text_key_ref,
    text_value_ref,
    mask_ref,
    gain_ref,
    steps_ref,
    ek_ref,
    ev_ref,
    eq_ref,
    dk_ref,
    dq_ref,
    sums_ref,
    top_ref,
    fill_ref,
    weight_ref,
    wide_gain_ref,
    *places
):
    chips = own_ref.shape[0]
    cols = text_key_ref.shape[2]
    spare = tokens - slots
    rest = slots // 2
    head = jnp.minimum(lax.axis_index("seq") // 2, cols // HEAD_DIM - 1)
    odd = lax.rem(head, 2) == 1
    lanes = pl.ds(pl.multiple_of((head // 2) * LANES, LANES), LANES)

    def low_high(rows):
        turned = pltpu.roll(rows, HEAD_DIM, 1)
        return jnp.where(odd, turned, rows), jnp.where(odd, rows, turned)

    key_low, key_high = low_high(text_key_ref[0, :, lanes].astype(jnp.float32))
    value_low, _ = low_high(text_value_ref[0, :, lanes].astype(jnp.float32))
    mask_row = jnp.zeros((1, LANES), jnp.float32)
    whole = mask_ref[...].astype(jnp.float32).reshape(1, cols)
    for tile in range(cols // LANES):
        mask_row = jnp.where(head // 2 == tile, whole[:, tile * LANES : (tile + 1) * LANES], mask_row)
    mask_row, _ = low_high(jnp.broadcast_to(mask_row, (8, LANES)))
    steps = jnp.full((8, LANES), steps_ref[0], jnp.int32).astype(jnp.float32)
    weight_ref[...] = 1.0 / (0.1 + steps / 999.0)
    wide_gain_ref[...] = jnp.broadcast_to(gain_ref[...].astype(jnp.float32).reshape(1, cols), (8, cols))
    low = lane_of(tokens) < HEAD_DIM
    fill_ref[...] = jnp.where(lane_of(8) < HEAD_DIM, mask_row, 1.0)
    ek_ref[0:tokens, :] = jnp.where(low, value_low, key_high).astype(jnp.bfloat16)
    ev_ref[0:tokens, :] = jnp.where(low, value_low, 1.0).astype(jnp.bfloat16)
    dk_ref[0:tokens, :] = key_low.astype(jnp.bfloat16)
    for block in range(chips):
        got = own_ref.at[block]
        unpack(slots, tokens, got, block, tokens, tokens, ek_ref, ev_ref, eq_ref, dk_ref)
        tail = got[2 * slots : slots + tokens, :].astype(jnp.float32)
        last = got[slots + tokens : slots + tokens + rest, :].astype(jnp.float32)
        base = block * tokens
        dq_ref[base : base + spare, :] = jnp.where(
            lane_of(spare) < HEAD_DIM, pltpu.roll(tail, HEAD_DIM, 1), 0.0
        ).astype(jnp.bfloat16)
        low_rest = lane_of(rest) < HEAD_DIM
        dq_ref[base + spare : base + spare + rest, :] = jnp.where(low_rest, last, 0.0).astype(jnp.bfloat16)
        dq_ref[base + spare + rest : base + tokens, :] = jnp.where(
            low_rest, pltpu.roll(last, HEAD_DIM, 1), 0.0
        ).astype(jnp.bfloat16)

    rows = chips // 2 * slots

    def job(tile):
        span = slice(tile * rows, (tile + 1) * rows)

        def use(top, sums):
            sums_ref[span, :] = sums
            top_ref[span, :] = jnp.broadcast_to(top, (rows, LANES))

        return (lambda: eq_ref[span, :], [ek_ref], [ev_ref], None, use)

    run_jobs([job(tile) for tile in range(2)], (places[0:2], places[2:4]))


def attend_kernel(
    slots,
    tokens,
    pair_ref,
    ek_ref,
    ev_ref,
    eq_ref,
    dk_ref,
    dq_ref,
    sums_ref,
    top_ref,
    fill_ref,
    out_ref,
    pair_ek_ref,
    pair_ev_ref,
    pair_eq_ref,
    pair_dk_ref,
    dv_ref,
    *places
):
    chips = pair_ref.shape[0]
    spare = tokens - slots
    for block in range(chips):
        unpack(
            slots, tokens, pair_ref.at[block], block, 0, 0, pair_ek_ref, pair_ev_ref, pair_eq_ref, pair_dk_ref
        )
    dv_ref[0:tokens, :] = ev_ref[0:tokens, :]
    mask_row = fill_ref[0:1, :]
    fill = jnp.broadcast_to(mask_row, (spare, LANES)).astype(jnp.bfloat16)
    group = chips // 2
    rows = group * slots

    def encode(tile, query_ref, first_block, key_refs, value_refs, earlier):
        span = slice(tile * rows, (tile + 1) * rows)

        def use(top, sums):
            found = sums / pltpu.roll(sums, HEAD_DIM, 1)
            for inner in range(group):
                mixed = query_ref[tile * rows + inner * slots : tile * rows + (inner + 1) * slots, :]
                live = pltpu.roll(mixed.astype(jnp.float32), HEAD_DIM, 1) < DEAD_EDGE
                base = tokens + (first_block + tile * group + inner) * tokens
                dv_ref[base : base + slots, :] = jnp.where(
                    (lane_of(slots) < HEAD_DIM) & live, found[inner * slots : (inner + 1) * slots, :], mask_row
                ).astype(jnp.bfloat16)
                dv_ref[base + slots : base + tokens, :] = fill

        before = (lambda: (sums_ref[span, :], top_ref[span, :])) if earlier else None
        return (lambda: query_ref[span, :], key_refs, value_refs, before, use)

    dec_group = 2
    dec_rows = dec_group * tokens
    half = tokens // 2

    def decode(tile):
        def use(top, sums):
            found = sums / pltpu.roll(sums, HEAD_DIM, 1)
            for inner in range(dec_group):
                first = inner * tokens
                out_ref[tile * dec_group + inner] = jnp.where(
                    lane_of(half) < HEAD_DIM,
                    found[first : first + half],
                    pltpu.roll(found[first + half : first + tokens], HEAD_DIM, 1),
                ).astype(jnp.bfloat16)

        span = slice(tile * dec_rows, (tile + 1) * dec_rows)
        return (lambda: dq_ref[span, :], [dk_ref, pair_dk_ref], [dv_ref], None, use)

    jobs = [encode(tile, eq_ref, 0, [pair_ek_ref], [pair_ev_ref], True) for tile in range(2)]
    jobs += [
        encode(tile, pair_eq_ref, chips, [ek_ref, pair_ek_ref], [ev_ref, pair_ev_ref], False) for tile in range(2)
    ]
    jobs += [decode(tile) for tile in range(chips // dec_group)]
    run_jobs(jobs, (places[0:2], places[2:4]))


def sums_kernel(got_ref, gain_ref, target_ref, weight_ref, att_ref, sums_ref):
    tokens, cols = att_ref.shape
    half = tokens // 2
    low = lax.broadcasted_iota(jnp.int32, (half, LANES), 1) < HEAD_DIM
    for tile in range(cols // LANES):
        even = got_ref[2 * tile].astype(jnp.float32)
        odd = got_ref[2 * tile + 1].astype(jnp.float32)
        span = slice(tile * LANES, (tile + 1) * LANES)
        att_ref[0:half, span] = jnp.where(low, even, pltpu.roll(odd, HEAD_DIM, 1))
        att_ref[half:tokens, span] = jnp.where(low, pltpu.roll(even, HEAD_DIM, 1), odd)
    att = att_ref[...]
    gained = att * gain_ref[0:1, :]
    target = target_ref[0].astype(jnp.float32)
    weight = weight_ref[0:1, :]
    lane = lax.broadcasted_iota(jnp.int32, (tokens, LANES), 1)

    def over(block):
        return jnp.sum(block, axis=1, keepdims=True)

    table = jnp.where(
        lane == 1,
        over(gained * gained),
        jnp.where(lane == 2, over(gained * target), over(target * target)),
    )
    table = jnp.where(lane == 0, over(att * att), table * weight)
    sums_ref[...] = jnp.broadcast_to(jnp.transpose(table)[None, 0:4, :], sums_ref.shape)


def loss_kernel(heads, total_cols, sums_ref, loss_ref):
    total = None
    for image in range(sums_ref.shape[0] // heads):
        sums = jnp.sum(sums_ref[image * heads : (image + 1) * heads], axis=0)
        factor = lax.rsqrt(sums[0:1, :] / total_cols + 1e-06)
        error = factor * factor * sums[1:2, :] - 2.0 * factor * sums[2:3, :] + sums[3:4, :]
        total = error if total is None else total + error
    loss_ref[...] = jnp.broadcast_to(jnp.sum(total, axis=1, keepdims=True)[None], loss_ref.shape)


def finish_kernel(heads, count, att_ref, gain_ref, sums_ref, got_ref, out_ref, loss_ref):
    tokens, cols = att_ref.shape
    loss_ref[...] = (jnp.sum(got_ref[...], axis=0) / count)[0:1, 0:1]
    own = jnp.sum(sums_ref[pl.ds(lax.axis_index("dp") * heads, heads)], axis=0)
    factor = lax.rsqrt(own[0:1, :] / (cols * heads) + 1e-06)
    column = jnp.transpose(jnp.broadcast_to(factor, (tokens, tokens)))[:, 0:1]
    out_ref[0] = (att_ref[...] * column * gain_ref[0:1, :]).astype(jnp.bfloat16)


def local(
    enc_query,
    enc_key,
    enc_value,
    keep_index,
    keep_count,
    text_key,
    text_value,
    dec_query,
    dec_key,
    mask_value,
    norm_gain,
    target,
    timesteps,
):
    images, seq, heads = (lax.axis_size(name) for name in ("dp", "seq", "head"))
    tokens, cols = enc_query.shape[1:]
    slots = keep_index.shape[1]
    local_heads = cols // HEAD_DIM
    chips = seq // 2
    packed = slots + tokens + slots // 2
    rings = [[2 * chip + (chip + ring) % 2 for chip in range(chips)] for ring in range(2)]
    bf16, f32 = jnp.bfloat16, jnp.float32

    send = pl.pallas_call(
        pack_kernel,
        out_shape=jax.ShapeDtypeStruct((chips, packed, LANES), bf16),
        in_specs=[pl.BlockSpec(memory_space=pltpu.HBM)] * 6,
        out_specs=vmem(1)[0],
        scratch_shapes=[pltpu.VMEM((1, slots), jnp.int32)]
        + [pltpu.VMEM((1, tokens, cols), bf16)] * 5
        + [pltpu.SemaphoreType.DMA((6,))],
        compiler_params=params(60),
        name="pack",
    )(keep_index, enc_query, enc_key, enc_value, dec_query, dec_key)
    own = lax.all_to_all(send, "seq", 0, 0, axis_index_groups=rings, tiled=True)
    pair = lax.ppermute(own, "seq", [(source, source ^ 1) for source in range(seq)])
    kept_own = chips * slots
    dec_own = chips * tokens
    *begun, weight, gain = pl.pallas_call(
        functools.partial(begin_kernel, slots, tokens),
        out_shape=(
            jax.ShapeDtypeStruct((tokens + kept_own, LANES), bf16),
            jax.ShapeDtypeStruct((tokens + kept_own, LANES), bf16),
            jax.ShapeDtypeStruct((kept_own, LANES), bf16),
            jax.ShapeDtypeStruct((tokens + dec_own, LANES), bf16),
            jax.ShapeDtypeStruct((dec_own, LANES), bf16),
            jax.ShapeDtypeStruct((kept_own, LANES), f32),
            jax.ShapeDtypeStruct((kept_own, LANES), f32),
            jax.ShapeDtypeStruct((8, LANES), f32),
            jax.ShapeDtypeStruct((8, LANES), f32),
            jax.ShapeDtypeStruct((8, cols), f32),
        ),
        in_specs=vmem(5) + [pl.BlockSpec(memory_space=pltpu.SMEM)],
        out_specs=tuple(vmem(10)),
        scratch_shapes=[
            pltpu.VMEM((kept_own // 2, tokens + kept_own), f32),
            pltpu.VMEM((kept_own // 2, LANES), f32),
        ]
        * 2,
        compiler_params=params(),
        cost_estimate=pl.CostEstimate(
            flops=4 * kept_own * (tokens + kept_own) * LANES,
            bytes_accessed=8 * MIB,
            transcendentals=kept_own * (tokens + kept_own),
        ),
        name="begin",
    )(own, text_key, text_value, mask_value, norm_gain, timesteps)
    out = pl.pallas_call(
        functools.partial(attend_kernel, slots, tokens),
        out_shape=jax.ShapeDtypeStruct((chips, tokens // 2, LANES), bf16),
        in_specs=vmem(9),
        out_specs=vmem(1)[0],
        scratch_shapes=[
            pltpu.VMEM((kept_own, LANES), bf16),
            pltpu.VMEM((kept_own, LANES), bf16),
            pltpu.VMEM((kept_own, LANES), bf16),
            pltpu.VMEM((dec_own, LANES), bf16),
            pltpu.VMEM((tokens + 2 * dec_own, LANES), bf16),
        ]
        + [
            pltpu.VMEM((kept_own // 2, tokens + 2 * dec_own), f32),
            pltpu.VMEM((kept_own // 2, LANES), f32),
        ]
        * 2,
        compiler_params=params(),
        name="attend",
    )(pair, *begun)
    got = lax.all_to_all(out, "seq", 0, 0, axis_index_groups=rings, tiled=True)
    att, sums = pl.pallas_call(
        sums_kernel,
        out_shape=(
            jax.ShapeDtypeStruct((tokens, cols), f32),
            jax.ShapeDtypeStruct((images * heads, 4, tokens), f32),
        ),
        in_specs=vmem(4),
        out_specs=tuple(vmem(2)),
        compiler_params=params(),
        name="sums",
    )(got, gain, target, weight)
    sums = lax.all_to_all(sums, ("dp", "head"), 0, 0, tiled=True)
    loss = pl.pallas_call(
        functools.partial(loss_kernel, heads, cols * heads),
        out_shape=jax.ShapeDtypeStruct((seq, 1, LANES), f32),
        in_specs=vmem(1),
        out_specs=vmem(1)[0],
        compiler_params=params(),
        name="loss",
    )(sums)
    got = lax.all_to_all(loss, "seq", 0, 0, tiled=True)
    decoded, loss = pl.pallas_call(
        functools.partial(finish_kernel, heads, float(images * tokens * seq * cols * heads)),
        out_shape=(
            jax.ShapeDtypeStruct((1, tokens, cols), bf16),
            jax.ShapeDtypeStruct((1, 1), f32),
        ),
        in_specs=vmem(4),
        out_specs=tuple(vmem(2)),
        compiler_params=params(),
        name="finish",
    )(att, gain, sums, got)
    total_loss = loss.reshape(())
    return (decoded, total_loss)


def solution(mesh):
    placed = (
        P("dp", "seq", "head"),
        P("dp", "seq", "head"),
        P("dp", "seq", "head"),
        P("dp", "seq"),
        P("dp", "seq"),
        P("dp", None, "head"),
        P("dp", None, "head"),
        P("dp", "seq", "head"),
        P("dp", "seq", "head"),
        P("head"),
        P("head"),
        P("dp", "seq", "head"),
        P("dp"),
    )
    return jax.shard_map(
        local, mesh=mesh, in_specs=placed, out_specs=(P("dp", "seq", "head"), P()), check_vma=False
    )
```

```python
import functools

import jax
import jax.numpy as jnp
from jax import lax
from jax.experimental import pallas as pl
from jax.experimental.pallas import tpu as pltpu
from jax.sharding import PartitionSpec as P

HEAD_DIM = 64
LANES = 128
DEAD = 1024.0
DEAD_EDGE = 512.0
MIB = 1024 * 1024


def params(mib=40):
    return pltpu.CompilerParams(vmem_limit_bytes=mib * MIB)


def vmem(count):
    return [pl.BlockSpec(memory_space=pltpu.VMEM)] * count


def one_hot_dot(table, rows):
    return lax.dot_general(
        table, rows, (((1,), (0,)), ((), ())), preferred_element_type=jnp.float32
    )


def pack_kernel(
    index_hbm, eq_hbm, ek_hbm, ev_hbm, dq_hbm, dk_hbm, send_ref, *scratch
):
    *held, sems = scratch
    given = (index_hbm, eq_hbm, ek_hbm, ev_hbm, dq_hbm, dk_hbm)
    copies = [
        pltpu.make_async_copy(source, place, sems.at[number])
        for number, (source, place) in enumerate(zip(given, held))
    ]
    for copy in copies:
        copy.start()
    copies[0].wait()
    index_ref, eq_ref, ek_ref, ev_ref, dq_ref, dk_ref = held
    tokens, cols = eq_ref.shape[1:]
    slots = index_ref.shape[1]
    heads = cols // HEAD_DIM
    spare = tokens - slots
    index = jnp.broadcast_to(index_ref[...].astype(jnp.float32), (tokens, slots))
    index = jnp.transpose(index)
    token = lax.broadcasted_iota(jnp.int32, (slots, tokens), 1).astype(jnp.float32)
    slot = lax.broadcasted_iota(jnp.int32, (slots, tokens), 0)
    live = (slot == 0) | (index > 0.5)
    match_live = jnp.where(live & (token == index), 1.0, 0.0)
    match_fill = jnp.where(token == jnp.where(live, index, index[0:1, :]), 1.0, 0.0)
    kept = jnp.sum(match_live, axis=0, keepdims=True)
    kept_slot = jnp.sum(match_live * slot.astype(jnp.float32), axis=0, keepdims=True)
    row = lax.broadcasted_iota(jnp.int32, (tokens, tokens), 0)
    col = lax.broadcasted_iota(jnp.int32, (tokens, tokens), 1)
    before = jnp.where(row < col, 1.0, 0.0).astype(jnp.bfloat16)
    left = jnp.broadcast_to(1.0 - kept, (16, tokens)).astype(jnp.bfloat16)
    rank = one_hot_dot(left, before)[0:1, :]
    place = jnp.where(kept > 0.5, kept_slot, jnp.sum(kept, axis=1, keepdims=True) + rank)
    order = jnp.where(row.astype(jnp.float32) == place, 1.0, 0.0).astype(jnp.bfloat16)

    for copy in copies[1:]:
        copy.wait()
    scale = HEAD_DIM ** (-0.5)
    match_live = match_live.astype(jnp.bfloat16)
    match_fill = match_fill.astype(jnp.bfloat16)
    query = one_hot_dot(match_live, eq_ref[0]) * scale
    dead = jnp.where(live, 0.0, DEAD)
    query = query + jnp.concatenate([dead] * (cols // tokens), axis=1)
    key = one_hot_dot(match_fill, ek_ref[0])
    value = one_hot_dot(match_live, ev_ref[0])
    dec_key = one_hot_dot(order, dk_ref[0])
    dec_query = dq_ref[0].astype(jnp.float32) * scale

    def low(block, head):
        tile = block[:, (head // 2) * LANES : (head // 2 + 1) * LANES]
        return tile if head % 2 == 0 else pltpu.roll(tile, HEAD_DIM, 1)

    def high(block, head):
        tile = block[:, (head // 2) * LANES : (head // 2 + 1) * LANES]
        return tile if head % 2 == 1 else pltpu.roll(tile, HEAD_DIM, 1)

    def join(first, second):
        lane = lax.broadcasted_iota(jnp.int32, first.shape, 1)
        return jnp.where(lane < HEAD_DIM, first, second).astype(jnp.bfloat16)

    for head in range(heads):
        kept_tile = join(low(value, head), high(key, head))
        query_high = high(query, head)
        dec_low = low(dec_key, head)
        dq_low = low(dec_query, head)
        dq_high = high(dec_query, head)
        send_ref[head, 0:slots, :] = kept_tile
        send_ref[head, slots : 2 * slots, :] = join(dec_low[0:slots], query_high)
        send_ref[head, 2 * slots : slots + tokens, :] = join(dec_low[slots:tokens], dq_high[0:spare])
        rest = slots // 2
        send_ref[head, slots + tokens : slots + tokens + rest, :] = join(
            dq_low[spare : spare + rest], dq_high[spare + rest : tokens]
        )


def put_scores(query, key_refs, place, peak):
    rows = query.shape[0]
    largest = None
    column = 0
    for key_ref in key_refs:
        keys = key_ref.shape[0]
        for first in range(0, keys, 2 * LANES):
            last = min(keys, first + 2 * LANES)
            part = lax.dot_general(
                query, key_ref[first:last, :], (((1,), (1,)), ((), ())), preferred_element_type=jnp.float32
            )
            place[0:rows, column : column + last - first] = part
            column += last - first
            for lane in range(0, last - first, LANES):
                tile = part[:, lane : lane + LANES]
                largest = tile if largest is None else jnp.maximum(largest, tile)
    peak[0:rows, :] = largest


def weigh(rows, place, peak, value_refs, earlier):
    top = jnp.max(peak[0:rows, :], axis=1, keepdims=True)
    sums = None
    if earlier is not None:
        earlier_sums, earlier_top = earlier
        top = jnp.maximum(top, earlier_top[:, 0:1])
        sums = earlier_sums * jnp.exp(earlier_top - top)
    column = 0
    for value_ref in value_refs:
        keys = value_ref.shape[0]
        weights = jnp.exp(place[0:rows, column : column + keys] - top).astype(jnp.bfloat16)
        column += keys
        part = lax.dot_general(
            weights, value_ref[...], (((1,), (0,)), ((), ())), preferred_element_type=jnp.float32
        )
        sums = part if sums is None else sums + part
    return top, sums


def run_jobs(jobs, buffers):
    def put(number):
        query, key_refs, _, _, _ = jobs[number]
        put_scores(query(), key_refs, *buffers[number % 2])

    put(0)
    for number, (query, _, value_refs, earlier, use) in enumerate(jobs):
        if number + 1 < len(jobs):
            put(number + 1)
        place, peak = buffers[number % 2]
        rows = query().shape[0]
        use(*weigh(rows, place, peak, value_refs, None if earlier is None else earlier()))


def lane_of(rows):
    return lax.broadcasted_iota(jnp.int32, (rows, LANES), 1)


def unpack(slots, tokens, got, block, first_key, first_dec, ek_ref, ev_ref, eq_ref, dk_ref):
    kept = got[0:slots, :]
    mixed = got[slots : 2 * slots, :].astype(jnp.float32)
    low = lane_of(slots) < HEAD_DIM
    base = first_key + block * slots
    ek_ref[base : base + slots, :] = kept
    ev_ref[base : base + slots, :] = jnp.where(
        low, kept.astype(jnp.float32), jnp.where(mixed < DEAD_EDGE, 1.0, 0.0)
    ).astype(jnp.bfloat16)
    eq_ref[block * slots : block * slots + slots, :] = jnp.where(low, 0.0, mixed).astype(jnp.bfloat16)
    base = first_dec + block * tokens
    dk_ref[base : base + tokens, :] = got[slots : slots + tokens, :]


def begin_kernel(
    slots,
    tokens,
    own_ref,
    text_key_ref,
    text_value_ref,
    mask_ref,
    gain_ref,
    steps_ref,
    ek_ref,
    ev_ref,
    eq_ref,
    dk_ref,
    dq_ref,
    sums_ref,
    top_ref,
    fill_ref,
    weight_ref,
    wide_gain_ref,
    *places
):
    chips = own_ref.shape[0]
    cols = text_key_ref.shape[2]
    spare = tokens - slots
    rest = slots // 2
    head = jnp.minimum(lax.axis_index("seq") // 2, cols // HEAD_DIM - 1)
    odd = lax.rem(head, 2) == 1
    lanes = pl.ds(pl.multiple_of((head // 2) * LANES, LANES), LANES)

    def low_high(rows):
        turned = pltpu.roll(rows, HEAD_DIM, 1)
        return jnp.where(odd, turned, rows), jnp.where(odd, rows, turned)

    key_low, key_high = low_high(text_key_ref[0, :, lanes].astype(jnp.float32))
    value_low, _ = low_high(text_value_ref[0, :, lanes].astype(jnp.float32))
    mask_row = jnp.zeros((1, LANES), jnp.float32)
    whole = mask_ref[...].astype(jnp.float32).reshape(1, cols)
    for tile in range(cols // LANES):
        mask_row = jnp.where(head // 2 == tile, whole[:, tile * LANES : (tile + 1) * LANES], mask_row)
    mask_row, _ = low_high(jnp.broadcast_to(mask_row, (8, LANES)))
    steps = jnp.full((8, LANES), steps_ref[0], jnp.int32).astype(jnp.float32)
    weight_ref[...] = 1.0 / (0.1 + steps / 999.0)
    wide_gain_ref[...] = jnp.broadcast_to(gain_ref[...].astype(jnp.float32).reshape(1, cols), (8, cols))
    low = lane_of(tokens) < HEAD_DIM
    fill_ref[...] = jnp.where(lane_of(8) < HEAD_DIM, mask_row, 1.0)
    ek_ref[0:tokens, :] = jnp.where(low, value_low, key_high).astype(jnp.bfloat16)
    ev_ref[0:tokens, :] = jnp.where(low, value_low, 1.0).astype(jnp.bfloat16)
    dk_ref[0:tokens, :] = key_low.astype(jnp.bfloat16)
    for block in range(chips):
        got = own_ref.at[block]
        unpack(slots, tokens, got, block, tokens, tokens, ek_ref, ev_ref, eq_ref, dk_ref)
        tail = got[2 * slots : slots + tokens, :].astype(jnp.float32)
        last = got[slots + tokens : slots + tokens + rest, :].astype(jnp.float32)
        base = block * tokens
        dq_ref[base : base + spare, :] = jnp.where(
            lane_of(spare) < HEAD_DIM, pltpu.roll(tail, HEAD_DIM, 1), 0.0
        ).astype(jnp.bfloat16)
        low_rest = lane_of(rest) < HEAD_DIM
        dq_ref[base + spare : base + spare + rest, :] = jnp.where(low_rest, last, 0.0).astype(jnp.bfloat16)
        dq_ref[base + spare + rest : base + tokens, :] = jnp.where(
            low_rest, pltpu.roll(last, HEAD_DIM, 1), 0.0
        ).astype(jnp.bfloat16)

    rows = chips // 2 * slots

    def job(tile):
        span = slice(tile * rows, (tile + 1) * rows)

        def use(top, sums):
            sums_ref[span, :] = sums
            top_ref[span, :] = jnp.broadcast_to(top, (rows, LANES))

        return (lambda: eq_ref[span, :], [ek_ref], [ev_ref], None, use)

    run_jobs([job(tile) for tile in range(2)], (places[0:2], places[2:4]))


def attend_kernel(
    slots,
    tokens,
    pair_ref,
    ek_ref,
    ev_ref,
    eq_ref,
    dk_ref,
    dq_ref,
    sums_ref,
    top_ref,
    fill_ref,
    out_ref,
    pair_ek_ref,
    pair_ev_ref,
    pair_eq_ref,
    pair_dk_ref,
    dv_ref,
    *places
):
    chips = pair_ref.shape[0]
    spare = tokens - slots
    for block in range(chips):
        unpack(
            slots, tokens, pair_ref.at[block], block, 0, 0, pair_ek_ref, pair_ev_ref, pair_eq_ref, pair_dk_ref
        )
    dv_ref[0:tokens, :] = ev_ref[0:tokens, :]
    mask_row = fill_ref[0:1, :]
    fill = jnp.broadcast_to(mask_row, (spare, LANES)).astype(jnp.bfloat16)
    group = chips // 2
    rows = group * slots

    def encode(tile, query_ref, first_block, key_refs, value_refs, earlier):
        span = slice(tile * rows, (tile + 1) * rows)

        def use(top, sums):
            found = sums / pltpu.roll(sums, HEAD_DIM, 1)
            for inner in range(group):
                mixed = query_ref[tile * rows + inner * slots : tile * rows + (inner + 1) * slots, :]
                live = pltpu.roll(mixed.astype(jnp.float32), HEAD_DIM, 1) < DEAD_EDGE
                base = tokens + (first_block + tile * group + inner) * tokens
                dv_ref[base : base + slots, :] = jnp.where(
                    (lane_of(slots) < HEAD_DIM) & live, found[inner * slots : (inner + 1) * slots, :], mask_row
                ).astype(jnp.bfloat16)
                dv_ref[base + slots : base + tokens, :] = fill

        before = (lambda: (sums_ref[span, :], top_ref[span, :])) if earlier else None
        return (lambda: query_ref[span, :], key_refs, value_refs, before, use)

    dec_group = 2
    dec_rows = dec_group * tokens
    half = tokens // 2

    def decode(tile):
        def use(top, sums):
            found = sums / pltpu.roll(sums, HEAD_DIM, 1)
            for inner in range(dec_group):
                first = inner * tokens
                out_ref[tile * dec_group + inner] = jnp.where(
                    lane_of(half) < HEAD_DIM,
                    found[first : first + half],
                    pltpu.roll(found[first + half : first + tokens], HEAD_DIM, 1),
                ).astype(jnp.bfloat16)

        span = slice(tile * dec_rows, (tile + 1) * dec_rows)
        return (lambda: dq_ref[span, :], [dk_ref, pair_dk_ref], [dv_ref], None, use)

    jobs = [encode(tile, eq_ref, 0, [pair_ek_ref], [pair_ev_ref], True) for tile in range(2)]
    jobs += [
        encode(tile, pair_eq_ref, chips, [ek_ref, pair_ek_ref], [ev_ref, pair_ev_ref], False) for tile in range(2)
    ]
    jobs += [decode(tile) for tile in range(chips // dec_group)]
    run_jobs(jobs, (places[0:2], places[2:4]))


def sums_kernel(got_ref, gain_ref, target_ref, weight_ref, att_ref, sums_ref):
    tokens, cols = att_ref.shape
    half = tokens // 2
    low = lax.broadcasted_iota(jnp.int32, (half, LANES), 1) < HEAD_DIM
    for tile in range(cols // LANES):
        even = got_ref[2 * tile].astype(jnp.float32)
        odd = got_ref[2 * tile + 1].astype(jnp.float32)
        span = slice(tile * LANES, (tile + 1) * LANES)
        att_ref[0:half, span] = jnp.where(low, even, pltpu.roll(odd, HEAD_DIM, 1))
        att_ref[half:tokens, span] = jnp.where(low, pltpu.roll(even, HEAD_DIM, 1), odd)
    att = att_ref[...]
    gained = att * gain_ref[0:1, :]
    target = target_ref[0].astype(jnp.float32)
    weight = weight_ref[0:1, :]
    lane = lax.broadcasted_iota(jnp.int32, (tokens, LANES), 1)

    def over(block):
        return jnp.sum(block, axis=1, keepdims=True)

    table = jnp.where(
        lane == 1,
        over(gained * gained),
        jnp.where(lane == 2, over(gained * target), over(target * target)),
    )
    table = jnp.where(lane == 0, over(att * att), table * weight)
    sums_ref[...] = jnp.broadcast_to(jnp.transpose(table)[None, 0:4, :], sums_ref.shape)


def loss_kernel(heads, total_cols, sums_ref, loss_ref):
    total = None
    for chip in range(sums_ref.shape[0] // heads):
        sums = jnp.sum(sums_ref[chip * heads : (chip + 1) * heads], axis=0)
        factor = lax.rsqrt(sums[0:1, :] / total_cols + 1e-06)
        error = factor * factor * sums[1:2, :] - 2.0 * factor * sums[2:3, :] + sums[3:4, :]
        total = error if total is None else total + error
    loss_ref[...] = jnp.broadcast_to(jnp.sum(total, axis=1, keepdims=True)[None], loss_ref.shape)


def finish_kernel(heads, count, att_ref, gain_ref, sums_ref, got_ref, out_ref, loss_ref):
    tokens, cols = att_ref.shape
    loss_ref[...] = (jnp.sum(got_ref[...], axis=0) / count)[0:1, 0:1]
    own = jnp.sum(sums_ref[pl.ds(lax.axis_index("seq") // 2 * heads, heads)], axis=0)
    factor = lax.rsqrt(own[0:1, :] / (cols * heads) + 1e-06)
    column = jnp.transpose(jnp.broadcast_to(factor, (tokens, tokens)))[:, 0:1]
    out_ref[0] = (att_ref[...] * column * gain_ref[0:1, :]).astype(jnp.bfloat16)


def local(
    enc_query,
    enc_key,
    enc_value,
    keep_index,
    keep_count,
    text_key,
    text_value,
    dec_query,
    dec_key,
    mask_value,
    norm_gain,
    target,
    timesteps,
):
    images, seq, heads = (lax.axis_size(name) for name in ("dp", "seq", "head"))
    tokens, cols = enc_query.shape[1:]
    slots = keep_index.shape[1]
    local_heads = cols // HEAD_DIM
    chips = seq // 2
    packed = slots + tokens + slots // 2
    same_core = [[2 * chip + core for chip in range(chips)] for core in range(2)]
    bf16, f32 = jnp.bfloat16, jnp.float32

    send = pl.pallas_call(
        pack_kernel,
        out_shape=jax.ShapeDtypeStruct((chips, packed, LANES), bf16),
        in_specs=[pl.BlockSpec(memory_space=pltpu.HBM)] * 6,
        out_specs=vmem(1)[0],
        scratch_shapes=[pltpu.VMEM((1, slots), jnp.int32)]
        + [pltpu.VMEM((1, tokens, cols), bf16)] * 5
        + [pltpu.SemaphoreType.DMA((6,))],
        compiler_params=params(60),
        name="pack",
    )(keep_index, enc_query, enc_key, enc_value, dec_query, dec_key)
    own = lax.all_to_all(send, "seq", 0, 0, axis_index_groups=same_core, tiled=True)
    pair = lax.ppermute(own, "seq", [(source, source ^ 1) for source in range(seq)])
    kept_own = chips * slots
    dec_own = chips * tokens
    *begun, weight, gain = pl.pallas_call(
        functools.partial(begin_kernel, slots, tokens),
        out_shape=(
            jax.ShapeDtypeStruct((tokens + kept_own, LANES), bf16),
            jax.ShapeDtypeStruct((tokens + kept_own, LANES), bf16),
            jax.ShapeDtypeStruct((kept_own, LANES), bf16),
            jax.ShapeDtypeStruct((tokens + dec_own, LANES), bf16),
            jax.ShapeDtypeStruct((dec_own, LANES), bf16),
            jax.ShapeDtypeStruct((kept_own, LANES), f32),
            jax.ShapeDtypeStruct((kept_own, LANES), f32),
            jax.ShapeDtypeStruct((8, LANES), f32),
            jax.ShapeDtypeStruct((8, LANES), f32),
            jax.ShapeDtypeStruct((8, cols), f32),
        ),
        in_specs=vmem(5) + [pl.BlockSpec(memory_space=pltpu.SMEM)],
        out_specs=tuple(vmem(10)),
        scratch_shapes=[
            pltpu.VMEM((kept_own // 2, tokens + kept_own), f32),
            pltpu.VMEM((kept_own // 2, LANES), f32),
        ]
        * 2,
        compiler_params=params(),
        cost_estimate=pl.CostEstimate(
            flops=4 * kept_own * (tokens + kept_own) * LANES,
            bytes_accessed=8 * MIB,
            transcendentals=kept_own * (tokens + kept_own),
        ),
        name="begin",
    )(own, text_key, text_value, mask_value, norm_gain, timesteps)
    out = pl.pallas_call(
        functools.partial(attend_kernel, slots, tokens),
        out_shape=jax.ShapeDtypeStruct((chips, tokens // 2, LANES), bf16),
        in_specs=vmem(9),
        out_specs=vmem(1)[0],
        scratch_shapes=[
            pltpu.VMEM((kept_own, LANES), bf16),
            pltpu.VMEM((kept_own, LANES), bf16),
            pltpu.VMEM((kept_own, LANES), bf16),
            pltpu.VMEM((dec_own, LANES), bf16),
            pltpu.VMEM((tokens + 2 * dec_own, LANES), bf16),
        ]
        + [
            pltpu.VMEM((kept_own // 2, tokens + 2 * dec_own), f32),
            pltpu.VMEM((kept_own // 2, LANES), f32),
        ]
        * 2,
        compiler_params=params(),
        name="attend",
    )(pair, *begun)
    got = lax.all_to_all(out, "seq", 0, 0, axis_index_groups=same_core, tiled=True)
    att, sums = pl.pallas_call(
        sums_kernel,
        out_shape=(
            jax.ShapeDtypeStruct((tokens, cols), f32),
            jax.ShapeDtypeStruct((chips * heads, 4, tokens), f32),
        ),
        in_specs=vmem(4),
        out_specs=tuple(vmem(2)),
        compiler_params=params(),
        name="sums",
    )(got, gain, target, weight)
    planes = [
        [(2 * chip + core) * heads + head for chip in range(chips) for head in range(heads)] for core in range(2)
    ]
    sums = lax.all_to_all(sums, ("seq", "head"), 0, 0, axis_index_groups=planes, tiled=True)
    loss = pl.pallas_call(
        functools.partial(loss_kernel, heads, cols * heads),
        out_shape=jax.ShapeDtypeStruct((2 * images, 1, LANES), f32),
        in_specs=vmem(1),
        out_specs=vmem(1)[0],
        compiler_params=params(),
        name="loss",
    )(sums)
    columns = [
        [image * seq + 2 * chip + core for image in range(images) for core in range(2)] for chip in range(chips)
    ]
    got = lax.all_to_all(loss, ("dp", "seq"), 0, 0, axis_index_groups=columns, tiled=True)
    decoded, loss = pl.pallas_call(
        functools.partial(finish_kernel, heads, float(images * tokens * seq * cols * heads)),
        out_shape=(
            jax.ShapeDtypeStruct((1, tokens, cols), bf16),
            jax.ShapeDtypeStruct((1, 1), f32),
        ),
        in_specs=vmem(4),
        out_specs=tuple(vmem(2)),
        compiler_params=params(),
        name="finish",
    )(att, gain, sums, got)
    total_loss = loss.reshape(())
    return (decoded, total_loss)


def solution(mesh):
    placed = (
        P("dp", "seq", "head"),
        P("dp", "seq", "head"),
        P("dp", "seq", "head"),
        P("dp", "seq"),
        P("dp", "seq"),
        P("dp", None, "head"),
        P("dp", None, "head"),
        P("dp", "seq", "head"),
        P("dp", "seq", "head"),
        P("head"),
        P("head"),
        P("dp", "seq", "head"),
        P("dp"),
    )
    return jax.shard_map(
        local, mesh=mesh, in_specs=placed, out_specs=(P("dp", "seq", "head"), P()), check_vma=False
    )
```

```python
import functools

import jax
import jax.numpy as jnp
from jax import lax
from jax.experimental import pallas as pl
from jax.experimental.pallas import tpu as pltpu
from jax.sharding import PartitionSpec as P

HEAD_DIM = 64
LANES = 128
DEAD = 1024.0
DEAD_EDGE = 512.0
MIB = 1024 * 1024


def params(mib=40):
    return pltpu.CompilerParams(vmem_limit_bytes=mib * MIB)


def vmem(count):
    return [pl.BlockSpec(memory_space=pltpu.VMEM)] * count


def one_hot_dot(table, rows):
    return lax.dot_general(
        table, rows, (((1,), (0,)), ((), ())), preferred_element_type=jnp.float32
    )


def pack_kernel(
    index_hbm, eq_hbm, ek_hbm, ev_hbm, dq_hbm, dk_hbm, enc_ref, dec_ref, *scratch
):
    *held, sems = scratch
    given = (index_hbm, eq_hbm, ek_hbm, ev_hbm, dq_hbm, dk_hbm)
    copies = [
        pltpu.make_async_copy(source, place, sems.at[number])
        for number, (source, place) in enumerate(zip(given, held))
    ]
    for copy in copies:
        copy.start()
    copies[0].wait()
    index_ref, eq_ref, ek_ref, ev_ref, dq_ref, dk_ref = held
    tokens, cols = eq_ref.shape[1:]
    slots = index_ref.shape[1]
    heads = cols // HEAD_DIM
    index = jnp.broadcast_to(index_ref[...].astype(jnp.float32), (tokens, slots))
    index = jnp.transpose(index)
    token = lax.broadcasted_iota(jnp.int32, (slots, tokens), 1).astype(jnp.float32)
    slot = lax.broadcasted_iota(jnp.int32, (slots, tokens), 0)
    live = (slot == 0) | (index > 0.5)
    match_live = jnp.where(live & (token == index), 1.0, 0.0)
    match_fill = jnp.where(token == jnp.where(live, index, index[0:1, :]), 1.0, 0.0)
    kept = jnp.sum(match_live, axis=0, keepdims=True)
    kept_slot = jnp.sum(match_live * slot.astype(jnp.float32), axis=0, keepdims=True)
    row = lax.broadcasted_iota(jnp.int32, (tokens, tokens), 0)
    col = lax.broadcasted_iota(jnp.int32, (tokens, tokens), 1)
    before = jnp.where(row < col, 1.0, 0.0).astype(jnp.bfloat16)
    left = jnp.broadcast_to(1.0 - kept, (16, tokens)).astype(jnp.bfloat16)
    rank = one_hot_dot(left, before)[0:1, :]
    place = jnp.where(kept > 0.5, kept_slot, jnp.sum(kept, axis=1, keepdims=True) + rank)
    order = jnp.where(row.astype(jnp.float32) == place, 1.0, 0.0).astype(jnp.bfloat16)

    for copy in copies[1:]:
        copy.wait()
    scale = HEAD_DIM ** (-0.5)
    match_live = match_live.astype(jnp.bfloat16)
    match_fill = match_fill.astype(jnp.bfloat16)
    query = one_hot_dot(match_live, eq_ref[0]) * scale
    dead = jnp.where(live, 0.0, DEAD)
    query = query + jnp.concatenate([dead] * (cols // tokens), axis=1)
    key = one_hot_dot(match_fill, ek_ref[0])
    value = one_hot_dot(match_live, ev_ref[0])
    dec_key = one_hot_dot(order, dk_ref[0])
    dec_query = dq_ref[0].astype(jnp.float32) * scale

    def low(block, head):
        tile = block[:, (head // 2) * LANES : (head // 2 + 1) * LANES]
        return tile if head % 2 == 0 else pltpu.roll(tile, HEAD_DIM, 1)

    def high(block, head):
        tile = block[:, (head // 2) * LANES : (head // 2 + 1) * LANES]
        return tile if head % 2 == 1 else pltpu.roll(tile, HEAD_DIM, 1)

    def join(first, second):
        lane = lax.broadcasted_iota(jnp.int32, first.shape, 1)
        return jnp.where(lane < HEAD_DIM, first, second).astype(jnp.bfloat16)

    half = slots // 2
    for head in range(heads):
        enc_ref[head, 0:slots, :] = join(low(value, head), high(key, head))
        enc_ref[head, slots : slots + half, :] = join(low(query, head)[0:half], high(query, head)[half:slots])
        dec_ref[head] = join(low(dec_key, head), high(dec_query, head))


def put_scores(query, key_refs, place, peak):
    rows = query.shape[0]
    largest = None
    column = 0
    for key_ref in key_refs:
        keys = key_ref.shape[0]
        for first in range(0, keys, 2 * LANES):
            last = min(keys, first + 2 * LANES)
            part = lax.dot_general(
                query, key_ref[first:last, :], (((1,), (1,)), ((), ())), preferred_element_type=jnp.float32
            )
            place[0:rows, column : column + last - first] = part
            column += last - first
            for lane in range(0, last - first, LANES):
                tile = part[:, lane : lane + LANES]
                largest = tile if largest is None else jnp.maximum(largest, tile)
    peak[0:rows, :] = largest


def weigh(rows, place, peak, value_refs, earlier):
    top = jnp.max(peak[0:rows, :], axis=1, keepdims=True)
    sums = None
    if earlier is not None:
        earlier_sums, earlier_top = earlier
        top = jnp.maximum(top, earlier_top[:, 0:1])
        sums = earlier_sums * jnp.exp(earlier_top - top)
    column = 0
    for value_ref in value_refs:
        keys = value_ref.shape[0]
        weights = jnp.exp(place[0:rows, column : column + keys] - top).astype(jnp.bfloat16)
        column += keys
        part = lax.dot_general(
            weights, value_ref[...], (((1,), (0,)), ((), ())), preferred_element_type=jnp.float32
        )
        sums = part if sums is None else sums + part
    return top, sums


def run_jobs(jobs, buffers):
    def put(number):
        query, key_refs, _, _, _ = jobs[number]
        put_scores(query(), key_refs, *buffers[number % 2])

    put(0)
    for number, (query, _, value_refs, earlier, use) in enumerate(jobs):
        if number + 1 < len(jobs):
            put(number + 1)
        place, peak = buffers[number % 2]
        rows = jax.eval_shape(query).shape[0]
        use(*weigh(rows, place, peak, value_refs, None if earlier is None else earlier()))


def lane_of(rows):
    return lax.broadcasted_iota(jnp.int32, (rows, LANES), 1)


def unpack(slots, got, block, first_key, ek_ref, ev_ref, eq_ref):
    half = slots // 2
    kept = got[0:slots, :]
    packed = got[slots : slots + half, :].astype(jnp.float32)
    query = jnp.concatenate([pltpu.roll(packed, HEAD_DIM, 1), packed], axis=0)
    low = lane_of(slots) < HEAD_DIM
    base = first_key + block * slots
    ek_ref[base : base + slots, :] = kept
    ev_ref[base : base + slots, :] = jnp.where(
        low, kept.astype(jnp.float32), jnp.where(query < DEAD_EDGE, 1.0, 0.0)
    ).astype(jnp.bfloat16)
    eq_ref[block * slots : block * slots + slots, :] = jnp.where(low, 0.0, query).astype(jnp.bfloat16)


def begin_kernel(
    slots,
    own_ref,
    text_key_ref,
    text_value_ref,
    mask_ref,
    gain_ref,
    steps_ref,
    ek_ref,
    ev_ref,
    eq_ref,
    dk_ref,
    sums_ref,
    top_ref,
    fill_ref,
    weight_ref,
    wide_gain_ref,
    *places
):
    chips = own_ref.shape[0]
    tokens, cols = text_key_ref.shape[1:]
    head = jnp.minimum(lax.axis_index("seq") // 2, cols // HEAD_DIM - 1)
    odd = lax.rem(head, 2) == 1
    lanes = pl.ds(pl.multiple_of((head // 2) * LANES, LANES), LANES)

    def low_high(rows):
        turned = pltpu.roll(rows, HEAD_DIM, 1)
        return jnp.where(odd, turned, rows), jnp.where(odd, rows, turned)

    key_low, key_high = low_high(text_key_ref[0, :, lanes].astype(jnp.float32))
    value_low, _ = low_high(text_value_ref[0, :, lanes].astype(jnp.float32))
    mask_row = jnp.zeros((1, LANES), jnp.float32)
    whole = mask_ref[...].astype(jnp.float32).reshape(1, cols)
    for tile in range(cols // LANES):
        mask_row = jnp.where(head // 2 == tile, whole[:, tile * LANES : (tile + 1) * LANES], mask_row)
    mask_row, _ = low_high(jnp.broadcast_to(mask_row, (8, LANES)))
    steps = jnp.full((8, LANES), steps_ref[0], jnp.int32).astype(jnp.float32)
    weight_ref[...] = 1.0 / (0.1 + steps / 999.0)
    wide_gain_ref[...] = jnp.broadcast_to(gain_ref[...].astype(jnp.float32).reshape(1, cols), (8, cols))
    low = lane_of(tokens) < HEAD_DIM
    fill_ref[...] = jnp.where(lane_of(8) < HEAD_DIM, mask_row, 1.0)
    ek_ref[0:tokens, :] = jnp.where(low, value_low, key_high).astype(jnp.bfloat16)
    ev_ref[0:tokens, :] = jnp.where(low, value_low, 1.0).astype(jnp.bfloat16)
    dk_ref[...] = key_low.astype(jnp.bfloat16)
    for block in range(chips):
        unpack(slots, own_ref.at[block], block, tokens, ek_ref, ev_ref, eq_ref)
    rows = chips // 2 * slots

    def job(tile):
        span = slice(tile * rows, (tile + 1) * rows)

        def use(top, sums):
            sums_ref[span, :] = sums
            top_ref[span, :] = jnp.broadcast_to(top, (rows, LANES))

        return (lambda: eq_ref[span, :], [ek_ref], [ev_ref], None, use)

    run_jobs([job(tile) for tile in range(2)], (places[0:2], places[2:4]))


def encode_kernel(
    slots,
    tokens,
    pair_ref,
    ek_ref,
    ev_ref,
    eq_ref,
    sums_ref,
    top_ref,
    fill_ref,
    dv_ref,
    pair_ek_ref,
    pair_ev_ref,
    pair_eq_ref,
    *places
):
    chips = pair_ref.shape[0]
    spare = tokens - slots
    for block in range(chips):
        unpack(slots, pair_ref.at[block], block, 0, pair_ek_ref, pair_ev_ref, pair_eq_ref)
    dv_ref[0:tokens, :] = ev_ref[0:tokens, :]
    mask_row = fill_ref[0:1, :]
    fill = jnp.broadcast_to(mask_row, (spare, LANES)).astype(jnp.bfloat16)
    group = chips // 2
    rows = group * slots

    def encode(tile, query_ref, first_block, key_refs, value_refs, earlier):
        span = slice(tile * rows, (tile + 1) * rows)

        def use(top, sums):
            found = sums / pltpu.roll(sums, HEAD_DIM, 1)
            for inner in range(group):
                mixed = query_ref[tile * rows + inner * slots : tile * rows + (inner + 1) * slots, :]
                live = pltpu.roll(mixed.astype(jnp.float32), HEAD_DIM, 1) < DEAD_EDGE
                base = tokens + (first_block + tile * group + inner) * tokens
                dv_ref[base : base + slots, :] = jnp.where(
                    (lane_of(slots) < HEAD_DIM) & live, found[inner * slots : (inner + 1) * slots, :], mask_row
                ).astype(jnp.bfloat16)
                dv_ref[base + slots : base + tokens, :] = fill

        before = (lambda: (sums_ref[span, :], top_ref[span, :])) if earlier else None
        return (lambda: query_ref[span, :], key_refs, value_refs, before, use)

    jobs = [encode(tile, eq_ref, 0, [pair_ek_ref], [pair_ev_ref], True) for tile in range(2)]
    jobs += [
        encode(tile, pair_eq_ref, chips, [ek_ref, pair_ek_ref], [ev_ref, pair_ev_ref], False) for tile in range(2)
    ]
    run_jobs(jobs, (places[0:2], places[2:4]))


def decode_kernel(tokens, own_ref, pair_ref, dk_ref, dv_ref, out_ref, *places):
    group = 2
    rows = group * tokens
    half = tokens // 2

    def decode(tile):
        span = slice(tile * rows, (tile + 1) * rows)

        def query():
            turned = pltpu.roll(own_ref[span, :].astype(jnp.float32), HEAD_DIM, 1)
            return jnp.where(lane_of(rows) < HEAD_DIM, turned, 0.0).astype(jnp.bfloat16)

        def use(top, sums):
            found = sums / pltpu.roll(sums, HEAD_DIM, 1)
            for inner in range(group):
                first = inner * tokens
                out_ref[tile * group + inner] = jnp.where(
                    lane_of(half) < HEAD_DIM,
                    found[first : first + half],
                    pltpu.roll(found[first + half : first + tokens], HEAD_DIM, 1),
                ).astype(jnp.bfloat16)

        return (query, [own_ref, pair_ref, dk_ref], [dv_ref.at[tokens:], dv_ref.at[0:tokens]], None, use)

    jobs = [decode(tile) for tile in range(out_ref.shape[0] // group)]
    run_jobs(jobs, (places[0:2], places[2:4]))


def sums_kernel(got_ref, gain_ref, target_ref, weight_ref, att_ref, sums_ref):
    tokens, cols = att_ref.shape
    half = tokens // 2
    low = lax.broadcasted_iota(jnp.int32, (half, LANES), 1) < HEAD_DIM
    for tile in range(cols // LANES):
        even = got_ref[2 * tile].astype(jnp.float32)
        odd = got_ref[2 * tile + 1].astype(jnp.float32)
        span = slice(tile * LANES, (tile + 1) * LANES)
        att_ref[0:half, span] = jnp.where(low, even, pltpu.roll(odd, HEAD_DIM, 1))
        att_ref[half:tokens, span] = jnp.where(low, pltpu.roll(even, HEAD_DIM, 1), odd)
    att = att_ref[...]
    gained = att * gain_ref[0:1, :]
    target = target_ref[0].astype(jnp.float32)
    weight = weight_ref[0:1, :]
    lane = lax.broadcasted_iota(jnp.int32, (tokens, LANES), 1)

    def over(block):
        return jnp.sum(block, axis=1, keepdims=True)

    table = jnp.where(
        lane == 1,
        over(gained * gained),
        jnp.where(lane == 2, over(gained * target), over(target * target)),
    )
    table = jnp.where(lane == 0, over(att * att), table * weight)
    sums_ref[...] = jnp.broadcast_to(jnp.transpose(table)[None, 0:4, :], sums_ref.shape)


def loss_kernel(heads, total_cols, sums_ref, loss_ref):
    total = None
    for chip in range(sums_ref.shape[0] // heads):
        sums = jnp.sum(sums_ref[chip * heads : (chip + 1) * heads], axis=0)
        factor = lax.rsqrt(sums[0:1, :] / total_cols + 1e-06)
        error = factor * factor * sums[1:2, :] - 2.0 * factor * sums[2:3, :] + sums[3:4, :]
        total = error if total is None else total + error
    loss_ref[...] = jnp.broadcast_to(jnp.sum(total, axis=1, keepdims=True)[None], loss_ref.shape)


def finish_kernel(heads, count, att_ref, gain_ref, sums_ref, got_ref, out_ref, loss_ref):
    tokens, cols = att_ref.shape
    loss_ref[...] = (jnp.sum(got_ref[...], axis=0) / count)[0:1, 0:1]
    own = jnp.sum(sums_ref[pl.ds(lax.axis_index("seq") // 2 * heads, heads)], axis=0)
    factor = lax.rsqrt(own[0:1, :] / (cols * heads) + 1e-06)
    column = jnp.transpose(jnp.broadcast_to(factor, (tokens, tokens)))[:, 0:1]
    out_ref[0] = (att_ref[...] * column * gain_ref[0:1, :]).astype(jnp.bfloat16)


def local(
    enc_query,
    enc_key,
    enc_value,
    keep_index,
    keep_count,
    text_key,
    text_value,
    dec_query,
    dec_key,
    mask_value,
    norm_gain,
    target,
    timesteps,
):
    images, seq, heads = (lax.axis_size(name) for name in ("dp", "seq", "head"))
    tokens, cols = enc_query.shape[1:]
    slots = keep_index.shape[1]
    local_heads = cols // HEAD_DIM
    chips = seq // 2
    rings = [[2 * chip + core for chip in range(chips)] for core in range(2)]
    bf16, f32 = jnp.bfloat16, jnp.float32

    kept_own = chips * slots
    dec_own = chips * tokens
    enc_rows = slots + slots // 2
    partner = [(source, source ^ 1) for source in range(seq)]

    def exchange(rows):
        return lax.all_to_all(rows, "seq", 0, 0, axis_index_groups=rings, tiled=True)

    def work(rows, keys):
        return pl.CostEstimate(flops=4 * rows * keys * LANES, bytes_accessed=8 * MIB, transcendentals=rows * keys)

    def scores(rows, keys):
        return [pltpu.VMEM((rows, keys), f32), pltpu.VMEM((rows, LANES), f32)] * 2

    enc_send, dec_send = pl.pallas_call(
        pack_kernel,
        out_shape=(
            jax.ShapeDtypeStruct((chips, enc_rows, LANES), bf16),
            jax.ShapeDtypeStruct((chips, tokens, LANES), bf16),
        ),
        in_specs=[pl.BlockSpec(memory_space=pltpu.HBM)] * 6,
        out_specs=tuple(vmem(2)),
        scratch_shapes=[pltpu.VMEM((1, slots), jnp.int32)]
        + [pltpu.VMEM((1, tokens, cols), bf16)] * 5
        + [pltpu.SemaphoreType.DMA((6,))],
        compiler_params=params(60),
        name="pack",
    )(keep_index, enc_query, enc_key, enc_value, dec_query, dec_key)
    enc_own = exchange(enc_send)
    dec_blocks = exchange(dec_send)
    enc_pair = lax.ppermute(enc_own, "seq", partner)
    dec_pair = lax.ppermute(dec_blocks, "seq", partner)
    *begun, fill, weight, gain = pl.pallas_call(
        functools.partial(begin_kernel, slots),
        out_shape=(
            jax.ShapeDtypeStruct((tokens + kept_own, LANES), bf16),
            jax.ShapeDtypeStruct((tokens + kept_own, LANES), bf16),
            jax.ShapeDtypeStruct((kept_own, LANES), bf16),
            jax.ShapeDtypeStruct((tokens, LANES), bf16),
            jax.ShapeDtypeStruct((kept_own, LANES), f32),
            jax.ShapeDtypeStruct((kept_own, LANES), f32),
            jax.ShapeDtypeStruct((8, LANES), f32),
            jax.ShapeDtypeStruct((8, LANES), f32),
            jax.ShapeDtypeStruct((8, cols), f32),
        ),
        in_specs=vmem(5) + [pl.BlockSpec(memory_space=pltpu.SMEM)],
        out_specs=tuple(vmem(9)),
        scratch_shapes=scores(kept_own // 2, tokens + kept_own),
        compiler_params=params(),
        cost_estimate=work(kept_own, tokens + kept_own),
        name="begin",
    )(enc_own, text_key, text_value, mask_value, norm_gain, timesteps)
    own_keys, own_values, own_queries, text_dec, sums, top = begun
    dec_values = pl.pallas_call(
        functools.partial(encode_kernel, slots, tokens),
        out_shape=jax.ShapeDtypeStruct((tokens + 2 * dec_own, LANES), bf16),
        in_specs=vmem(7),
        out_specs=vmem(1)[0],
        scratch_shapes=[pltpu.VMEM((kept_own, LANES), bf16)] * 3 + scores(kept_own // 2, tokens + 2 * kept_own),
        compiler_params=params(),
        cost_estimate=work(2 * kept_own, tokens + 2 * kept_own),
        name="encode",
    )(enc_pair, own_keys, own_values, own_queries, sums, top, fill)
    out = pl.pallas_call(
        functools.partial(decode_kernel, tokens),
        out_shape=jax.ShapeDtypeStruct((chips, tokens // 2, LANES), bf16),
        in_specs=vmem(4),
        out_specs=vmem(1)[0],
        scratch_shapes=scores(2 * tokens, tokens + 2 * dec_own),
        compiler_params=params(),
        name="decode",
    )(dec_blocks.reshape(dec_own, LANES), dec_pair.reshape(dec_own, LANES), text_dec, dec_values)
    got = lax.all_to_all(out, "seq", 0, 0, axis_index_groups=rings, tiled=True)
    att, sums = pl.pallas_call(
        sums_kernel,
        out_shape=(
            jax.ShapeDtypeStruct((tokens, cols), f32),
            jax.ShapeDtypeStruct((chips * heads, 4, tokens), f32),
        ),
        in_specs=vmem(4),
        out_specs=tuple(vmem(2)),
        compiler_params=params(),
        name="sums",
    )(got, gain, target, weight)
    planes = [
        [(2 * chip + core) * heads + head for chip in range(chips) for head in range(heads)] for core in range(2)
    ]
    sums = lax.all_to_all(sums, ("seq", "head"), 0, 0, axis_index_groups=planes, tiled=True)
    loss = pl.pallas_call(
        functools.partial(loss_kernel, heads, cols * heads),
        out_shape=jax.ShapeDtypeStruct((2 * images, 1, LANES), f32),
        in_specs=vmem(1),
        out_specs=vmem(1)[0],
        compiler_params=params(),
        name="loss",
    )(sums)
    columns = [
        [image * seq + 2 * chip + core for image in range(images) for core in range(2)] for chip in range(chips)
    ]
    got = lax.all_to_all(loss, ("dp", "seq"), 0, 0, axis_index_groups=columns, tiled=True)
    decoded, loss = pl.pallas_call(
        functools.partial(finish_kernel, heads, float(images * tokens * seq * cols * heads)),
        out_shape=(
            jax.ShapeDtypeStruct((1, tokens, cols), bf16),
            jax.ShapeDtypeStruct((1, 1), f32),
        ),
        in_specs=vmem(4),
        out_specs=tuple(vmem(2)),
        compiler_params=params(),
        name="finish",
    )(att, gain, sums, got)
    total_loss = loss.reshape(())
    return (decoded, total_loss)


def solution(mesh):
    placed = (
        P("dp", "seq", "head"),
        P("dp", "seq", "head"),
        P("dp", "seq", "head"),
        P("dp", "seq"),
        P("dp", "seq"),
        P("dp", None, "head"),
        P("dp", None, "head"),
        P("dp", "seq", "head"),
        P("dp", "seq", "head"),
        P("head"),
        P("head"),
        P("dp", "seq", "head"),
        P("dp"),
    )
    return jax.shard_map(
        local, mesh=mesh, in_specs=placed, out_specs=(P("dp", "seq", "head"), P()), check_vma=False
    )
```

```python
import functools

import jax
import jax.numpy as jnp
from jax import lax
from jax.experimental import pallas as pl
from jax.experimental.pallas import tpu as pltpu
from jax.sharding import PartitionSpec as P

HEAD_DIM = 64
LANES = 128
DEAD = 1024.0
DEAD_EDGE = 512.0
MIB = 1024 * 1024


def params(mib=40):
    return pltpu.CompilerParams(vmem_limit_bytes=mib * MIB)


def vmem(count):
    return [pl.BlockSpec(memory_space=pltpu.VMEM)] * count


def one_hot_dot(table, rows):
    return lax.dot_general(
        table, rows, (((1,), (0,)), ((), ())), preferred_element_type=jnp.float32
    )


def pack_kernel(
    index_hbm, eq_hbm, ek_hbm, ev_hbm, dq_hbm, dk_hbm, send_ref, *scratch
):
    *held, sems = scratch
    given = (index_hbm, eq_hbm, ek_hbm, ev_hbm, dq_hbm, dk_hbm)
    copies = [
        pltpu.make_async_copy(source, place, sems.at[number])
        for number, (source, place) in enumerate(zip(given, held))
    ]
    for copy in copies:
        copy.start()
    copies[0].wait()
    index_ref, eq_ref, ek_ref, ev_ref, dq_ref, dk_ref = held
    tokens, cols = eq_ref.shape[1:]
    slots = index_ref.shape[1]
    heads = cols // HEAD_DIM
    spare = tokens - slots
    index = jnp.broadcast_to(index_ref[...].astype(jnp.float32), (tokens, slots))
    index = jnp.transpose(index)
    token = lax.broadcasted_iota(jnp.int32, (slots, tokens), 1).astype(jnp.float32)
    slot = lax.broadcasted_iota(jnp.int32, (slots, tokens), 0)
    live = (slot == 0) | (index > 0.5)
    match_live = jnp.where(live & (token == index), 1.0, 0.0)
    match_fill = jnp.where(token == jnp.where(live, index, index[0:1, :]), 1.0, 0.0)
    kept = jnp.sum(match_live, axis=0, keepdims=True)
    kept_slot = jnp.sum(match_live * slot.astype(jnp.float32), axis=0, keepdims=True)
    row = lax.broadcasted_iota(jnp.int32, (tokens, tokens), 0)
    col = lax.broadcasted_iota(jnp.int32, (tokens, tokens), 1)
    before = jnp.where(row < col, 1.0, 0.0).astype(jnp.bfloat16)
    left = jnp.broadcast_to(1.0 - kept, (16, tokens)).astype(jnp.bfloat16)
    rank = one_hot_dot(left, before)[0:1, :]
    place = jnp.where(kept > 0.5, kept_slot, jnp.sum(kept, axis=1, keepdims=True) + rank)
    order = jnp.where(row.astype(jnp.float32) == place, 1.0, 0.0).astype(jnp.bfloat16)

    scale = HEAD_DIM ** (-0.5)
    match_live = match_live.astype(jnp.bfloat16)
    match_fill = match_fill.astype(jnp.bfloat16)
    copies[1].wait()
    query = one_hot_dot(match_live, eq_ref[0]) * scale
    dead = jnp.where(live, 0.0, DEAD)
    query = query + jnp.concatenate([dead] * (cols // tokens), axis=1)
    copies[2].wait()
    key = one_hot_dot(match_fill, ek_ref[0])
    copies[3].wait()
    value = one_hot_dot(match_live, ev_ref[0])
    copies[5].wait()
    dec_key = one_hot_dot(order, dk_ref[0])
    copies[4].wait()
    dec_query = dq_ref[0].astype(jnp.float32) * scale

    def low(block, head):
        tile = block[:, (head // 2) * LANES : (head // 2 + 1) * LANES]
        return tile if head % 2 == 0 else pltpu.roll(tile, HEAD_DIM, 1)

    def high(block, head):
        tile = block[:, (head // 2) * LANES : (head // 2 + 1) * LANES]
        return tile if head % 2 == 1 else pltpu.roll(tile, HEAD_DIM, 1)

    def join(first, second):
        lane = lax.broadcasted_iota(jnp.int32, first.shape, 1)
        return jnp.where(lane < HEAD_DIM, first, second).astype(jnp.bfloat16)

    for head in range(heads):
        kept_tile = join(low(value, head), high(key, head))
        query_high = high(query, head)
        dec_low = low(dec_key, head)
        dq_low = low(dec_query, head)
        dq_high = high(dec_query, head)
        send_ref[head, 0:slots, :] = kept_tile
        send_ref[head, slots : 2 * slots, :] = join(dec_low[0:slots], query_high)
        send_ref[head, 2 * slots : slots + tokens, :] = join(dec_low[slots:tokens], dq_high[0:spare])
        rest = slots // 2
        send_ref[head, slots + tokens : slots + tokens + rest, :] = join(
            dq_low[spare : spare + rest], dq_high[spare + rest : tokens]
        )


def put_scores(query, key_refs, place, peak):
    rows = query.shape[0]
    largest = None
    column = 0
    for key_ref in key_refs:
        keys = key_ref.shape[0]
        for first in range(0, keys, 2 * LANES):
            last = min(keys, first + 2 * LANES)
            part = lax.dot_general(
                query, key_ref[first:last, :], (((1,), (1,)), ((), ())), preferred_element_type=jnp.float32
            )
            place[0:rows, column : column + last - first] = part
            column += last - first
            for lane in range(0, last - first, LANES):
                tile = part[:, lane : lane + LANES]
                largest = tile if largest is None else jnp.maximum(largest, tile)
    peak[0:rows, :] = largest


def weigh(rows, place, peak, value_refs, earlier):
    top = jnp.max(peak[0:rows, :], axis=1, keepdims=True)
    sums = None
    if earlier is not None:
        earlier_sums, earlier_top = earlier
        top = jnp.maximum(top, earlier_top[:, 0:1])
        sums = earlier_sums * jnp.exp(earlier_top - top)
    column = 0
    for value_ref in value_refs:
        keys = value_ref.shape[0]
        weights = jnp.exp(place[0:rows, column : column + keys] - top).astype(jnp.bfloat16)
        column += keys
        part = lax.dot_general(
            weights, value_ref[...], (((1,), (0,)), ((), ())), preferred_element_type=jnp.float32
        )
        sums = part if sums is None else sums + part
    return top, sums


def run_jobs(jobs, buffers):
    def put(number):
        query, key_refs, _, _, _ = jobs[number]
        put_scores(query(), key_refs, *buffers[number % 2])

    put(0)
    for number, (query, _, value_refs, earlier, use) in enumerate(jobs):
        if number + 1 < len(jobs):
            put(number + 1)
        place, peak = buffers[number % 2]
        rows = query().shape[0]
        use(*weigh(rows, place, peak, value_refs, None if earlier is None else earlier()))


def lane_of(rows):
    return lax.broadcasted_iota(jnp.int32, (rows, LANES), 1)


def unpack(slots, tokens, got, block, first_key, first_dec, ek_ref, ev_ref, eq_ref, dk_ref):
    kept = got[0:slots, :]
    mixed = got[slots : 2 * slots, :].astype(jnp.float32)
    low = lane_of(slots) < HEAD_DIM
    base = first_key + block * slots
    ek_ref[base : base + slots, :] = kept
    ev_ref[base : base + slots, :] = jnp.where(
        low, kept.astype(jnp.float32), jnp.where(mixed < DEAD_EDGE, 1.0, 0.0)
    ).astype(jnp.bfloat16)
    eq_ref[block * slots : block * slots + slots, :] = jnp.where(low, 0.0, mixed).astype(jnp.bfloat16)
    base = first_dec + block * tokens
    dk_ref[base : base + tokens, :] = got[slots : slots + tokens, :]


def begin_kernel(
    slots,
    tokens,
    own_ref,
    text_key_ref,
    text_value_ref,
    mask_ref,
    gain_ref,
    steps_ref,
    ek_ref,
    ev_ref,
    eq_ref,
    dk_ref,
    dq_ref,
    sums_ref,
    top_ref,
    fill_ref,
    weight_ref,
    wide_gain_ref,
    *places
):
    chips = own_ref.shape[0]
    cols = text_key_ref.shape[2]
    spare = tokens - slots
    rest = slots // 2
    head = jnp.minimum(lax.axis_index("seq") // 2, cols // HEAD_DIM - 1)
    odd = lax.rem(head, 2) == 1
    lanes = pl.ds(pl.multiple_of((head // 2) * LANES, LANES), LANES)

    def low_high(rows):
        turned = pltpu.roll(rows, HEAD_DIM, 1)
        return jnp.where(odd, turned, rows), jnp.where(odd, rows, turned)

    key_low, key_high = low_high(text_key_ref[0, :, lanes].astype(jnp.float32))
    value_low, _ = low_high(text_value_ref[0, :, lanes].astype(jnp.float32))
    mask_row = jnp.zeros((1, LANES), jnp.float32)
    whole = mask_ref[...].astype(jnp.float32).reshape(1, cols)
    for tile in range(cols // LANES):
        mask_row = jnp.where(head // 2 == tile, whole[:, tile * LANES : (tile + 1) * LANES], mask_row)
    mask_row, _ = low_high(jnp.broadcast_to(mask_row, (8, LANES)))
    steps = jnp.full((8, LANES), steps_ref[0], jnp.int32).astype(jnp.float32)
    weight_ref[...] = 1.0 / (0.1 + steps / 999.0)
    wide_gain_ref[...] = jnp.broadcast_to(gain_ref[...].astype(jnp.float32).reshape(1, cols), (8, cols))
    low = lane_of(tokens) < HEAD_DIM
    fill_ref[...] = jnp.where(lane_of(8) < HEAD_DIM, mask_row, 1.0)
    ek_ref[0:tokens, :] = jnp.where(low, value_low, key_high).astype(jnp.bfloat16)
    ev_ref[0:tokens, :] = jnp.where(low, value_low, 1.0).astype(jnp.bfloat16)
    dk_ref[0:tokens, :] = key_low.astype(jnp.bfloat16)
    for block in range(chips):
        got = own_ref.at[block]
        unpack(slots, tokens, got, block, tokens, tokens, ek_ref, ev_ref, eq_ref, dk_ref)
        tail = got[2 * slots : slots + tokens, :].astype(jnp.float32)
        last = got[slots + tokens : slots + tokens + rest, :].astype(jnp.float32)
        base = block * tokens
        dq_ref[base : base + spare, :] = jnp.where(
            lane_of(spare) < HEAD_DIM, pltpu.roll(tail, HEAD_DIM, 1), 0.0
        ).astype(jnp.bfloat16)
        low_rest = lane_of(rest) < HEAD_DIM
        dq_ref[base + spare : base + spare + rest, :] = jnp.where(low_rest, last, 0.0).astype(jnp.bfloat16)
        dq_ref[base + spare + rest : base + tokens, :] = jnp.where(
            low_rest, pltpu.roll(last, HEAD_DIM, 1), 0.0
        ).astype(jnp.bfloat16)

    rows = chips // 2 * slots

    def job(tile):
        span = slice(tile * rows, (tile + 1) * rows)

        def use(top, sums):
            sums_ref[span, :] = sums
            top_ref[span, :] = jnp.broadcast_to(top, (rows, LANES))

        return (lambda: eq_ref[span, :], [ek_ref], [ev_ref], None, use)

    run_jobs([job(tile) for tile in range(2)], (places[0:2], places[2:4]))


def attend_kernel(
    slots,
    tokens,
    pair_ref,
    ek_ref,
    ev_ref,
    eq_ref,
    dk_ref,
    dq_ref,
    sums_ref,
    top_ref,
    fill_ref,
    out_ref,
    pair_ek_ref,
    pair_ev_ref,
    pair_eq_ref,
    pair_dk_ref,
    dv_ref,
    *places
):
    chips = pair_ref.shape[0]
    spare = tokens - slots
    for block in range(chips):
        unpack(
            slots, tokens, pair_ref.at[block], block, 0, 0, pair_ek_ref, pair_ev_ref, pair_eq_ref, pair_dk_ref
        )
    dv_ref[0:tokens, :] = ev_ref[0:tokens, :]
    mask_row = fill_ref[0:1, :]
    fill = jnp.broadcast_to(mask_row, (spare, LANES)).astype(jnp.bfloat16)
    group = chips // 2
    rows = group * slots

    def encode(tile, query_ref, first_block, key_refs, value_refs, earlier):
        span = slice(tile * rows, (tile + 1) * rows)

        def use(top, sums):
            found = sums / pltpu.roll(sums, HEAD_DIM, 1)
            for inner in range(group):
                mixed = query_ref[tile * rows + inner * slots : tile * rows + (inner + 1) * slots, :]
                live = pltpu.roll(mixed.astype(jnp.float32), HEAD_DIM, 1) < DEAD_EDGE
                base = tokens + (first_block + tile * group + inner) * tokens
                dv_ref[base : base + slots, :] = jnp.where(
                    (lane_of(slots) < HEAD_DIM) & live, found[inner * slots : (inner + 1) * slots, :], mask_row
                ).astype(jnp.bfloat16)
                dv_ref[base + slots : base + tokens, :] = fill

        before = (lambda: (sums_ref[span, :], top_ref[span, :])) if earlier else None
        return (lambda: query_ref[span, :], key_refs, value_refs, before, use)

    dec_group = 2
    half = tokens // 2

    def decode(block, count):
        def use(top, sums):
            found = sums / pltpu.roll(sums, HEAD_DIM, 1)
            for inner in range(count):
                first = inner * tokens
                out_ref[block + inner] = jnp.where(
                    lane_of(half) < HEAD_DIM,
                    found[first : first + half],
                    pltpu.roll(found[first + half : first + tokens], HEAD_DIM, 1),
                ).astype(jnp.bfloat16)

        span = slice(block * tokens, (block + count) * tokens)
        return (lambda: dq_ref[span, :], [dk_ref, pair_dk_ref], [dv_ref], None, use)

    jobs = [encode(tile, eq_ref, 0, [pair_ek_ref], [pair_ev_ref], True) for tile in range(2)]
    jobs += [
        encode(tile, pair_eq_ref, chips, [ek_ref, pair_ek_ref], [ev_ref, pair_ev_ref], False) for tile in range(2)
    ]
    jobs += [decode(block, dec_group) for block in range(0, chips - dec_group, dec_group)]
    jobs += [decode(block, 1) for block in range(chips - dec_group, chips)]
    run_jobs(jobs, (places[0:2], places[2:4]))


def sums_kernel(got_ref, gain_ref, target_ref, weight_ref, att_ref, sums_ref):
    tokens, cols = att_ref.shape
    half = tokens // 2
    low = lax.broadcasted_iota(jnp.int32, (half, LANES), 1) < HEAD_DIM
    for tile in range(cols // LANES):
        even = got_ref[2 * tile].astype(jnp.float32)
        odd = got_ref[2 * tile + 1].astype(jnp.float32)
        span = slice(tile * LANES, (tile + 1) * LANES)
        att_ref[0:half, span] = jnp.where(low, even, pltpu.roll(odd, HEAD_DIM, 1))
        att_ref[half:tokens, span] = jnp.where(low, pltpu.roll(even, HEAD_DIM, 1), odd)
    att = att_ref[...]
    gained = att * gain_ref[0:1, :]
    target = target_ref[0].astype(jnp.float32)
    weight = weight_ref[0:1, :]
    lane = lax.broadcasted_iota(jnp.int32, (tokens, LANES), 1)

    def over(block):
        return jnp.sum(block, axis=1, keepdims=True)

    table = jnp.where(
        lane == 1,
        over(gained * gained),
        jnp.where(lane == 2, over(gained * target), over(target * target)),
    )
    table = jnp.where(lane == 0, over(att * att), table * weight)
    sums_ref[...] = jnp.broadcast_to(jnp.transpose(table)[None, 0:4, :], sums_ref.shape)


def loss_kernel(heads, total_cols, sums_ref, loss_ref):
    total = None
    for chip in range(sums_ref.shape[0] // heads):
        sums = jnp.sum(sums_ref[chip * heads : (chip + 1) * heads], axis=0)
        factor = lax.rsqrt(sums[0:1, :] / total_cols + 1e-06)
        error = factor * factor * sums[1:2, :] - 2.0 * factor * sums[2:3, :] + sums[3:4, :]
        total = error if total is None else total + error
    loss_ref[...] = jnp.broadcast_to(jnp.sum(total, axis=1, keepdims=True)[None], loss_ref.shape)


def finish_kernel(heads, count, att_ref, gain_ref, sums_ref, got_ref, out_ref, loss_ref, done_ref, sems):
    tokens, cols = att_ref.shape
    own = jnp.sum(sums_ref[pl.ds(lax.axis_index("seq") // 2 * heads, heads)], axis=0)
    factor = lax.rsqrt(own[0:1, :] / (cols * heads) + 1e-06)
    column = jnp.transpose(jnp.broadcast_to(factor, (tokens, tokens)))[:, 0:1]
    half = tokens // 2
    copies = []
    for part in range(2):
        span = slice(part * half, (part + 1) * half)
        done_ref[span, :] = (att_ref[span, :] * column[span] * gain_ref[0:1, :]).astype(jnp.bfloat16)
        copies.append(pltpu.make_async_copy(done_ref.at[span], out_ref.at[0, span], sems.at[part]))
        copies[-1].start()
    loss_ref[...] = (jnp.sum(got_ref[...], axis=0) / count)[0:1, 0:1]
    for copy in copies:
        copy.wait()


def local(
    enc_query,
    enc_key,
    enc_value,
    keep_index,
    keep_count,
    text_key,
    text_value,
    dec_query,
    dec_key,
    mask_value,
    norm_gain,
    target,
    timesteps,
):
    images, seq, heads = (lax.axis_size(name) for name in ("dp", "seq", "head"))
    tokens, cols = enc_query.shape[1:]
    slots = keep_index.shape[1]
    local_heads = cols // HEAD_DIM
    chips = seq // 2
    packed = slots + tokens + slots // 2
    same_core = [[2 * chip + core for chip in range(chips)] for core in range(2)]
    bf16, f32 = jnp.bfloat16, jnp.float32

    send = pl.pallas_call(
        pack_kernel,
        out_shape=jax.ShapeDtypeStruct((chips, packed, LANES), bf16),
        in_specs=[pl.BlockSpec(memory_space=pltpu.HBM)] * 6,
        out_specs=vmem(1)[0],
        scratch_shapes=[pltpu.VMEM((1, slots), jnp.int32)]
        + [pltpu.VMEM((1, tokens, cols), bf16)] * 5
        + [pltpu.SemaphoreType.DMA((6,))],
        compiler_params=params(60),
        name="pack",
    )(keep_index, enc_query, enc_key, enc_value, dec_query, dec_key)
    own = lax.all_to_all(send, "seq", 0, 0, axis_index_groups=same_core, tiled=True)
    pair = lax.ppermute(own, "seq", [(source, source ^ 1) for source in range(seq)])
    kept_own = chips * slots
    dec_own = chips * tokens
    *begun, weight, gain = pl.pallas_call(
        functools.partial(begin_kernel, slots, tokens),
        out_shape=(
            jax.ShapeDtypeStruct((tokens + kept_own, LANES), bf16),
            jax.ShapeDtypeStruct((tokens + kept_own, LANES), bf16),
            jax.ShapeDtypeStruct((kept_own, LANES), bf16),
            jax.ShapeDtypeStruct((tokens + dec_own, LANES), bf16),
            jax.ShapeDtypeStruct((dec_own, LANES), bf16),
            jax.ShapeDtypeStruct((kept_own, LANES), f32),
            jax.ShapeDtypeStruct((kept_own, LANES), f32),
            jax.ShapeDtypeStruct((8, LANES), f32),
            jax.ShapeDtypeStruct((8, LANES), f32),
            jax.ShapeDtypeStruct((8, cols), f32),
        ),
        in_specs=vmem(5) + [pl.BlockSpec(memory_space=pltpu.SMEM)],
        out_specs=tuple(vmem(10)),
        scratch_shapes=[
            pltpu.VMEM((kept_own // 2, tokens + kept_own), f32),
            pltpu.VMEM((kept_own // 2, LANES), f32),
        ]
        * 2,
        compiler_params=params(),
        cost_estimate=pl.CostEstimate(
            flops=4 * kept_own * (tokens + kept_own) * LANES,
            bytes_accessed=8 * MIB,
            transcendentals=kept_own * (tokens + kept_own),
        ),
        name="begin",
    )(own, text_key, text_value, mask_value, norm_gain, timesteps)
    out = pl.pallas_call(
        functools.partial(attend_kernel, slots, tokens),
        out_shape=jax.ShapeDtypeStruct((chips, tokens // 2, LANES), bf16),
        in_specs=vmem(9),
        out_specs=vmem(1)[0],
        scratch_shapes=[
            pltpu.VMEM((kept_own, LANES), bf16),
            pltpu.VMEM((kept_own, LANES), bf16),
            pltpu.VMEM((kept_own, LANES), bf16),
            pltpu.VMEM((dec_own, LANES), bf16),
            pltpu.VMEM((tokens + 2 * dec_own, LANES), bf16),
        ]
        + [
            pltpu.VMEM((kept_own // 2, tokens + 2 * dec_own), f32),
            pltpu.VMEM((kept_own // 2, LANES), f32),
        ]
        * 2,
        compiler_params=params(),
        name="attend",
    )(pair, *begun)
    got = lax.all_to_all(out, "seq", 0, 0, axis_index_groups=same_core, tiled=True)
    att, sums = pl.pallas_call(
        sums_kernel,
        out_shape=(
            jax.ShapeDtypeStruct((tokens, cols), f32),
            jax.ShapeDtypeStruct((chips * heads, 4, tokens), f32),
        ),
        in_specs=vmem(4),
        out_specs=tuple(vmem(2)),
        compiler_params=params(),
        name="sums",
    )(got, gain, target, weight)
    planes = [
        [(2 * chip + core) * heads + head for chip in range(chips) for head in range(heads)] for core in range(2)
    ]
    sums = lax.all_to_all(sums, ("seq", "head"), 0, 0, axis_index_groups=planes, tiled=True)
    loss = pl.pallas_call(
        functools.partial(loss_kernel, heads, cols * heads),
        out_shape=jax.ShapeDtypeStruct((2 * images, 1, LANES), f32),
        in_specs=vmem(1),
        out_specs=vmem(1)[0],
        compiler_params=params(),
        name="loss",
    )(sums)
    columns = [
        [image * seq + 2 * chip + core for image in range(images) for core in range(2)] for chip in range(chips)
    ]
    got = lax.all_to_all(loss, ("dp", "seq"), 0, 0, axis_index_groups=columns, tiled=True)
    decoded, loss = pl.pallas_call(
        functools.partial(finish_kernel, heads, float(images * tokens * seq * cols * heads)),
        out_shape=(
            jax.ShapeDtypeStruct((1, tokens, cols), bf16),
            jax.ShapeDtypeStruct((1, 1), f32),
        ),
        in_specs=vmem(4),
        out_specs=(pl.BlockSpec(memory_space=pltpu.HBM), pl.BlockSpec(memory_space=pltpu.VMEM)),
        scratch_shapes=[pltpu.VMEM((tokens, cols), bf16), pltpu.SemaphoreType.DMA((2,))],
        compiler_params=params(),
        name="finish",
    )(att, gain, sums, got)
    total_loss = loss.reshape(())
    return (decoded, total_loss)


def solution(mesh):
    placed = (
        P("dp", "seq", "head"),
        P("dp", "seq", "head"),
        P("dp", "seq", "head"),
        P("dp", "seq"),
        P("dp", "seq"),
        P("dp", None, "head"),
        P("dp", None, "head"),
        P("dp", "seq", "head"),
        P("dp", "seq", "head"),
        P("head"),
        P("head"),
        P("dp", "seq", "head"),
        P("dp"),
    )
    return jax.shard_map(
        local, mesh=mesh, in_specs=placed, out_specs=(P("dp", "seq", "head"), P()), check_vma=False
    )
```

```python
import functools

import jax
import jax.numpy as jnp
from jax import lax
from jax.experimental import pallas as pl
from jax.experimental.pallas import tpu as pltpu
from jax.sharding import PartitionSpec as P

HEAD_DIM = 64
LANES = 128
DEAD = 1024.0
DEAD_EDGE = 512.0
MIB = 1024 * 1024


def params(mib=40):
    return pltpu.CompilerParams(vmem_limit_bytes=mib * MIB)


def vmem(count):
    return [pl.BlockSpec(memory_space=pltpu.VMEM)] * count


def one_hot_dot(table, rows):
    return lax.dot_general(
        table, rows, (((1,), (0,)), ((), ())), preferred_element_type=jnp.float32
    )


def pack_kernel(index_ref, eq_ref, ek_ref, ev_ref, dq_ref, dk_ref, send_ref):
    tokens, cols = eq_ref.shape[1:]
    slots = index_ref.shape[1]
    heads = cols // HEAD_DIM
    spare = tokens - slots
    index = jnp.broadcast_to(index_ref[...].astype(jnp.float32), (tokens, slots))
    index = jnp.transpose(index)
    token = lax.broadcasted_iota(jnp.int32, (slots, tokens), 1).astype(jnp.float32)
    slot = lax.broadcasted_iota(jnp.int32, (slots, tokens), 0)
    live = (slot == 0) | (index > 0.5)
    match_live = jnp.where(live & (token == index), 1.0, 0.0)
    match_fill = jnp.where(token == jnp.where(live, index, index[0:1, :]), 1.0, 0.0)
    kept = jnp.sum(match_live, axis=0, keepdims=True)
    kept_slot = jnp.sum(match_live * slot.astype(jnp.float32), axis=0, keepdims=True)
    row = lax.broadcasted_iota(jnp.int32, (tokens, tokens), 0)
    col = lax.broadcasted_iota(jnp.int32, (tokens, tokens), 1)
    before = jnp.where(row < col, 1.0, 0.0).astype(jnp.bfloat16)
    left = jnp.broadcast_to(1.0 - kept, (16, tokens)).astype(jnp.bfloat16)
    rank = one_hot_dot(left, before)[0:1, :]
    place = jnp.where(kept > 0.5, kept_slot, jnp.sum(kept, axis=1, keepdims=True) + rank)
    order = jnp.where(row.astype(jnp.float32) == place, 1.0, 0.0).astype(jnp.bfloat16)

    scale = HEAD_DIM ** (-0.5)
    match_live = match_live.astype(jnp.bfloat16)
    match_fill = match_fill.astype(jnp.bfloat16)
    query = one_hot_dot(match_live, eq_ref[0]) * scale
    dead = jnp.where(live, 0.0, DEAD)
    query = query + jnp.concatenate([dead] * (cols // tokens), axis=1)
    key = one_hot_dot(match_fill, ek_ref[0])
    value = one_hot_dot(match_live, ev_ref[0])
    dec_key = one_hot_dot(order, dk_ref[0])
    dec_query = dq_ref[0].astype(jnp.float32) * scale

    def low(block, head):
        tile = block[:, (head // 2) * LANES : (head // 2 + 1) * LANES]
        return tile if head % 2 == 0 else pltpu.roll(tile, HEAD_DIM, 1)

    def high(block, head):
        tile = block[:, (head // 2) * LANES : (head // 2 + 1) * LANES]
        return tile if head % 2 == 1 else pltpu.roll(tile, HEAD_DIM, 1)

    def join(first, second):
        lane = lax.broadcasted_iota(jnp.int32, first.shape, 1)
        return jnp.where(lane < HEAD_DIM, first, second).astype(jnp.bfloat16)

    for head in range(heads):
        kept_tile = join(low(value, head), high(key, head))
        query_high = high(query, head)
        dec_low = low(dec_key, head)
        dq_low = low(dec_query, head)
        dq_high = high(dec_query, head)
        send_ref[head, 0:slots, :] = kept_tile
        send_ref[head, slots : 2 * slots, :] = join(dec_low[0:slots], query_high)
        send_ref[head, 2 * slots : slots + tokens, :] = join(dec_low[slots:tokens], dq_high[0:spare])
        rest = slots // 2
        send_ref[head, slots + tokens : slots + tokens + rest, :] = join(
            dq_low[spare : spare + rest], dq_high[spare + rest : tokens]
        )


def put_scores(query, key_refs, place, peak):
    rows = query.shape[0]
    largest = None
    column = 0
    for key_ref in key_refs:
        keys = key_ref.shape[0]
        for first in range(0, keys, 2 * LANES):
            last = min(keys, first + 2 * LANES)
            part = lax.dot_general(
                query, key_ref[first:last, :], (((1,), (1,)), ((), ())), preferred_element_type=jnp.float32
            )
            place[0:rows, column : column + last - first] = part
            column += last - first
            for lane in range(0, last - first, LANES):
                tile = part[:, lane : lane + LANES]
                largest = tile if largest is None else jnp.maximum(largest, tile)
    peak[0:rows, :] = largest


def weigh(rows, place, peak, value_refs, earlier):
    top = jnp.max(peak[0:rows, :], axis=1, keepdims=True)
    sums = None
    if earlier is not None:
        earlier_sums, earlier_top = earlier
        top = jnp.maximum(top, earlier_top[:, 0:1])
        sums = earlier_sums * jnp.exp(earlier_top - top)
    column = 0
    for value_ref in value_refs:
        keys = value_ref.shape[0]
        weights = jnp.exp(place[0:rows, column : column + keys] - top).astype(jnp.bfloat16)
        column += keys
        part = lax.dot_general(
            weights, value_ref[...], (((1,), (0,)), ((), ())), preferred_element_type=jnp.float32
        )
        sums = part if sums is None else sums + part
    return top, sums


def run_jobs(jobs, buffers):
    def put(number):
        query, key_refs, _, _, _ = jobs[number]
        put_scores(query(), key_refs, *buffers[number % 2])

    put(0)
    for number, (query, _, value_refs, earlier, use) in enumerate(jobs):
        if number + 1 < len(jobs):
            put(number + 1)
        place, peak = buffers[number % 2]
        rows = query().shape[0]
        use(*weigh(rows, place, peak, value_refs, None if earlier is None else earlier()))


def lane_of(rows):
    return lax.broadcasted_iota(jnp.int32, (rows, LANES), 1)


def unpack(slots, tokens, got, block, first_key, first_dec, ek_ref, ev_ref, eq_ref, dk_ref):
    kept = got[0:slots, :]
    mixed = got[slots : 2 * slots, :].astype(jnp.float32)
    low = lane_of(slots) < HEAD_DIM
    base = first_key + block * slots
    ek_ref[base : base + slots, :] = kept
    ev_ref[base : base + slots, :] = jnp.where(
        low, kept.astype(jnp.float32), jnp.where(mixed < DEAD_EDGE, 1.0, 0.0)
    ).astype(jnp.bfloat16)
    eq_ref[block * slots : block * slots + slots, :] = jnp.where(low, 0.0, mixed).astype(jnp.bfloat16)
    base = first_dec + block * tokens
    dk_ref[base : base + tokens, :] = got[slots : slots + tokens, :]


def begin_kernel(
    slots,
    tokens,
    own_ref,
    text_key_ref,
    text_value_ref,
    mask_ref,
    gain_ref,
    steps_ref,
    ek_ref,
    ev_ref,
    eq_ref,
    dk_ref,
    dq_ref,
    sums_ref,
    top_ref,
    fill_ref,
    weight_ref,
    wide_gain_ref,
    *places
):
    chips = own_ref.shape[0]
    cols = text_key_ref.shape[2]
    spare = tokens - slots
    rest = slots // 2
    head = jnp.minimum(lax.axis_index("seq") // 2, cols // HEAD_DIM - 1)
    odd = lax.rem(head, 2) == 1
    lanes = pl.ds(pl.multiple_of((head // 2) * LANES, LANES), LANES)

    def low_high(rows):
        turned = pltpu.roll(rows, HEAD_DIM, 1)
        return jnp.where(odd, turned, rows), jnp.where(odd, rows, turned)

    key_low, key_high = low_high(text_key_ref[0, :, lanes].astype(jnp.float32))
    value_low, _ = low_high(text_value_ref[0, :, lanes].astype(jnp.float32))
    mask_row = jnp.zeros((1, LANES), jnp.float32)
    whole = mask_ref[...].astype(jnp.float32).reshape(1, cols)
    for tile in range(cols // LANES):
        mask_row = jnp.where(head // 2 == tile, whole[:, tile * LANES : (tile + 1) * LANES], mask_row)
    mask_row, _ = low_high(jnp.broadcast_to(mask_row, (8, LANES)))
    steps = jnp.full((8, LANES), steps_ref[0], jnp.int32).astype(jnp.float32)
    weight_ref[...] = 1.0 / (0.1 + steps / 999.0)
    wide_gain_ref[...] = jnp.broadcast_to(gain_ref[...].astype(jnp.float32).reshape(1, cols), (8, cols))
    low = lane_of(tokens) < HEAD_DIM
    fill_ref[...] = jnp.where(lane_of(8) < HEAD_DIM, mask_row, 1.0)
    ek_ref[0:tokens, :] = jnp.where(low, value_low, key_high).astype(jnp.bfloat16)
    ev_ref[0:tokens, :] = jnp.where(low, value_low, 1.0).astype(jnp.bfloat16)
    dk_ref[0:tokens, :] = key_low.astype(jnp.bfloat16)
    for block in range(chips):
        got = own_ref.at[block]
        unpack(slots, tokens, got, block, tokens, tokens, ek_ref, ev_ref, eq_ref, dk_ref)
        tail = got[2 * slots : slots + tokens, :].astype(jnp.float32)
        last = got[slots + tokens : slots + tokens + rest, :].astype(jnp.float32)
        base = block * tokens
        dq_ref[base : base + spare, :] = jnp.where(
            lane_of(spare) < HEAD_DIM, pltpu.roll(tail, HEAD_DIM, 1), 0.0
        ).astype(jnp.bfloat16)
        low_rest = lane_of(rest) < HEAD_DIM
        dq_ref[base + spare : base + spare + rest, :] = jnp.where(low_rest, last, 0.0).astype(jnp.bfloat16)
        dq_ref[base + spare + rest : base + tokens, :] = jnp.where(
            low_rest, pltpu.roll(last, HEAD_DIM, 1), 0.0
        ).astype(jnp.bfloat16)

    rows = chips // 2 * slots

    def job(tile):
        span = slice(tile * rows, (tile + 1) * rows)

        def use(top, sums):
            sums_ref[span, :] = sums
            top_ref[span, :] = jnp.broadcast_to(top, (rows, LANES))

        return (lambda: eq_ref[span, :], [ek_ref], [ev_ref], None, use)

    run_jobs([job(tile) for tile in range(2)], (places[0:2], places[2:4]))


def attend_kernel(
    slots,
    tokens,
    pair_ref,
    ek_ref,
    ev_ref,
    eq_ref,
    dk_ref,
    dq_ref,
    sums_ref,
    top_ref,
    fill_ref,
    out_ref,
    pair_ek_ref,
    pair_ev_ref,
    pair_eq_ref,
    pair_dk_ref,
    dv_ref,
    *places
):
    chips = pair_ref.shape[0]
    spare = tokens - slots
    for block in range(chips):
        unpack(
            slots, tokens, pair_ref.at[block], block, 0, 0, pair_ek_ref, pair_ev_ref, pair_eq_ref, pair_dk_ref
        )
    dv_ref[0:tokens, :] = ev_ref[0:tokens, :]
    mask_row = fill_ref[0:1, :]
    fill = jnp.broadcast_to(mask_row, (spare, LANES)).astype(jnp.bfloat16)
    group = chips // 2
    rows = group * slots

    def encode(tile, query_ref, first_block, key_refs, value_refs, earlier):
        span = slice(tile * rows, (tile + 1) * rows)

        def use(top, sums):
            found = sums / pltpu.roll(sums, HEAD_DIM, 1)
            for inner in range(group):
                mixed = query_ref[tile * rows + inner * slots : tile * rows + (inner + 1) * slots, :]
                live = pltpu.roll(mixed.astype(jnp.float32), HEAD_DIM, 1) < DEAD_EDGE
                base = tokens + (first_block + tile * group + inner) * tokens
                dv_ref[base : base + slots, :] = jnp.where(
                    (lane_of(slots) < HEAD_DIM) & live, found[inner * slots : (inner + 1) * slots, :], mask_row
                ).astype(jnp.bfloat16)
                dv_ref[base + slots : base + tokens, :] = fill

        before = (lambda: (sums_ref[span, :], top_ref[span, :])) if earlier else None
        return (lambda: query_ref[span, :], key_refs, value_refs, before, use)

    dec_group = 2
    dec_rows = dec_group * tokens
    half = tokens // 2

    def decode(tile):
        def use(top, sums):
            found = sums / pltpu.roll(sums, HEAD_DIM, 1)
            for inner in range(dec_group):
                first = inner * tokens
                out_ref[tile * dec_group + inner] = jnp.where(
                    lane_of(half) < HEAD_DIM,
                    found[first : first + half],
                    pltpu.roll(found[first + half : first + tokens], HEAD_DIM, 1),
                ).astype(jnp.bfloat16)

        span = slice(tile * dec_rows, (tile + 1) * dec_rows)
        return (lambda: dq_ref[span, :], [dk_ref, pair_dk_ref], [dv_ref], None, use)

    jobs = [encode(tile, eq_ref, 0, [pair_ek_ref], [pair_ev_ref], True) for tile in range(2)]
    jobs += [
        encode(tile, pair_eq_ref, chips, [ek_ref, pair_ek_ref], [ev_ref, pair_ev_ref], False) for tile in range(2)
    ]
    jobs += [decode(tile) for tile in range(chips // dec_group)]
    run_jobs(jobs, (places[0:2], places[2:4]))


def sums_kernel(got_ref, gain_ref, target_ref, weight_ref, att_ref, sums_ref):
    tokens, cols = att_ref.shape
    half = tokens // 2
    low = lax.broadcasted_iota(jnp.int32, (half, LANES), 1) < HEAD_DIM
    for tile in range(cols // LANES):
        even = got_ref[2 * tile].astype(jnp.float32)
        odd = got_ref[2 * tile + 1].astype(jnp.float32)
        span = slice(tile * LANES, (tile + 1) * LANES)
        att_ref[0:half, span] = jnp.where(low, even, pltpu.roll(odd, HEAD_DIM, 1))
        att_ref[half:tokens, span] = jnp.where(low, pltpu.roll(even, HEAD_DIM, 1), odd)
    att = att_ref[...]
    gained = att * gain_ref[0:1, :]
    target = target_ref[0].astype(jnp.float32)
    weight = weight_ref[0:1, :]
    lane = lax.broadcasted_iota(jnp.int32, (tokens, LANES), 1)

    def over(block):
        return jnp.sum(block, axis=1, keepdims=True)

    table = jnp.where(
        lane == 1,
        over(gained * gained),
        jnp.where(lane == 2, over(gained * target), over(target * target)),
    )
    table = jnp.where(lane == 0, over(att * att), table * weight)
    sums_ref[...] = jnp.broadcast_to(jnp.transpose(table)[None, 0:4, :], sums_ref.shape)


def loss_kernel(heads, total_cols, sums_ref, loss_ref):
    total = None
    for chip in range(sums_ref.shape[0] // heads):
        sums = jnp.sum(sums_ref[chip * heads : (chip + 1) * heads], axis=0)
        factor = lax.rsqrt(sums[0:1, :] / total_cols + 1e-06)
        error = factor * factor * sums[1:2, :] - 2.0 * factor * sums[2:3, :] + sums[3:4, :]
        total = error if total is None else total + error
    loss_ref[...] = jnp.broadcast_to(jnp.sum(total, axis=1, keepdims=True)[None], loss_ref.shape)


def finish_kernel(heads, count, att_ref, gain_ref, sums_ref, got_ref, out_ref, loss_ref):
    tokens, cols = att_ref.shape
    loss_ref[...] = (jnp.sum(got_ref[...], axis=0) / count)[0:1, 0:1]
    own = jnp.sum(sums_ref[pl.ds(lax.axis_index("seq") // 2 * heads, heads)], axis=0)
    factor = lax.rsqrt(own[0:1, :] / (cols * heads) + 1e-06)
    column = jnp.transpose(jnp.broadcast_to(factor, (tokens, tokens)))[:, 0:1]
    out_ref[0] = (att_ref[...] * column * gain_ref[0:1, :]).astype(jnp.bfloat16)


def local(
    enc_query,
    enc_key,
    enc_value,
    keep_index,
    keep_count,
    text_key,
    text_value,
    dec_query,
    dec_key,
    mask_value,
    norm_gain,
    target,
    timesteps,
):
    images, seq, heads = (lax.axis_size(name) for name in ("dp", "seq", "head"))
    tokens, cols = enc_query.shape[1:]
    slots = keep_index.shape[1]
    local_heads = cols // HEAD_DIM
    chips = seq // 2
    packed = slots + tokens + slots // 2
    same_core = [[2 * chip + core for chip in range(chips)] for core in range(2)]
    bf16, f32 = jnp.bfloat16, jnp.float32

    send = pl.pallas_call(
        pack_kernel,
        out_shape=jax.ShapeDtypeStruct((chips, packed, LANES), bf16),
        in_specs=vmem(6),
        out_specs=vmem(1)[0],
        compiler_params=params(60),
        name="pack",
    )(keep_index, enc_query, enc_key, enc_value, dec_query, dec_key)
    own = lax.all_to_all(send, "seq", 0, 0, axis_index_groups=same_core, tiled=True)
    pair = lax.ppermute(own, "seq", [(source, source ^ 1) for source in range(seq)])
    kept_own = chips * slots
    dec_own = chips * tokens
    *begun, weight, gain = pl.pallas_call(
        functools.partial(begin_kernel, slots, tokens),
        out_shape=(
            jax.ShapeDtypeStruct((tokens + kept_own, LANES), bf16),
            jax.ShapeDtypeStruct((tokens + kept_own, LANES), bf16),
            jax.ShapeDtypeStruct((kept_own, LANES), bf16),
            jax.ShapeDtypeStruct((tokens + dec_own, LANES), bf16),
            jax.ShapeDtypeStruct((dec_own, LANES), bf16),
            jax.ShapeDtypeStruct((kept_own, LANES), f32),
            jax.ShapeDtypeStruct((kept_own, LANES), f32),
            jax.ShapeDtypeStruct((8, LANES), f32),
            jax.ShapeDtypeStruct((8, LANES), f32),
            jax.ShapeDtypeStruct((8, cols), f32),
        ),
        in_specs=vmem(5) + [pl.BlockSpec(memory_space=pltpu.SMEM)],
        out_specs=tuple(vmem(10)),
        scratch_shapes=[
            pltpu.VMEM((kept_own // 2, tokens + kept_own), f32),
            pltpu.VMEM((kept_own // 2, LANES), f32),
        ]
        * 2,
        compiler_params=params(),
        cost_estimate=pl.CostEstimate(
            flops=4 * kept_own * (tokens + kept_own) * LANES,
            bytes_accessed=8 * MIB,
            transcendentals=kept_own * (tokens + kept_own),
        ),
        name="begin",
    )(own, text_key, text_value, mask_value, norm_gain, timesteps)
    out = pl.pallas_call(
        functools.partial(attend_kernel, slots, tokens),
        out_shape=jax.ShapeDtypeStruct((chips, tokens // 2, LANES), bf16),
        in_specs=vmem(9),
        out_specs=vmem(1)[0],
        scratch_shapes=[
            pltpu.VMEM((kept_own, LANES), bf16),
            pltpu.VMEM((kept_own, LANES), bf16),
            pltpu.VMEM((kept_own, LANES), bf16),
            pltpu.VMEM((dec_own, LANES), bf16),
            pltpu.VMEM((tokens + 2 * dec_own, LANES), bf16),
        ]
        + [
            pltpu.VMEM((kept_own // 2, tokens + 2 * dec_own), f32),
            pltpu.VMEM((kept_own // 2, LANES), f32),
        ]
        * 2,
        compiler_params=params(),
        name="attend",
    )(pair, *begun)
    got = lax.all_to_all(out, "seq", 0, 0, axis_index_groups=same_core, tiled=True)
    att, sums = pl.pallas_call(
        sums_kernel,
        out_shape=(
            jax.ShapeDtypeStruct((tokens, cols), f32),
            jax.ShapeDtypeStruct((chips * heads, 4, tokens), f32),
        ),
        in_specs=vmem(4),
        out_specs=tuple(vmem(2)),
        compiler_params=params(),
        name="sums",
    )(got, gain, target, weight)
    planes = [
        [(2 * chip + core) * heads + head for chip in range(chips) for head in range(heads)] for core in range(2)
    ]
    sums = lax.all_to_all(sums, ("seq", "head"), 0, 0, axis_index_groups=planes, tiled=True)
    loss = pl.pallas_call(
        functools.partial(loss_kernel, heads, cols * heads),
        out_shape=jax.ShapeDtypeStruct((2 * images, 1, LANES), f32),
        in_specs=vmem(1),
        out_specs=vmem(1)[0],
        compiler_params=params(),
        name="loss",
    )(sums)
    columns = [
        [image * seq + 2 * chip + core for image in range(images) for core in range(2)] for chip in range(chips)
    ]
    got = lax.all_to_all(loss, ("dp", "seq"), 0, 0, axis_index_groups=columns, tiled=True)
    decoded, loss = pl.pallas_call(
        functools.partial(finish_kernel, heads, float(images * tokens * seq * cols * heads)),
        out_shape=(
            jax.ShapeDtypeStruct((1, tokens, cols), bf16),
            jax.ShapeDtypeStruct((1, 1), f32),
        ),
        in_specs=vmem(4),
        out_specs=tuple(vmem(2)),
        compiler_params=params(),
        name="finish",
    )(att, gain, sums, got)
    total_loss = loss.reshape(())
    return (decoded, total_loss)


def solution(mesh):
    placed = (
        P("dp", "seq", "head"),
        P("dp", "seq", "head"),
        P("dp", "seq", "head"),
        P("dp", "seq"),
        P("dp", "seq"),
        P("dp", None, "head"),
        P("dp", None, "head"),
        P("dp", "seq", "head"),
        P("dp", "seq", "head"),
        P("head"),
        P("head"),
        P("dp", "seq", "head"),
        P("dp"),
    )
    return jax.shard_map(
        local, mesh=mesh, in_specs=placed, out_specs=(P("dp", "seq", "head"), P()), check_vma=False
    )
```

```python
import functools

import jax
import jax.numpy as jnp
from jax import lax
from jax.experimental import pallas as pl
from jax.experimental.pallas import tpu as pltpu
from jax.sharding import PartitionSpec as P

HEAD_DIM = 64
LANES = 128
DEAD = 1024.0
DEAD_EDGE = 512.0
MIB = 1024 * 1024


def params(mib=40):
    return pltpu.CompilerParams(vmem_limit_bytes=mib * MIB)


def vmem(count):
    return [pl.BlockSpec(memory_space=pltpu.VMEM)] * count


def one_hot_dot(table, rows):
    return lax.dot_general(
        table, rows, (((1,), (0,)), ((), ())), preferred_element_type=jnp.float32
    )


def pack_kernel(
    index_hbm, eq_hbm, ek_hbm, ev_hbm, dq_hbm, dk_hbm, send_ref, *scratch
):
    *held, sems = scratch
    given = (index_hbm, eq_hbm, ek_hbm, ev_hbm, dq_hbm, dk_hbm)
    copies = [
        pltpu.make_async_copy(source, place, sems.at[number])
        for number, (source, place) in enumerate(zip(given, held))
    ]
    for copy in copies:
        copy.start()
    copies[0].wait()
    index_ref, eq_ref, ek_ref, ev_ref, dq_ref, dk_ref = held
    tokens, cols = eq_ref.shape[1:]
    slots = index_ref.shape[1]
    heads = cols // HEAD_DIM
    spare = tokens - slots
    index = jnp.broadcast_to(index_ref[...].astype(jnp.float32), (tokens, slots))
    index = jnp.transpose(index)
    token = lax.broadcasted_iota(jnp.int32, (slots, tokens), 1).astype(jnp.float32)
    slot = lax.broadcasted_iota(jnp.int32, (slots, tokens), 0)
    live = (slot == 0) | (index > 0.5)
    match_live = jnp.where(live & (token == index), 1.0, 0.0)
    match_fill = jnp.where(token == jnp.where(live, index, index[0:1, :]), 1.0, 0.0)
    kept = jnp.sum(match_live, axis=0, keepdims=True)
    kept_slot = jnp.sum(match_live * slot.astype(jnp.float32), axis=0, keepdims=True)
    row = lax.broadcasted_iota(jnp.int32, (tokens, tokens), 0)
    col = lax.broadcasted_iota(jnp.int32, (tokens, tokens), 1)
    before = jnp.where(row < col, 1.0, 0.0).astype(jnp.bfloat16)
    left = jnp.broadcast_to(1.0 - kept, (16, tokens)).astype(jnp.bfloat16)
    rank = one_hot_dot(left, before)[0:1, :]
    place = jnp.where(kept > 0.5, kept_slot, jnp.sum(kept, axis=1, keepdims=True) + rank)
    order = jnp.where(row.astype(jnp.float32) == place, 1.0, 0.0).astype(jnp.bfloat16)

    for copy in copies[1:]:
        copy.wait()
    scale = HEAD_DIM ** (-0.5)
    match_live = match_live.astype(jnp.bfloat16)
    match_fill = match_fill.astype(jnp.bfloat16)
    query = one_hot_dot(match_live, eq_ref[0]) * scale
    dead = jnp.where(live, 0.0, DEAD)
    query = query + jnp.concatenate([dead] * (cols // tokens), axis=1)
    key = one_hot_dot(match_fill, ek_ref[0])
    value = one_hot_dot(match_live, ev_ref[0])
    dec_key = one_hot_dot(order, dk_ref[0])
    dec_query = dq_ref[0].astype(jnp.float32) * scale

    def low(block, head):
        tile = block[:, (head // 2) * LANES : (head // 2 + 1) * LANES]
        return tile if head % 2 == 0 else pltpu.roll(tile, HEAD_DIM, 1)

    def high(block, head):
        tile = block[:, (head // 2) * LANES : (head // 2 + 1) * LANES]
        return tile if head % 2 == 1 else pltpu.roll(tile, HEAD_DIM, 1)

    def join(first, second):
        lane = lax.broadcasted_iota(jnp.int32, first.shape, 1)
        return jnp.where(lane < HEAD_DIM, first, second).astype(jnp.bfloat16)

    for head in range(heads):
        kept_tile = join(low(value, head), high(key, head))
        query_high = high(query, head)
        dec_low = low(dec_key, head)
        dq_low = low(dec_query, head)
        dq_high = high(dec_query, head)
        send_ref[head, 0:slots, :] = kept_tile
        send_ref[head, slots : 2 * slots, :] = join(dec_low[0:slots], query_high)
        send_ref[head, 2 * slots : slots + tokens, :] = join(dec_low[slots:tokens], dq_high[0:spare])
        rest = slots // 2
        send_ref[head, slots + tokens : slots + tokens + rest, :] = join(
            dq_low[spare : spare + rest], dq_high[spare + rest : tokens]
        )


def put_scores(query, key_refs, place, peak):
    rows = query.shape[0]
    largest = None
    column = 0
    for key_ref in key_refs:
        keys = key_ref.shape[0]
        for first in range(0, keys, 2 * LANES):
            last = min(keys, first + 2 * LANES)
            part = lax.dot_general(
                query, key_ref[first:last, :], (((1,), (1,)), ((), ())), preferred_element_type=jnp.float32
            )
            place[0:rows, column : column + last - first] = part
            column += last - first
            for lane in range(0, last - first, LANES):
                tile = part[:, lane : lane + LANES]
                largest = tile if largest is None else jnp.maximum(largest, tile)
    peak[0:rows, :] = largest


def weigh(rows, place, peak, value_refs, earlier):
    top = jnp.max(peak[0:rows, :], axis=1, keepdims=True)
    sums = None
    if earlier is not None:
        earlier_sums, earlier_top = earlier
        top = jnp.maximum(top, earlier_top[:, 0:1])
        sums = earlier_sums * jnp.exp(earlier_top - top)
    column = 0
    for value_ref in value_refs:
        keys = value_ref.shape[0]
        weights = jnp.exp(place[0:rows, column : column + keys] - top).astype(jnp.bfloat16)
        column += keys
        part = lax.dot_general(
            weights, value_ref[...], (((1,), (0,)), ((), ())), preferred_element_type=jnp.float32
        )
        sums = part if sums is None else sums + part
    return top, sums


def run_jobs(jobs, buffers):
    def put(number):
        query, key_refs, _, _, _ = jobs[number]
        put_scores(query(), key_refs, *buffers[number % 2])

    put(0)
    for number, (query, _, value_refs, earlier, use) in enumerate(jobs):
        if number + 1 < len(jobs):
            put(number + 1)
        place, peak = buffers[number % 2]
        rows = query().shape[0]
        use(*weigh(rows, place, peak, value_refs, None if earlier is None else earlier()))


def lane_of(rows):
    return lax.broadcasted_iota(jnp.int32, (rows, LANES), 1)


def unpack(slots, tokens, got, block, first_key, first_dec, ek_ref, ev_ref, eq_ref, dk_ref):
    kept = got[0:slots, :]
    mixed = got[slots : 2 * slots, :].astype(jnp.float32)
    low = lane_of(slots) < HEAD_DIM
    base = first_key + block * slots
    ek_ref[base : base + slots, :] = kept
    ev_ref[base : base + slots, :] = jnp.where(
        low, kept.astype(jnp.float32), jnp.where(mixed < DEAD_EDGE, 1.0, 0.0)
    ).astype(jnp.bfloat16)
    eq_ref[block * slots : block * slots + slots, :] = jnp.where(low, 0.0, mixed).astype(jnp.bfloat16)
    base = first_dec + block * tokens
    dk_ref[base : base + tokens, :] = got[slots : slots + tokens, :]


def begin_kernel(
    slots,
    tokens,
    own_ref,
    text_key_ref,
    text_value_ref,
    mask_ref,
    gain_ref,
    steps_ref,
    ek_ref,
    ev_ref,
    eq_ref,
    dk_ref,
    dq_ref,
    sums_ref,
    top_ref,
    fill_ref,
    weight_ref,
    wide_gain_ref,
    *places
):
    chips = own_ref.shape[0]
    cols = text_key_ref.shape[2]
    spare = tokens - slots
    rest = slots // 2
    head = jnp.minimum(lax.axis_index("seq") // 2, cols // HEAD_DIM - 1)
    odd = lax.rem(head, 2) == 1
    lanes = pl.ds(pl.multiple_of((head // 2) * LANES, LANES), LANES)

    def low_high(rows):
        turned = pltpu.roll(rows, HEAD_DIM, 1)
        return jnp.where(odd, turned, rows), jnp.where(odd, rows, turned)

    key_low, key_high = low_high(text_key_ref[0, :, lanes].astype(jnp.float32))
    value_low, _ = low_high(text_value_ref[0, :, lanes].astype(jnp.float32))
    mask_row = jnp.zeros((1, LANES), jnp.float32)
    whole = mask_ref[...].astype(jnp.float32).reshape(1, cols)
    for tile in range(cols // LANES):
        mask_row = jnp.where(head // 2 == tile, whole[:, tile * LANES : (tile + 1) * LANES], mask_row)
    mask_row, _ = low_high(jnp.broadcast_to(mask_row, (8, LANES)))
    steps = jnp.full((8, LANES), steps_ref[0], jnp.int32).astype(jnp.float32)
    weight_ref[...] = 1.0 / (0.1 + steps / 999.0)
    wide_gain_ref[...] = jnp.broadcast_to(gain_ref[...].astype(jnp.float32).reshape(1, cols), (8, cols))
    low = lane_of(tokens) < HEAD_DIM
    fill_ref[...] = jnp.where(lane_of(8) < HEAD_DIM, mask_row, 1.0)
    ek_ref[0:tokens, :] = jnp.where(low, value_low, key_high).astype(jnp.bfloat16)
    ev_ref[0:tokens, :] = jnp.where(low, value_low, 1.0).astype(jnp.bfloat16)
    dk_ref[0:tokens, :] = key_low.astype(jnp.bfloat16)
    for block in range(chips):
        got = own_ref.at[block]
        unpack(slots, tokens, got, block, tokens, tokens, ek_ref, ev_ref, eq_ref, dk_ref)
        tail = got[2 * slots : slots + tokens, :].astype(jnp.float32)
        last = got[slots + tokens : slots + tokens + rest, :].astype(jnp.float32)
        base = block * tokens
        dq_ref[base : base + spare, :] = jnp.where(
            lane_of(spare) < HEAD_DIM, pltpu.roll(tail, HEAD_DIM, 1), 0.0
        ).astype(jnp.bfloat16)
        low_rest = lane_of(rest) < HEAD_DIM
        dq_ref[base + spare : base + spare + rest, :] = jnp.where(low_rest, last, 0.0).astype(jnp.bfloat16)
        dq_ref[base + spare + rest : base + tokens, :] = jnp.where(
            low_rest, pltpu.roll(last, HEAD_DIM, 1), 0.0
        ).astype(jnp.bfloat16)

    rows = chips // 2 * slots

    def job(tile):
        span = slice(tile * rows, (tile + 1) * rows)

        def use(top, sums):
            sums_ref[span, :] = sums
            top_ref[span, :] = jnp.broadcast_to(top, (rows, LANES))

        return (lambda: eq_ref[span, :], [ek_ref], [ev_ref], None, use)

    run_jobs([job(tile) for tile in range(2)], (places[0:2], places[2:4]))


def attend_kernel(
    slots,
    tokens,
    pair_ref,
    ek_ref,
    ev_ref,
    eq_ref,
    dk_ref,
    dq_ref,
    sums_ref,
    top_ref,
    fill_ref,
    out_ref,
    pair_ek_ref,
    pair_ev_ref,
    pair_eq_ref,
    pair_dk_ref,
    dv_ref,
    *places
):
    chips = pair_ref.shape[0]
    spare = tokens - slots
    for block in range(chips):
        unpack(
            slots, tokens, pair_ref.at[block], block, 0, 0, pair_ek_ref, pair_ev_ref, pair_eq_ref, pair_dk_ref
        )
    dv_ref[0:tokens, :] = ev_ref[0:tokens, :]
    mask_row = fill_ref[0:1, :]
    fill = jnp.broadcast_to(mask_row, (spare, LANES)).astype(jnp.bfloat16)
    group = chips // 2
    rows = group * slots

    def encode(tile, query_ref, first_block, key_refs, value_refs, earlier):
        span = slice(tile * rows, (tile + 1) * rows)

        def use(top, sums):
            found = sums / pltpu.roll(sums, HEAD_DIM, 1)
            for inner in range(group):
                mixed = query_ref[tile * rows + inner * slots : tile * rows + (inner + 1) * slots, :]
                live = pltpu.roll(mixed.astype(jnp.float32), HEAD_DIM, 1) < DEAD_EDGE
                base = tokens + (first_block + tile * group + inner) * tokens
                dv_ref[base : base + slots, :] = jnp.where(
                    (lane_of(slots) < HEAD_DIM) & live, found[inner * slots : (inner + 1) * slots, :], mask_row
                ).astype(jnp.bfloat16)
                dv_ref[base + slots : base + tokens, :] = fill

        before = (lambda: (sums_ref[span, :], top_ref[span, :])) if earlier else None
        return (lambda: query_ref[span, :], key_refs, value_refs, before, use)

    dec_group = 2
    dec_rows = dec_group * tokens
    half = tokens // 2

    def decode(tile):
        def use(top, sums):
            found = sums / pltpu.roll(sums, HEAD_DIM, 1)
            for inner in range(dec_group):
                first = inner * tokens
                out_ref[tile * dec_group + inner] = jnp.where(
                    lane_of(half) < HEAD_DIM,
                    found[first : first + half],
                    pltpu.roll(found[first + half : first + tokens], HEAD_DIM, 1),
                ).astype(jnp.bfloat16)

        span = slice(tile * dec_rows, (tile + 1) * dec_rows)
        return (lambda: dq_ref[span, :], [dk_ref, pair_dk_ref], [dv_ref], None, use)

    jobs = [encode(tile, eq_ref, 0, [pair_ek_ref], [pair_ev_ref], True) for tile in range(2)]
    jobs += [
        encode(tile, pair_eq_ref, chips, [ek_ref, pair_ek_ref], [ev_ref, pair_ev_ref], False) for tile in range(2)
    ]
    jobs += [decode(tile) for tile in range(chips // dec_group)]
    run_jobs(jobs, (places[0:2], places[2:4]))


def sums_kernel(got_ref, gain_ref, target_ref, weight_ref, att_ref, sums_ref):
    tokens, cols = att_ref.shape
    half = tokens // 2
    low = lax.broadcasted_iota(jnp.int32, (half, LANES), 1) < HEAD_DIM
    for tile in range(cols // LANES):
        even = got_ref[2 * tile].astype(jnp.float32)
        odd = got_ref[2 * tile + 1].astype(jnp.float32)
        span = slice(tile * LANES, (tile + 1) * LANES)
        att_ref[0:half, span] = jnp.where(low, even, pltpu.roll(odd, HEAD_DIM, 1))
        att_ref[half:tokens, span] = jnp.where(low, pltpu.roll(even, HEAD_DIM, 1), odd)
    att = att_ref[...]
    gained = att * gain_ref[0:1, :]
    target = target_ref[0].astype(jnp.float32)
    weight = weight_ref[0:1, :]
    lane = lax.broadcasted_iota(jnp.int32, (tokens, LANES), 1)

    def over(block):
        return jnp.sum(block, axis=1, keepdims=True)

    table = jnp.where(
        lane == 1,
        over(gained * gained),
        jnp.where(lane == 2, over(gained * target), over(target * target)),
    )
    table = jnp.where(lane == 0, over(att * att), table * weight)
    sums_ref[...] = jnp.broadcast_to(jnp.transpose(table)[None, 0:4, :], sums_ref.shape)


def loss_kernel(heads, total_cols, sums_ref, loss_ref):
    total = None
    for chip in range(sums_ref.shape[0] // heads):
        sums = jnp.sum(sums_ref[chip * heads : (chip + 1) * heads], axis=0)
        factor = lax.rsqrt(sums[0:1, :] / total_cols + 1e-06)
        error = factor * factor * sums[1:2, :] - 2.0 * factor * sums[2:3, :] + sums[3:4, :]
        total = error if total is None else total + error
    loss_ref[...] = jnp.broadcast_to(jnp.sum(total, axis=1, keepdims=True)[None], loss_ref.shape)


def finish_kernel(heads, count, att_ref, gain_ref, sums_ref, got_ref, out_ref, loss_ref):
    tokens, cols = att_ref.shape
    loss_ref[...] = (jnp.sum(got_ref[...], axis=0) / count)[0:1, 0:1]
    half = sums_ref.shape[0] // heads // 2
    chip = lax.axis_index("seq") // 2
    listed = 2 * lax.rem(chip, half) + chip // half
    own = jnp.sum(sums_ref[pl.ds(listed * heads, heads)], axis=0)
    factor = lax.rsqrt(own[0:1, :] / (cols * heads) + 1e-06)
    column = jnp.transpose(jnp.broadcast_to(factor, (tokens, tokens)))[:, 0:1]
    out_ref[0] = (att_ref[...] * column * gain_ref[0:1, :]).astype(jnp.bfloat16)


def far_first(count):
    half = max(count // 2, 1)
    return [place + side * half for place in range(half) for side in range(count // half)]


def local(
    enc_query,
    enc_key,
    enc_value,
    keep_index,
    keep_count,
    text_key,
    text_value,
    dec_query,
    dec_key,
    mask_value,
    norm_gain,
    target,
    timesteps,
):
    images, seq, heads = (lax.axis_size(name) for name in ("dp", "seq", "head"))
    tokens, cols = enc_query.shape[1:]
    slots = keep_index.shape[1]
    local_heads = cols // HEAD_DIM
    chips = seq // 2
    packed = slots + tokens + slots // 2
    same_core = [[2 * chip + core for chip in range(chips)] for core in range(2)]
    bf16, f32 = jnp.bfloat16, jnp.float32

    send = pl.pallas_call(
        pack_kernel,
        out_shape=jax.ShapeDtypeStruct((chips, packed, LANES), bf16),
        in_specs=[pl.BlockSpec(memory_space=pltpu.HBM)] * 6,
        out_specs=vmem(1)[0],
        scratch_shapes=[pltpu.VMEM((1, slots), jnp.int32)]
        + [pltpu.VMEM((1, tokens, cols), bf16)] * 5
        + [pltpu.SemaphoreType.DMA((6,))],
        compiler_params=params(60),
        name="pack",
    )(keep_index, enc_query, enc_key, enc_value, dec_query, dec_key)
    own = lax.all_to_all(send, "seq", 0, 0, axis_index_groups=same_core, tiled=True)
    pair = lax.ppermute(own, "seq", [(source, source ^ 1) for source in range(seq)])
    kept_own = chips * slots
    dec_own = chips * tokens
    *begun, weight, gain = pl.pallas_call(
        functools.partial(begin_kernel, slots, tokens),
        out_shape=(
            jax.ShapeDtypeStruct((tokens + kept_own, LANES), bf16),
            jax.ShapeDtypeStruct((tokens + kept_own, LANES), bf16),
            jax.ShapeDtypeStruct((kept_own, LANES), bf16),
            jax.ShapeDtypeStruct((tokens + dec_own, LANES), bf16),
            jax.ShapeDtypeStruct((dec_own, LANES), bf16),
            jax.ShapeDtypeStruct((kept_own, LANES), f32),
            jax.ShapeDtypeStruct((kept_own, LANES), f32),
            jax.ShapeDtypeStruct((8, LANES), f32),
            jax.ShapeDtypeStruct((8, LANES), f32),
            jax.ShapeDtypeStruct((8, cols), f32),
        ),
        in_specs=vmem(5) + [pl.BlockSpec(memory_space=pltpu.SMEM)],
        out_specs=tuple(vmem(10)),
        scratch_shapes=[
            pltpu.VMEM((kept_own // 2, tokens + kept_own), f32),
            pltpu.VMEM((kept_own // 2, LANES), f32),
        ]
        * 2,
        compiler_params=params(),
        cost_estimate=pl.CostEstimate(
            flops=4 * kept_own * (tokens + kept_own) * LANES,
            bytes_accessed=8 * MIB,
            transcendentals=kept_own * (tokens + kept_own),
        ),
        name="begin",
    )(own, text_key, text_value, mask_value, norm_gain, timesteps)
    out = pl.pallas_call(
        functools.partial(attend_kernel, slots, tokens),
        out_shape=jax.ShapeDtypeStruct((chips, tokens // 2, LANES), bf16),
        in_specs=vmem(9),
        out_specs=vmem(1)[0],
        scratch_shapes=[
            pltpu.VMEM((kept_own, LANES), bf16),
            pltpu.VMEM((kept_own, LANES), bf16),
            pltpu.VMEM((kept_own, LANES), bf16),
            pltpu.VMEM((dec_own, LANES), bf16),
            pltpu.VMEM((tokens + 2 * dec_own, LANES), bf16),
        ]
        + [
            pltpu.VMEM((kept_own // 2, tokens + 2 * dec_own), f32),
            pltpu.VMEM((kept_own // 2, LANES), f32),
        ]
        * 2,
        compiler_params=params(),
        name="attend",
    )(pair, *begun)
    got = lax.all_to_all(out, "seq", 0, 0, axis_index_groups=same_core, tiled=True)
    att, sums = pl.pallas_call(
        sums_kernel,
        out_shape=(
            jax.ShapeDtypeStruct((tokens, cols), f32),
            jax.ShapeDtypeStruct((chips * heads, 4, tokens), f32),
        ),
        in_specs=vmem(4),
        out_specs=tuple(vmem(2)),
        compiler_params=params(),
        name="sums",
    )(got, gain, target, weight)
    planes = [
        [(2 * chip + core) * heads + head for chip in far_first(chips) for head in range(heads)] for core in range(2)
    ]
    sums = lax.all_to_all(sums, ("seq", "head"), 0, 0, axis_index_groups=planes, tiled=True)
    loss = pl.pallas_call(
        functools.partial(loss_kernel, heads, cols * heads),
        out_shape=jax.ShapeDtypeStruct((2 * images, 1, LANES), f32),
        in_specs=vmem(1),
        out_specs=vmem(1)[0],
        compiler_params=params(),
        name="loss",
    )(sums)
    columns = [
        [image * seq + 2 * chip + core for image in far_first(images) for core in range(2)] for chip in range(chips)
    ]
    got = lax.all_to_all(loss, ("dp", "seq"), 0, 0, axis_index_groups=columns, tiled=True)
    decoded, loss = pl.pallas_call(
        functools.partial(finish_kernel, heads, float(images * tokens * seq * cols * heads)),
        out_shape=(
            jax.ShapeDtypeStruct((1, tokens, cols), bf16),
            jax.ShapeDtypeStruct((1, 1), f32),
        ),
        in_specs=vmem(4),
        out_specs=tuple(vmem(2)),
        compiler_params=params(),
        name="finish",
    )(att, gain, sums, got)
    total_loss = loss.reshape(())
    return (decoded, total_loss)


def solution(mesh):
    placed = (
        P("dp", "seq", "head"),
        P("dp", "seq", "head"),
        P("dp", "seq", "head"),
        P("dp", "seq"),
        P("dp", "seq"),
        P("dp", None, "head"),
        P("dp", None, "head"),
        P("dp", "seq", "head"),
        P("dp", "seq", "head"),
        P("head"),
        P("head"),
        P("dp", "seq", "head"),
        P("dp"),
    )
    return jax.shard_map(
        local, mesh=mesh, in_specs=placed, out_specs=(P("dp", "seq", "head"), P()), check_vma=False
    )
```

```python
import functools

import jax
import jax.numpy as jnp
from jax import lax
from jax.experimental import pallas as pl
from jax.experimental.pallas import tpu as pltpu
from jax.sharding import PartitionSpec as P

HEAD_DIM = 64
LANES = 128
DEAD = 1024.0
DEAD_EDGE = 512.0
MIB = 1024 * 1024


def params(mib=40):
    return pltpu.CompilerParams(vmem_limit_bytes=mib * MIB)


def vmem(count):
    return [pl.BlockSpec(memory_space=pltpu.VMEM)] * count


def one_hot_dot(table, rows):
    return lax.dot_general(
        table, rows, (((1,), (0,)), ((), ())), preferred_element_type=jnp.float32
    )


def pack_kernel(
    index_hbm, eq_hbm, ek_hbm, ev_hbm, dq_hbm, dk_hbm, send_ref, *scratch
):
    *held, sems = scratch
    given = (index_hbm, eq_hbm, ek_hbm, ev_hbm, dq_hbm, dk_hbm)
    copies = [
        pltpu.make_async_copy(source, place, sems.at[number])
        for number, (source, place) in enumerate(zip(given, held))
    ]
    for copy in copies:
        copy.start()
    copies[0].wait()
    index_ref, eq_ref, ek_ref, ev_ref, dq_ref, dk_ref = held
    tokens, cols = eq_ref.shape[1:]
    slots = index_ref.shape[1]
    heads = cols // HEAD_DIM
    spare = tokens - slots
    index = jnp.broadcast_to(index_ref[...].astype(jnp.float32), (tokens, slots))
    index = jnp.transpose(index)
    token = lax.broadcasted_iota(jnp.int32, (slots, tokens), 1).astype(jnp.float32)
    slot = lax.broadcasted_iota(jnp.int32, (slots, tokens), 0)
    live = (slot == 0) | (index > 0.5)
    match_live = jnp.where(live & (token == index), 1.0, 0.0)
    match_fill = jnp.where(token == jnp.where(live, index, index[0:1, :]), 1.0, 0.0)
    kept = jnp.sum(match_live, axis=0, keepdims=True)
    kept_slot = jnp.sum(match_live * slot.astype(jnp.float32), axis=0, keepdims=True)
    row = lax.broadcasted_iota(jnp.int32, (tokens, tokens), 0)
    col = lax.broadcasted_iota(jnp.int32, (tokens, tokens), 1)
    before = jnp.where(row < col, 1.0, 0.0).astype(jnp.bfloat16)
    left = jnp.broadcast_to(1.0 - kept, (16, tokens)).astype(jnp.bfloat16)
    rank = one_hot_dot(left, before)[0:1, :]
    place = jnp.where(kept > 0.5, kept_slot, jnp.sum(kept, axis=1, keepdims=True) + rank)
    order = jnp.where(row.astype(jnp.float32) == place, 1.0, 0.0).astype(jnp.bfloat16)

    for copy in copies[1:]:
        copy.wait()
    scale = HEAD_DIM ** (-0.5)
    match_live = match_live.astype(jnp.bfloat16)
    match_fill = match_fill.astype(jnp.bfloat16)
    query = one_hot_dot(match_live, eq_ref[0]) * scale
    dead = jnp.where(live, 0.0, DEAD)
    query = query + jnp.concatenate([dead] * (cols // tokens), axis=1)
    key = one_hot_dot(match_fill, ek_ref[0])
    value = one_hot_dot(match_live, ev_ref[0])
    dec_key = one_hot_dot(order, dk_ref[0])
    dec_query = dq_ref[0].astype(jnp.float32) * scale

    def low(block, head):
        tile = block[:, (head // 2) * LANES : (head // 2 + 1) * LANES]
        return tile if head % 2 == 0 else pltpu.roll(tile, HEAD_DIM, 1)

    def high(block, head):
        tile = block[:, (head // 2) * LANES : (head // 2 + 1) * LANES]
        return tile if head % 2 == 1 else pltpu.roll(tile, HEAD_DIM, 1)

    def join(first, second):
        lane = lax.broadcasted_iota(jnp.int32, first.shape, 1)
        return jnp.where(lane < HEAD_DIM, first, second).astype(jnp.bfloat16)

    for head in range(heads):
        kept_tile = join(low(value, head), high(key, head))
        query_high = high(query, head)
        dec_low = low(dec_key, head)
        dq_low = low(dec_query, head)
        dq_high = high(dec_query, head)
        send_ref[head, 0:slots, :] = kept_tile
        send_ref[head, slots : 2 * slots, :] = join(dec_low[0:slots], query_high)
        send_ref[head, 2 * slots : slots + tokens, :] = join(dec_low[slots:tokens], dq_high[0:spare])
        rest = slots // 2
        send_ref[head, slots + tokens : slots + tokens + rest, :] = join(
            dq_low[spare : spare + rest], dq_high[spare + rest : tokens]
        )


def put_scores(query, key_refs, place, peak):
    rows = query.shape[0]
    largest = None
    column = 0
    for key_ref in key_refs:
        keys = key_ref.shape[0]
        for first in range(0, keys, 2 * LANES):
            last = min(keys, first + 2 * LANES)
            part = lax.dot_general(
                query, key_ref[first:last, :], (((1,), (1,)), ((), ())), preferred_element_type=jnp.float32
            )
            place[0:rows, column : column + last - first] = part
            column += last - first
            for lane in range(0, last - first, LANES):
                tile = part[:, lane : lane + LANES]
                largest = tile if largest is None else jnp.maximum(largest, tile)
    peak[0:rows, :] = largest


def weigh(rows, place, peak, value_refs, earlier):
    top = jnp.max(peak[0:rows, :], axis=1, keepdims=True)
    sums = None
    if earlier is not None:
        earlier_sums, earlier_top = earlier
        top = jnp.maximum(top, earlier_top[:, 0:1])
        sums = earlier_sums * jnp.exp(earlier_top - top)
    column = 0
    for value_ref in value_refs:
        keys = value_ref.shape[0]
        weights = jnp.exp(place[0:rows, column : column + keys] - top).astype(jnp.bfloat16)
        column += keys
        part = lax.dot_general(
            weights, value_ref[...], (((1,), (0,)), ((), ())), preferred_element_type=jnp.float32
        )
        sums = part if sums is None else sums + part
    return top, sums


def run_jobs(jobs, buffers):
    def put(number):
        query, key_refs, _, _, _ = jobs[number]
        put_scores(query(), key_refs, *buffers[number % 2])

    put(0)
    for number, (query, _, value_refs, earlier, use) in enumerate(jobs):
        if number + 1 < len(jobs):
            put(number + 1)
        place, peak = buffers[number % 2]
        rows = query().shape[0]
        use(*weigh(rows, place, peak, value_refs, None if earlier is None else earlier()))


def lane_of(rows):
    return lax.broadcasted_iota(jnp.int32, (rows, LANES), 1)


def unpack(slots, tokens, got, block, first_key, first_dec, ek_ref, ev_ref, eq_ref, dk_ref):
    kept = got[0:slots, :]
    mixed = got[slots : 2 * slots, :].astype(jnp.float32)
    low = lane_of(slots) < HEAD_DIM
    base = first_key + block * slots
    ek_ref[base : base + slots, :] = kept
    ev_ref[base : base + slots, :] = jnp.where(
        low, kept.astype(jnp.float32), jnp.where(mixed < DEAD_EDGE, 1.0, 0.0)
    ).astype(jnp.bfloat16)
    eq_ref[block * slots : block * slots + slots, :] = jnp.where(low, 0.0, mixed).astype(jnp.bfloat16)
    base = first_dec + block * tokens
    dk_ref[base : base + tokens, :] = got[slots : slots + tokens, :]


def begin_kernel(
    slots,
    tokens,
    own_ref,
    text_key_ref,
    text_value_ref,
    mask_ref,
    gain_ref,
    steps_ref,
    ek_ref,
    ev_ref,
    eq_ref,
    dk_ref,
    dq_ref,
    sums_ref,
    top_ref,
    fill_ref,
    weight_ref,
    wide_gain_ref,
    *places
):
    chips = own_ref.shape[0]
    cols = text_key_ref.shape[2]
    spare = tokens - slots
    rest = slots // 2
    head = jnp.minimum(lax.axis_index("seq") // 2, cols // HEAD_DIM - 1)
    odd = lax.rem(head, 2) == 1
    lanes = pl.ds(pl.multiple_of((head // 2) * LANES, LANES), LANES)

    def low_high(rows):
        turned = pltpu.roll(rows, HEAD_DIM, 1)
        return jnp.where(odd, turned, rows), jnp.where(odd, rows, turned)

    key_low, key_high = low_high(text_key_ref[0, :, lanes].astype(jnp.float32))
    value_low, _ = low_high(text_value_ref[0, :, lanes].astype(jnp.float32))
    mask_row = jnp.zeros((1, LANES), jnp.float32)
    whole = mask_ref[...].astype(jnp.float32).reshape(1, cols)
    for tile in range(cols // LANES):
        mask_row = jnp.where(head // 2 == tile, whole[:, tile * LANES : (tile + 1) * LANES], mask_row)
    mask_row, _ = low_high(jnp.broadcast_to(mask_row, (8, LANES)))
    steps = jnp.full((8, LANES), steps_ref[0], jnp.int32).astype(jnp.float32)
    weight_ref[...] = 1.0 / (0.1 + steps / 999.0)
    wide_gain_ref[...] = jnp.broadcast_to(gain_ref[...].astype(jnp.float32).reshape(1, cols), (8, cols))
    low = lane_of(tokens) < HEAD_DIM
    fill_ref[...] = jnp.where(lane_of(8) < HEAD_DIM, mask_row, 1.0)
    ek_ref[0:tokens, :] = jnp.where(low, value_low, key_high).astype(jnp.bfloat16)
    ev_ref[0:tokens, :] = jnp.where(low, value_low, 1.0).astype(jnp.bfloat16)
    dk_ref[0:tokens, :] = key_low.astype(jnp.bfloat16)
    for block in range(chips):
        got = own_ref.at[block]
        unpack(slots, tokens, got, block, tokens, tokens, ek_ref, ev_ref, eq_ref, dk_ref)
        tail = got[2 * slots : slots + tokens, :].astype(jnp.float32)
        last = got[slots + tokens : slots + tokens + rest, :].astype(jnp.float32)
        base = block * tokens
        dq_ref[base : base + spare, :] = jnp.where(
            lane_of(spare) < HEAD_DIM, pltpu.roll(tail, HEAD_DIM, 1), 0.0
        ).astype(jnp.bfloat16)
        low_rest = lane_of(rest) < HEAD_DIM
        dq_ref[base + spare : base + spare + rest, :] = jnp.where(low_rest, last, 0.0).astype(jnp.bfloat16)
        dq_ref[base + spare + rest : base + tokens, :] = jnp.where(
            low_rest, pltpu.roll(last, HEAD_DIM, 1), 0.0
        ).astype(jnp.bfloat16)

    rows = chips // 2 * slots

    def job(tile):
        span = slice(tile * rows, (tile + 1) * rows)

        def use(top, sums):
            sums_ref[span, :] = sums
            top_ref[span, :] = jnp.broadcast_to(top, (rows, LANES))

        return (lambda: eq_ref[span, :], [ek_ref], [ev_ref], None, use)

    run_jobs([job(tile) for tile in range(2)], (places[0:2], places[2:4]))


def attend_kernel(
    slots,
    tokens,
    pair_ref,
    ek_ref,
    ev_ref,
    eq_ref,
    dk_ref,
    dq_ref,
    sums_ref,
    top_ref,
    fill_ref,
    out_ref,
    pair_ek_ref,
    pair_ev_ref,
    pair_eq_ref,
    pair_dk_ref,
    dv_ref,
    *places
):
    chips = pair_ref.shape[0]
    spare = tokens - slots
    for block in range(chips):
        unpack(
            slots, tokens, pair_ref.at[block], block, 0, 0, pair_ek_ref, pair_ev_ref, pair_eq_ref, pair_dk_ref
        )
    dv_ref[0:tokens, :] = ev_ref[0:tokens, :]
    mask_row = fill_ref[0:1, :]
    fill = jnp.broadcast_to(mask_row, (spare, LANES)).astype(jnp.bfloat16)

    def encode(tile, group, query_ref, first_block, key_refs, value_refs, earlier):
        rows = group * slots
        span = slice(tile * rows, (tile + 1) * rows)

        def use(top, sums):
            found = sums / pltpu.roll(sums, HEAD_DIM, 1)
            for inner in range(group):
                mixed = query_ref[tile * rows + inner * slots : tile * rows + (inner + 1) * slots, :]
                live = pltpu.roll(mixed.astype(jnp.float32), HEAD_DIM, 1) < DEAD_EDGE
                base = tokens + (first_block + tile * group + inner) * tokens
                dv_ref[base : base + slots, :] = jnp.where(
                    (lane_of(slots) < HEAD_DIM) & live, found[inner * slots : (inner + 1) * slots, :], mask_row
                ).astype(jnp.bfloat16)
                dv_ref[base + slots : base + tokens, :] = fill

        before = (lambda: (sums_ref[span, :], top_ref[span, :])) if earlier else None
        return (lambda: query_ref[span, :], key_refs, value_refs, before, use)

    dec_group = 2
    dec_rows = dec_group * tokens
    half = tokens // 2

    def decode(tile):
        def use(top, sums):
            found = sums / pltpu.roll(sums, HEAD_DIM, 1)
            for inner in range(dec_group):
                first = inner * tokens
                out_ref[tile * dec_group + inner] = jnp.where(
                    lane_of(half) < HEAD_DIM,
                    found[first : first + half],
                    pltpu.roll(found[first + half : first + tokens], HEAD_DIM, 1),
                ).astype(jnp.bfloat16)

        span = slice(tile * dec_rows, (tile + 1) * dec_rows)
        return (lambda: dq_ref[span, :], [dk_ref, pair_dk_ref], [dv_ref], None, use)

    jobs = [encode(0, chips, eq_ref, 0, [pair_ek_ref], [pair_ev_ref], True)]
    jobs += [
        encode(tile, chips // 2, pair_eq_ref, chips, [ek_ref, pair_ek_ref], [ev_ref, pair_ev_ref], False)
        for tile in range(2)
    ]
    jobs += [decode(tile) for tile in range(chips // dec_group)]
    run_jobs(jobs, (places[0:2], places[2:4]))


def sums_kernel(got_ref, gain_ref, target_ref, weight_ref, att_ref, sums_ref):
    tokens, cols = att_ref.shape
    half = tokens // 2
    low = lax.broadcasted_iota(jnp.int32, (half, LANES), 1) < HEAD_DIM
    for tile in range(cols // LANES):
        even = got_ref[2 * tile].astype(jnp.float32)
        odd = got_ref[2 * tile + 1].astype(jnp.float32)
        span = slice(tile * LANES, (tile + 1) * LANES)
        att_ref[0:half, span] = jnp.where(low, even, pltpu.roll(odd, HEAD_DIM, 1))
        att_ref[half:tokens, span] = jnp.where(low, pltpu.roll(even, HEAD_DIM, 1), odd)
    att = att_ref[...]
    gained = att * gain_ref[0:1, :]
    target = target_ref[0].astype(jnp.float32)
    weight = weight_ref[0:1, :]
    lane = lax.broadcasted_iota(jnp.int32, (tokens, LANES), 1)

    def over(block):
        return jnp.sum(block, axis=1, keepdims=True)

    table = jnp.where(
        lane == 1,
        over(gained * gained),
        jnp.where(lane == 2, over(gained * target), over(target * target)),
    )
    table = jnp.where(lane == 0, over(att * att), table * weight)
    sums_ref[...] = jnp.broadcast_to(jnp.transpose(table)[None, 0:4, :], sums_ref.shape)


def loss_kernel(heads, total_cols, sums_ref, loss_ref):
    total = None
    for chip in range(sums_ref.shape[0] // heads):
        sums = jnp.sum(sums_ref[chip * heads : (chip + 1) * heads], axis=0)
        factor = lax.rsqrt(sums[0:1, :] / total_cols + 1e-06)
        error = factor * factor * sums[1:2, :] - 2.0 * factor * sums[2:3, :] + sums[3:4, :]
        total = error if total is None else total + error
    loss_ref[...] = jnp.broadcast_to(jnp.sum(total, axis=1, keepdims=True)[None], loss_ref.shape)


def finish_kernel(heads, count, att_ref, gain_ref, sums_ref, got_ref, out_ref, loss_ref):
    tokens, cols = att_ref.shape
    loss_ref[...] = (jnp.sum(got_ref[...], axis=0) / count)[0:1, 0:1]
    own = jnp.sum(sums_ref[pl.ds(lax.axis_index("seq") // 2 * heads, heads)], axis=0)
    factor = lax.rsqrt(own[0:1, :] / (cols * heads) + 1e-06)
    column = jnp.transpose(jnp.broadcast_to(factor, (tokens, tokens)))[:, 0:1]
    out_ref[0] = (att_ref[...] * column * gain_ref[0:1, :]).astype(jnp.bfloat16)


def local(
    enc_query,
    enc_key,
    enc_value,
    keep_index,
    keep_count,
    text_key,
    text_value,
    dec_query,
    dec_key,
    mask_value,
    norm_gain,
    target,
    timesteps,
):
    images, seq, heads = (lax.axis_size(name) for name in ("dp", "seq", "head"))
    tokens, cols = enc_query.shape[1:]
    slots = keep_index.shape[1]
    local_heads = cols // HEAD_DIM
    chips = seq // 2
    packed = slots + tokens + slots // 2
    same_core = [[2 * chip + core for chip in range(chips)] for core in range(2)]
    bf16, f32 = jnp.bfloat16, jnp.float32

    send = pl.pallas_call(
        pack_kernel,
        out_shape=jax.ShapeDtypeStruct((chips, packed, LANES), bf16),
        in_specs=[pl.BlockSpec(memory_space=pltpu.HBM)] * 6,
        out_specs=vmem(1)[0],
        scratch_shapes=[pltpu.VMEM((1, slots), jnp.int32)]
        + [pltpu.VMEM((1, tokens, cols), bf16)] * 5
        + [pltpu.SemaphoreType.DMA((6,))],
        compiler_params=params(60),
        name="pack",
    )(keep_index, enc_query, enc_key, enc_value, dec_query, dec_key)
    own = lax.all_to_all(send, "seq", 0, 0, axis_index_groups=same_core, tiled=True)
    pair = lax.ppermute(own, "seq", [(source, source ^ 1) for source in range(seq)])
    kept_own = chips * slots
    dec_own = chips * tokens
    *begun, weight, gain = pl.pallas_call(
        functools.partial(begin_kernel, slots, tokens),
        out_shape=(
            jax.ShapeDtypeStruct((tokens + kept_own, LANES), bf16),
            jax.ShapeDtypeStruct((tokens + kept_own, LANES), bf16),
            jax.ShapeDtypeStruct((kept_own, LANES), bf16),
            jax.ShapeDtypeStruct((tokens + dec_own, LANES), bf16),
            jax.ShapeDtypeStruct((dec_own, LANES), bf16),
            jax.ShapeDtypeStruct((kept_own, LANES), f32),
            jax.ShapeDtypeStruct((kept_own, LANES), f32),
            jax.ShapeDtypeStruct((8, LANES), f32),
            jax.ShapeDtypeStruct((8, LANES), f32),
            jax.ShapeDtypeStruct((8, cols), f32),
        ),
        in_specs=vmem(5) + [pl.BlockSpec(memory_space=pltpu.SMEM)],
        out_specs=tuple(vmem(10)),
        scratch_shapes=[
            pltpu.VMEM((kept_own // 2, tokens + kept_own), f32),
            pltpu.VMEM((kept_own // 2, LANES), f32),
        ]
        * 2,
        compiler_params=params(),
        cost_estimate=pl.CostEstimate(
            flops=4 * kept_own * (tokens + kept_own) * LANES,
            bytes_accessed=8 * MIB,
            transcendentals=kept_own * (tokens + kept_own),
        ),
        name="begin",
    )(own, text_key, text_value, mask_value, norm_gain, timesteps)
    out = pl.pallas_call(
        functools.partial(attend_kernel, slots, tokens),
        out_shape=jax.ShapeDtypeStruct((chips, tokens // 2, LANES), bf16),
        in_specs=vmem(9),
        out_specs=vmem(1)[0],
        scratch_shapes=[
            pltpu.VMEM((kept_own, LANES), bf16),
            pltpu.VMEM((kept_own, LANES), bf16),
            pltpu.VMEM((kept_own, LANES), bf16),
            pltpu.VMEM((dec_own, LANES), bf16),
            pltpu.VMEM((tokens + 2 * dec_own, LANES), bf16),
        ]
        + [
            pltpu.VMEM((kept_own, tokens + 2 * dec_own), f32),
            pltpu.VMEM((kept_own, LANES), f32),
        ]
        * 2,
        compiler_params=params(),
        name="attend",
    )(pair, *begun)
    got = lax.all_to_all(out, "seq", 0, 0, axis_index_groups=same_core, tiled=True)
    att, sums = pl.pallas_call(
        sums_kernel,
        out_shape=(
            jax.ShapeDtypeStruct((tokens, cols), f32),
            jax.ShapeDtypeStruct((chips * heads, 4, tokens), f32),
        ),
        in_specs=vmem(4),
        out_specs=tuple(vmem(2)),
        compiler_params=params(),
        name="sums",
    )(got, gain, target, weight)
    planes = [
        [(2 * chip + core) * heads + head for chip in range(chips) for head in range(heads)] for core in range(2)
    ]
    sums = lax.all_to_all(sums, ("seq", "head"), 0, 0, axis_index_groups=planes, tiled=True)
    loss = pl.pallas_call(
        functools.partial(loss_kernel, heads, cols * heads),
        out_shape=jax.ShapeDtypeStruct((2 * images, 1, LANES), f32),
        in_specs=vmem(1),
        out_specs=vmem(1)[0],
        compiler_params=params(),
        name="loss",
    )(sums)
    columns = [
        [image * seq + 2 * chip + core for image in range(images) for core in range(2)] for chip in range(chips)
    ]
    got = lax.all_to_all(loss, ("dp", "seq"), 0, 0, axis_index_groups=columns, tiled=True)
    decoded, loss = pl.pallas_call(
        functools.partial(finish_kernel, heads, float(images * tokens * seq * cols * heads)),
        out_shape=(
            jax.ShapeDtypeStruct((1, tokens, cols), bf16),
            jax.ShapeDtypeStruct((1, 1), f32),
        ),
        in_specs=vmem(4),
        out_specs=tuple(vmem(2)),
        compiler_params=params(),
        name="finish",
    )(att, gain, sums, got)
    total_loss = loss.reshape(())
    return (decoded, total_loss)


def solution(mesh):
    placed = (
        P("dp", "seq", "head"),
        P("dp", "seq", "head"),
        P("dp", "seq", "head"),
        P("dp", "seq"),
        P("dp", "seq"),
        P("dp", None, "head"),
        P("dp", None, "head"),
        P("dp", "seq", "head"),
        P("dp", "seq", "head"),
        P("head"),
        P("head"),
        P("dp", "seq", "head"),
        P("dp"),
    )
    return jax.shard_map(
        local, mesh=mesh, in_specs=placed, out_specs=(P("dp", "seq", "head"), P()), check_vma=False
    )
```
